256 devices in a mesh: pb: 8 (over z), col: 32 (over y, x, core).
Axes of the slice: x: 4, y: 4, z: 8, core: 2. Of those that a mesh axis runs over, the one named last changes fastest.
Arguments:
- queries: bfloat16 [16384, 512], P('pb'), may hold values from -0.29882812 to 0.29882812
- positive: int32 [16384], P('pb'), may hold values from 0 to 16383, each once
- items: bfloat16 [16384, 512], P('col'), may hold values from -0.29882812 to 0.29882812
- item_counts: int32 [16384], P('col'), may hold values from 1 to 189
- cache: bfloat16 [32768, 512], P('col'), may hold values from -0.29882812 to 0.29882812
- neg_owner: int32 [16384, 1], P('col'), may hold values from 0 to 31; in each aligned block of 512 rows (0 to 511, 512 to 1023, ...) at most 32 rows name the same one
- neg_row: int32 [16384], P('col'), may hold values from 0 to 1023
- neg_counts: int32 [16384], P('col'), may hold values from 1 to 189
Outputs:
- query_loss: float32 [16384], P('pb')
- query_grad: float32 [16384, 512], P(('pb', 'col'))
- item_grad: float32 [16384, 512], P('col')
- cache_grad: float32 [32768, 512], P('col')
The draws below stay inside these ranges and needn't reach their ends.
Inputs may be any that keep to these rules, and one draw needn't show every extreme that they name: `neg_owner`: within the 512 rows of one index of col no owner is named more than 32 times.
All inputs are finite; a program needn't handle non-finite values.
Results may differ from the reference program's by a relative error of at most 0.0009.
The reference program's roundings to bfloat16 on the way count: a program that leaves them out, or rounds other values in their place, can miss the bound.
Values may be sent and summed in bfloat16 or wider, within the bound.
A program may use at most 64 MiB of HBM per device.

```python
import math
import jax
import jax.numpy as jnp
import numpy as np
from jax import lax

E = 512
Q_DEV = 2048
CACHE_DEV = 1024
QUERIES = 16384
ITEMS = 16384
NEG_DEV = 512
NEGS = 16384
CAP = 32
CACHE = 32768
N_PB = 8
N_COL = 32


def count_values(key, total):
    power = jax.random.randint(key, (total,), 0, 6)
    base = jnp.left_shift(jnp.ones((total,), jnp.int32), power)
    extra = jax.random.randint(jax.random.fold_in(key, 1), (total,), 0, base)
    factor = 1 + 3 * jnp.arange(total, dtype=jnp.int32) // total
    return ((base + extra) * factor).astype(jnp.int32)


def draw_item_counts(key, part):
    key = jax.random.fold_in(key, 11)
    return count_values(key, ITEMS)


def draw_neg_counts(key, part):
    key = jax.random.fold_in(key, 23)
    return count_values(key, NEGS)


def plant(entries, rng, smallest, top_value):
    longest = entries.shape.index(max(entries.shape))
    spots = []
    for shift in (0, 1):
        where = [jax.random.randint(jax.random.fold_in(rng, axis), (), 0, length) for axis, length in enumerate(entries.shape)]
        where[longest] = (where[longest] + shift) % entries.shape[longest]
        spots.append(tuple(where))
    return entries.at[spots[0]].set(smallest).at[spots[1]].set(top_value)


def block_scale(rng, extent, cuts, low, top_value):
    def one(dim, shards_of):
        heights = jax.random.uniform(jax.random.fold_in(jax.random.fold_in(rng, 6), dim), (shards_of,), jnp.float32, low / len(cuts), top_value / len(cuts))
        return jnp.repeat(jnp.exp(heights), extent[dim] // shards_of).reshape((-1,) + (1,) * (len(extent) - dim - 1))

    gain = one(*cuts[0])
    for cut in cuts[1:]:
        gain = gain * one(*cut)
    return gain


def deal_out(stream_key, own, number, rows, amount, top, bound, slope):
    ranking = jax.random.permutation(stream_key, amount)
    heavy_load, ordinary = shares(amount, rows * top, bound, slope, True), shares(amount, rows * top, bound, slope, False)
    places = jnp.arange(amount)

    def named(sizes, offset_by):
        used = int((sizes > 0).sum())
        fixed = max(1, used // 4)
        passed = fixed + (places - fixed + offset_by * (used - fixed)) % max(1, amount - fixed)
        return jnp.zeros((amount,), jnp.int32).at[ranking[jnp.where(places < fixed, places, passed)]].set(jnp.asarray(sizes, jnp.int32))

    sizes = jnp.where(number % 4 == 0, named(heavy_load, number // 4), named(ordinary, number - number // 4 - 1))
    mixed = jax.random.permutation(jax.random.fold_in(own, 3), amount)
    donor, taker = mixed[0:amount // 2 * 2:2], mixed[1:amount // 2 * 2:2]
    margin = jnp.minimum(sizes[donor] - 1, bound - sizes[taker]) // 2
    margin = jnp.where((donor == ranking[0]) | (taker == ranking[0]) | (sizes[taker] == 0), 0, jnp.maximum(margin, 0))
    passed = jax.random.randint(jax.random.fold_in(own, 4), (amount // 2,), 0, 1 << 20) % (margin + 1)
    sizes = sizes.at[donor].add(-passed).at[taker].add(passed)
    items = jnp.searchsorted(jnp.cumsum(sizes), jnp.arange(rows * top), side="right").astype(jnp.int32)
    listing = items.reshape(top, rows).T
    listing = listing[jax.random.permutation(jax.random.fold_in(own, 1), rows)]
    offset_by = jax.random.randint(jax.random.fold_in(own, 2), (rows, 1), 0, top)
    return jnp.take_along_axis(listing, (jnp.arange(top)[None, :] + offset_by) % top, axis=1)


def shares(number_of, total, bound, lean, full):
    weights = [(1 << 20) // math.isqrt(rank ** lean) + 1 for rank in range(1, number_of + 1)]
    largest = bound if full else min(bound, max(-(-total // number_of), total * weights[0] // sum(weights)))
    least = 1 if total - largest >= number_of - 1 else 0
    holding, rest = [largest] + [least] * (number_of - 1), total - largest - least * (number_of - 1)
    while rest > 0:
        candidates = [i for i in range(1, number_of) if holding[i] < largest] or [i for i in range(1, number_of) if holding[i] < bound]
        mass, left = sum([weights[i] for i in candidates]), rest
        for i in candidates:
            more = min(bound - holding[i], max(1, left * weights[i] // mass), rest)
            holding[i] = holding[i] + more
            rest = rest - more
    return np.array(holding)


def bell_draw(rng, extent, deviation, reach, shards=(), kind=jnp.bfloat16):
    loudness = block_scale(rng, extent, shards, -0.22, 0.18) if shards else 1.0
    drawn = jax.random.normal(rng, extent, jnp.float32) * deviation * loudness
    return jnp.minimum(jnp.maximum(drawn, -reach), reach).astype(kind)


def setup_inputs(seed: int = 0) -> dict:
    seeds = jax.random.split(jax.random.key(seed), 9)
    queries = bell_draw(seeds[0], (QUERIES, E), 0.05, 0.29882812, ((0, 8),))
    positive = jax.random.permutation(seeds[1], ITEMS).astype(jnp.int32)
    items = bell_draw(seeds[2], (ITEMS, E), 0.05, 0.29882812, ((0, 32),))
    item_counts = draw_item_counts(jax.random.fold_in(seeds[8], 71), 0)
    cache = bell_draw(seeds[4], (CACHE, E), 0.05, 0.29882812, ((0, 32),))
    neg_owner_keys = jax.random.split(jax.random.fold_in(seeds[5], 1), NEGS // NEG_DEV)
    neg_owner_turns = jax.random.permutation(jax.random.fold_in(seeds[5], 3), NEGS // NEG_DEV)
    neg_owner = jax.vmap(lambda own, number: deal_out(jax.random.fold_in(seeds[5], 2), own, number, NEG_DEV, N_COL, 1, CAP, 2))(neg_owner_keys, neg_owner_turns).reshape((NEGS, 1))
    neg_row = plant(jax.random.randint(seeds[6], (NEGS,), 0, CACHE_DEV), jax.random.fold_in(seeds[6], 1), 0, CACHE_DEV - 1).astype(jnp.int32)
    neg_counts = draw_neg_counts(jax.random.fold_in(seeds[8], 71), 0)
    return {"queries": queries, "positive": positive, "items": items, "item_counts": item_counts, "cache": cache, "neg_owner": neg_owner, "neg_row": neg_row, "neg_counts": neg_counts}


def unit_rows(rows):
    values = rows.astype(jnp.float32)
    scale = jnp.sqrt(lax.optimization_barrier(jnp.sum(values * values, axis=-1, keepdims=True)) + 1e-06)
    return (values / scale, scale)

def unit_back(grad, direction, scale):
    return (grad - direction * lax.optimization_barrier(jnp.sum(grad * direction, axis=-1, keepdims=True))) / scale

def reference(queries, positive, items, item_counts, cache, neg_owner, neg_row, neg_counts):
    q_dir, q_scale = unit_rows(queries)
    q_unit = q_dir.astype(jnp.bfloat16)
    i_dir, i_scale = unit_rows(items)
    i_unit = i_dir.astype(jnp.bfloat16)
    neg_id = (neg_owner[:, 0] * CACHE_DEV + neg_row).astype(jnp.int32)
    negatives = cache[neg_id]
    n_dir, n_scale = unit_rows(negatives)
    n_unit = n_dir.astype(jnp.bfloat16)
    item_total = jnp.sum(item_counts.astype(jnp.float32))
    neg_total = jnp.sum(neg_counts.astype(jnp.float32))
    item_shift = jnp.log(item_counts.astype(jnp.float32)) - jnp.log(item_total)
    neg_shift = jnp.log(neg_counts.astype(jnp.float32)) - jnp.log(neg_total)
    item_index = jnp.arange(ITEMS, dtype=jnp.int32)

    def block_step(carry, inputs):
        item_acc, neg_acc = carry
        q_block, pos_block = inputs
        item_logits = jnp.dot(q_block, i_unit.T, preferred_element_type=jnp.float32) / 0.05 - item_shift[None, :]
        neg_logits = jnp.dot(q_block, n_unit.T, preferred_element_type=jnp.float32) / 0.05 - neg_shift[None, :]
        lse = jnp.log(lax.optimization_barrier(jnp.sum(jnp.exp(item_logits), axis=1)) + lax.optimization_barrier(jnp.sum(jnp.exp(neg_logits), axis=1)))
        hit = (pos_block[:, None] == item_index[None, :]).astype(jnp.float32)
        pos_logit = lax.optimization_barrier(jnp.sum(hit * item_logits, axis=1))
        item_weight = (jnp.exp(item_logits - lse[:, None]) - hit).astype(jnp.bfloat16)
        neg_weight = jnp.exp(neg_logits - lse[:, None]).astype(jnp.bfloat16)
        q_grad = (jnp.dot(item_weight, i_unit, preferred_element_type=jnp.float32) + jnp.dot(neg_weight, n_unit, preferred_element_type=jnp.float32)) / 0.05
        item_acc = item_acc + jnp.dot(item_weight.T, q_block, preferred_element_type=jnp.float32) / 0.05
        neg_acc = neg_acc + jnp.dot(neg_weight.T, q_block, preferred_element_type=jnp.float32) / 0.05
        return ((item_acc, neg_acc), (lse - pos_logit, q_grad))
    start = (jnp.zeros((ITEMS, E), jnp.float32), jnp.zeros((NEGS, E), jnp.float32))
    (item_acc, neg_acc), (losses, q_grads) = lax.scan(block_step, start, (q_unit.reshape(N_PB, Q_DEV, E), positive.reshape(N_PB, Q_DEV)))
    query_loss = losses.reshape(QUERIES)
    query_grad = unit_back(q_grads.reshape(QUERIES, E), q_dir, q_scale)
    item_grad = unit_back(item_acc, i_dir, i_scale)
    neg_grad = unit_back(neg_acc, n_dir, n_scale)
    cache_grad = jax.ops.segment_sum(neg_grad, neg_id, num_segments=CACHE)
    return (query_loss, query_grad, item_grad, cache_grad)
```

```python
import functools

import jax
import jax.numpy as jnp
from jax import lax
from jax.experimental import pallas as pl
from jax.experimental.pallas import tpu as pltpu
from jax.sharding import PartitionSpec as P

MESH = pl.DeviceIdType.MESH
F32 = jnp.float32
BF16 = jnp.bfloat16
I32 = jnp.int32
I16 = jnp.int16

E = 512
H = E // 2
NQ = 2048
QB = 256
NB = NQ // QB
NI = 512
NN = 512
NC = 32
NX = 4
NY = 4
NZ = 8
CAP = 32
ROWS = 1024
CH = 64
INV_T = 20.0


def iota(shape, dim):
    return lax.broadcasted_iota(I32, shape, dim)


def onehot(cond):
    return jnp.where(cond, 1.0, 0.0).astype(BF16)


def dot_nn(a, b):
    return lax.dot_general(a, b, (((1,), (0,)), ((), ())), preferred_element_type=F32)


def dot_nt(a, b):
    return lax.dot_general(a, b, (((1,), (1,)), ((), ())), preferred_element_type=F32)


def dot_tn(a, b):
    return lax.dot_general(a, b, (((0,), (0,)), ((), ())), preferred_element_type=F32)


def halves(x):
    hi = x.astype(BF16)
    return hi, (x - hi.astype(F32)).astype(BF16)


def encode(x, group):
    rows, width = x.shape
    cube = x.reshape(rows // group, group, width)
    top = jnp.max(jnp.abs(cube), axis=0)
    expo = jnp.ceil(jnp.log2(jnp.maximum(top, 1e-30)))
    code = jnp.round(cube * jnp.exp2(14.99 - expo)[None])
    return code.reshape(rows, width).astype(I32).astype(I16), expo


def decode(code, expo):
    rows, width = code.shape
    group = expo.shape[0]
    cube = code.astype(I32).astype(F32).reshape(rows // group, group, width)
    return (cube * jnp.exp2(expo - 14.99)[None]).reshape(rows, width)


def to_i16(x):
    return x.astype(I32).astype(I16)


def from_i16(x):
    return x.astype(I32).astype(F32)


def unit(x):
    scale = jnp.sqrt(jnp.sum(x * x, axis=1, keepdims=True) + 1e-06)
    return x / scale, scale


def unit_back(grad, rows):
    direction, scale = unit(rows)
    return (grad - direction * jnp.sum(grad * direction, axis=1, keepdims=True)) / scale


def kernel(
    queries, positive, items, small, cache,
    loss_out, query_out, item_out, cache_out,
    msg, mrecv, rows_buf, fetched, perm, scat, q_unit, cand_i, cand_n, negs, shift,
    expo_i, expo_n, sums, core_sums, x_sums, y_sums, weight, part, rs_send, rs_recv,
    ag_item, sel_out, n_recv, ag_cache, grad_hi, grad_lo, q_part, q_core, q_msg, q_recv,
    m_s, m_r, f_s, f_r, c_s, c_r, x_s, x_r, y_s, y_r, rs_s, rs_r, ai_s, ai_r, n_s, n_r, ac_s, ac_r,
    qc_s, qc_r, qd_s, qd_r,
):
    me = lax.axis_index("col")
    z = lax.axis_index("pb")
    core = me % 2
    chip = me // 2
    my_x = chip % NX
    my_y = chip // NX
    up = (z + 1) % NZ
    down = (z + NZ - 1) % NZ
    sibling = chip * 2 + 1 - core

    barrier = pltpu.get_barrier_semaphore()

    @pl.loop(1, NC)
    def _(s):
        pl.semaphore_signal(barrier, inc=1, device_id={"col": (me + s) % NC}, device_id_type=MESH)

    for other in (up, down):
        pl.semaphore_signal(barrier, inc=1, device_id={"pb": other}, device_id_type=MESH)

    def remote(src, dst, send, recv, **where):
        return pltpu.make_async_remote_copy(
            src_ref=src, dst_ref=dst, send_sem=send, recv_sem=recv, device_id=where, device_id_type=MESH
        )

    counts_i = small[0:1, :]
    counts_n = small[1:2, :]
    owner = small[2:3, :]
    row = small[3:4, :]
    table = jnp.where(iota((NC, NN), 0) == owner, 1.0, 0.0)
    before = onehot(iota((NN, NN), 0) < iota((NN, NN), 1))
    earlier = dot_nn(table.astype(BF16), before)
    rank = jnp.sum(earlier * table, axis=0, keepdims=True).astype(I32)
    per_owner = jnp.sum(table, axis=1, keepdims=True)
    first = jnp.sum(jnp.where(iota((NC, NN), 0) < owner, per_owner, 0.0), axis=0, keepdims=True).astype(I32)
    place = first + rank
    plane = place & (NZ - 1)
    index = place >> 3
    slot4 = rank >> 3
    slot = 4 * plane + slot4

    row_hi = (row >> 5).astype(F32)
    row_lo = (row & 31).astype(F32)
    to_plane = jnp.where(iota((NC * NZ, NN), 0) == NZ * owner + plane, 1.0, 0.0)
    lane1 = onehot(iota((128, NN), 0) == 4 * me + slot4)
    asked_msg = dot_nt((to_plane * row_hi).astype(BF16), lane1) * 32.0 + dot_nt(
        (to_plane * row_lo).astype(BF16), lane1
    )
    msg[:, 0:8, :] = asked_msg.reshape(NC, NZ, 128)
    lane2 = onehot(iota((128, NN), 0) == CAP * (me % 4) + slot)
    asked_rows = dot_nt((table * row_hi).astype(BF16), lane2) * 32.0 + dot_nt((table * row_lo).astype(BF16), lane2)
    mine = iota((NC, 8, 128), 1) == me // 4
    msg[:, 8:16, :] = jnp.where(mine, asked_rows.reshape(NC, 1, 128), 0.0)
    total_i = jnp.sum(counts_i.astype(F32), axis=1, keepdims=True)
    total_n = jnp.sum(counts_n.astype(F32), axis=1, keepdims=True)
    totals = jnp.where(iota((8, 128), 0) < 4, total_i, total_n)
    msg[:, 16:24, :] = jnp.broadcast_to(totals[None], (NC, 8, 128))

    pl.semaphore_wait(barrier, NC + 1)

    @pl.loop(1, NC)
    def _(s):
        other = (me + s) % NC
        remote(msg.at[other], mrecv.at[me], m_s.at[other], m_r.at[me], col=other).start()

    mrecv[me] = msg[me]

    item_rows = items[...].astype(F32)
    cand_i[...] = unit(item_rows)[0].astype(BF16)

    @pl.loop(0, NB)
    def _(b):
        at = pl.ds(pl.multiple_of(b * QB, QB), QB)
        q_unit[at, :] = unit(queries[at, :].astype(F32))[0].astype(BF16)

    ordered = jnp.where(iota((NN, NN), 0) == CH * plane + index, 1.0, 0.0)
    by_slot = onehot(iota((NC * CAP, NN), 0) == CAP * owner + slot)
    perm[...] = dot_nt(ordered.astype(BF16), by_slot).astype(BF16)
    log_i = jnp.log(
        jnp.sum(
            jnp.where(iota((NI, NI), 0) == iota((NI, NI), 1), counts_i.astype(F32), 0.0), axis=1, keepdims=True
        )
    )
    log_n = jnp.log(jnp.sum(ordered * counts_n.astype(F32), axis=1, keepdims=True))

    @pl.loop(1, NC)
    def _(s):
        other = (me + s) % NC
        remote(msg.at[other], mrecv.at[other], m_s.at[other], m_r.at[other], col=other).wait()

    asked = jnp.sum(mrecv[...], axis=0)
    asked_planes = asked[0:8, :].astype(I32)
    shift[0:NI, :] = log_i - jnp.log(asked[16:17, 0:1])
    shift[NI:, :] = log_n - jnp.log(asked[20:21, 0:1])

    by_sender = jnp.concatenate([asked[8:16, :], jnp.zeros((120, 128), F32)], axis=0).T

    @pl.loop(0, NC // 4)
    def _(s):
        group = (me // 4 + s) % (NC // 4)
        wanted = jnp.sum(jnp.where(iota((128, 128), 1) == group, by_sender, 0.0), axis=1, keepdims=True)
        pick = onehot(iota((128, ROWS), 1) == wanted.astype(I32))
        found = dot_nn(pick, cache[...]).astype(BF16).reshape(4, CAP, E)
        for i in range(4):
            other = group * 4 + i
            rows_buf[other] = found[i]

            @pl.when(other != me)
            def _():
                remote(rows_buf.at[other], fetched.at[me], f_s.at[other], f_r.at[me], col=other).start()

            @pl.when(other == me)
            def _():
                fetched[me] = found[i]

    first_item = me * NI

    @pl.loop(0, NB)
    def _(b):
        at = pl.ds(pl.multiple_of(b * QB, QB), QB)
        logits = dot_nt(cand_i[...], q_unit[at, :]) * INV_T - shift[0:NI, :]
        hit = positive[:, at] == first_item + iota((NI, QB), 0)
        expo = jnp.exp(logits)
        expo_i[:, at] = expo
        sums[pl.ds(b, 1), :] = jnp.sum(expo, axis=0, keepdims=True)
        sums[pl.ds(b + NB, 1), :] = jnp.sum(jnp.where(hit, logits, 0.0), axis=0, keepdims=True)

    for p in range(NZ):
        scat[:, p * 128 : (p + 1) * 128] = onehot(iota((ROWS, 128), 0) == asked_planes[p : p + 1, :])

    @pl.loop(1, NC)
    def _(s):
        other = (me + s) % NC
        remote(rows_buf.at[other], fetched.at[other], f_s.at[other], f_r.at[other], col=other).wait()

    neg_rows = dot_nn(perm[...], fetched[...].reshape(NC * CAP, E))
    negs[...] = neg_rows.astype(BF16)
    cand_n[...] = unit(neg_rows)[0].astype(BF16)

    @pl.loop(0, NB)
    def _(b):
        at = pl.ds(pl.multiple_of(b * QB, QB), QB)
        expo = jnp.exp(dot_nt(cand_n[...], q_unit[at, :]) * INV_T - shift[NI:, :])
        expo_n[:, at] = expo
        sums[pl.ds(b, 1), :] = sums[pl.ds(b, 1), :] + jnp.sum(expo, axis=0, keepdims=True)

    copy = remote(sums, core_sums, c_s, c_r, col=sibling)
    copy.start()
    copy.wait()
    x_sums[my_x] = sums[...] + core_sums[...]

    def x_col(s):
        other = (my_x + s) % NX
        return other, (my_y * NX + other) * 2 + core

    def y_col(s):
        other = (my_y + s) % NY
        return other, (other * NX + my_x) * 2 + core

    for s in range(1, NX):
        other, col = x_col(s)
        remote(x_sums.at[my_x], x_sums.at[my_x], x_s.at[other], x_r.at[my_x], col=col).start()
    for s in range(1, NX):
        other, col = x_col(s)
        remote(x_sums.at[my_x], x_sums.at[other], x_s.at[other], x_r.at[other], col=col).wait()
    y_sums[my_y] = ((x_sums[0] + x_sums[1]) + x_sums[2]) + x_sums[3]
    for s in range(1, NY):
        other, col = y_col(s)
        remote(y_sums.at[my_y], y_sums.at[my_y], y_s.at[other], y_r.at[my_y], col=col).start()
    for s in range(1, NY):
        other, col = y_col(s)
        remote(y_sums.at[my_y], y_sums.at[other], y_s.at[other], y_r.at[other], col=col).wait()
    summed = ((y_sums[0] + y_sums[1]) + y_sums[2]) + y_sums[3]
    loss_out[...] = jnp.log(summed[0:NB]) - summed[NB:]
    sums[0:NB] = 1.0 / summed[0:NB]

    @pl.loop(0, NB)
    def _(b):
        at = pl.ds(pl.multiple_of(b * QB, QB), QB)
        inverse = sums[pl.ds(b, 1), :]
        hit = positive[:, at] == first_item + iota((NI, QB), 0)
        weight[0:NI, at] = (expo_i[:, at] * inverse - jnp.where(hit, 1.0, 0.0)).astype(BF16)
        weight[NI:, at] = (expo_n[:, at] * inverse).astype(BF16)

    def cand_part(p):
        for base, at0 in ((0, 0), (NI, CH)):
            grad = dot_nn(weight[pl.ds(pl.multiple_of(base + p * CH, CH), CH), :], q_unit[...]) * INV_T
            part[0, p, at0 : at0 + CH, :] = grad[:, :H]
            part[1, p, at0 : at0 + CH, :] = grad[:, H:]

    @pl.loop(0, NZ)
    def _(p):
        cand_part(p)

    def ring_peer(d):
        return up if d == 0 else down

    def ring_chunk(d, t):
        return (z + 2 * NZ - 1 - t) % NZ if d == 0 else (z + 1 + t) % NZ

    def pack(ref, chunk):
        code, e = encode(chunk[0:CH], 8)
        ref[0:CH] = code
        code, e2 = encode(chunk[CH:], 8)
        ref[CH : 2 * CH] = code
        ref[2 * CH :] = to_i16(jnp.concatenate([e, e2], axis=0))

    def unpack(ref):
        e = from_i16(ref[2 * CH :])
        return jnp.concatenate([decode(ref[0:CH], e[0:8]), decode(ref[CH : 2 * CH], e[8:16])], axis=0)

    def rs_copy(d, t):
        return remote(
            rs_send.at[d, t], rs_recv.at[d, t], rs_s.at[d, t], rs_r.at[d, t], pb=ring_peer(d)
        )

    for d in range(2):
        pack(rs_send.at[d, 0], part[d, ring_chunk(d, 0)])
        rs_copy(d, 0).start()

    def q_block(b):
        at = pl.ds(pl.multiple_of(b * QB, QB), QB)
        grad = dot_tn(weight[0:NI, at], cand_i[...]) + dot_tn(weight[NI:, at], cand_n[...])
        q_part[pl.ds(b * 2, 2)] = (grad * INV_T).reshape(2, 2, CH, E)

    for t in range(1, NZ - 1):
        for d in range(2):
            rs_copy(d, t - 1).wait()
            pack(rs_send.at[d, t], part[d, ring_chunk(d, t)] + unpack(rs_recv.at[d, t - 1]))
            rs_copy(d, t).start()
        if t <= 4:
            q_block(2 * t - 2)
            q_block(2 * t - 1)
        if t == 4:
            q_copy = remote(q_part.at[:, 1 - core], q_core, qc_s, qc_r, col=sibling)
            q_copy.start()

    for d in range(2):
        rs_copy(d, NZ - 2).wait()
    own = jnp.concatenate([part[d, z] + unpack(rs_recv.at[d, NZ - 2]) for d in range(2)], axis=1)

    mine_at = pl.ds(pl.multiple_of(z * CH, CH), CH)
    item_grad = unit_back(own[0:CH], items[mine_at, :].astype(F32))
    neg_grad = unit_back(own[CH:], negs[mine_at, :].astype(F32))
    for h in range(2):
        code, e = encode(item_grad[:, h * H : (h + 1) * H], 16)
        ag_item[z, h, 0:CH] = code
        ag_item[z, h, CH:] = to_i16(e)

    def gather_copy(ref, send, recv, d, s, h):
        source = (z + 2 * NZ - s) % NZ if d == 0 else (z + s) % NZ
        return remote(
            ref.at[source, h], ref.at[source, h], send.at[d, s, h], recv.at[d, s, h], pb=ring_peer(d)
        )

    def steps(d, h):
        return 4 if d == h else 3

    def gather_start(ref, send, recv, s):
        for d in range(2):
            for h in (d, 1 - d):
                if s < steps(d, h):
                    if s > 0:
                        gather_copy(ref, send, recv, d, s - 1, h).wait()
                    gather_copy(ref, send, recv, d, s, h).start()

    def gather_finish(ref, send, recv):
        for d in range(2):
            for h in range(2):
                gather_copy(ref, send, recv, d, steps(d, h) - 1, h).wait()

    gather_start(ag_item, ai_s, ai_r, 0)

    q_row = iota((NC * 8, NN), 0)
    sel_slot = onehot(CAP * owner + slot == CAP * (q_row >> 3) + 4 * z + (q_row & 3))
    sel_index = onehot((iota((CH, NN), 0) == index) & (plane == z))
    select = dot_nt(sel_slot, sel_index).astype(BF16)
    hi, lo = halves(neg_grad)
    wide = dot_nn(select, hi) + dot_nn(select, lo)
    left = (iota((NC * 8, H), 0) & 4) == 0
    sel_out[...] = jnp.where(left, wide[:, :H], wide[:, H:]).reshape(NC, 8, H)

    @pl.loop(1, NC)
    def _(s):
        other = (me + s) % NC
        remote(sel_out.at[other], n_recv.at[me], n_s.at[other], n_r.at[me], col=other).start()

    n_recv[me] = sel_out[me]

    q_copy.wait()

    @pl.loop(0, NC // 2)
    def _(c):
        code, e = encode(q_part[c, core] + q_core[c], 16)
        q_msg[c, 0:CH] = code
        q_msg[c, CH:] = to_i16(e)

    gather_start(ag_item, ai_s, ai_r, 1)

    @pl.loop(1, NC)
    def _(s):
        other = (me + s) % NC
        remote(sel_out.at[other], n_recv.at[other], n_s.at[other], n_r.at[other], col=other).wait()

    @pl.loop(1, NC // 2)
    def _(s):
        other = (chip + s) % (NC // 2)
        remote(q_msg.at[other], q_recv.at[chip], qd_s.at[other], qd_r.at[chip], col=other * 2 + core).start()

    q_recv[chip] = q_msg[chip]

    received = halves(n_recv[...].reshape(NC * 8, H))
    want = iota((128, NC * 8), 0)
    have = iota((128, NC * 8), 1)
    for h in range(2):
        order = onehot(have == 8 * (want >> 2) + 4 * h + (want & 3))
        code, e = encode(dot_nn(order, received[0]) + dot_nn(order, received[1]), 16)
        ag_cache[z, h, 0:128] = code
        ag_cache[z, h, 128:] = to_i16(e)

    gather_start(ag_cache, ac_s, ac_r, 0)
    gather_start(ag_item, ai_s, ai_r, 2)
    gather_start(ag_item, ai_s, ai_r, 3)
    gather_start(ag_cache, ac_s, ac_r, 1)
    gather_finish(ag_item, ai_s, ai_r)
    for p in range(NZ):
        for h in range(2):
            item_out[p * CH : (p + 1) * CH, h * H : (h + 1) * H] = decode(
                ag_item[p, h, 0:CH], from_i16(ag_item[p, h, CH:])
            )
    gather_start(ag_cache, ac_s, ac_r, 2)

    @pl.loop(1, NC // 2)
    def _(s):
        other = (chip + s) % (NC // 2)
        remote(q_msg.at[other], q_recv.at[other], qd_s.at[other], qd_r.at[other], col=other * 2 + core).wait()

    q_grad = decode(q_recv[0, 0:CH], from_i16(q_recv[0, CH:]))
    for c in range(1, NC // 2):
        q_grad = q_grad + decode(q_recv[c, 0:CH], from_i16(q_recv[c, CH:]))
    query_out[...] = unit_back(q_grad, queries[pl.ds(pl.multiple_of(me * CH, CH), CH), :].astype(F32))

    gather_start(ag_cache, ac_s, ac_r, 3)
    gather_finish(ag_cache, ac_s, ac_r)

    @pl.loop(0, NZ)
    def _(p):
        at = pl.ds(pl.multiple_of(p * 128, 128), 128)
        for h in range(2):
            hi, lo = halves(decode(ag_cache[p, h, 0:128], from_i16(ag_cache[p, h, 128:])))
            grad_hi[at, h * H : (h + 1) * H] = hi
            grad_lo[at, h * H : (h + 1) * H] = lo

    @pl.loop(0, ROWS // 256)
    def _(r):
        at = pl.ds(pl.multiple_of(r * 256, 256), 256)
        cache_out[at, :] = dot_nn(scat[at, :], grad_hi[...]) + dot_nn(scat[at, :], grad_lo[...])


def body(queries, positive, items, item_counts, cache, neg_owner, neg_row, neg_counts):
    zero = jnp.zeros_like(neg_row)
    small = jnp.stack([item_counts, neg_counts, neg_owner[:, 0], neg_row, zero, zero, zero, zero])
    vmem = pl.BlockSpec(memory_space=pltpu.VMEM)
    dma = pltpu.SemaphoreType.DMA
    scratch = [
        pltpu.VMEM((NC, 24, 128), F32),
        pltpu.VMEM((NC, 24, 128), F32),
        pltpu.VMEM((NC, CAP, E), BF16),
        pltpu.VMEM((NC, CAP, E), BF16),
        pltpu.VMEM((NN, NC * CAP), BF16),
        pltpu.VMEM((ROWS, NZ * 128), BF16),
        pltpu.VMEM((NQ, E), BF16),
        pltpu.VMEM((NI, E), BF16),
        pltpu.VMEM((NN, E), BF16),
        pltpu.VMEM((NN, E), BF16),
        pltpu.VMEM((NI + NN, 1), F32),
        pltpu.VMEM((NI, NQ), F32),
        pltpu.VMEM((NN, NQ), F32),
        pltpu.VMEM((2 * NB, QB), F32),
        pltpu.VMEM((2 * NB, QB), F32),
        pltpu.VMEM((NX, 2 * NB, QB), F32),
        pltpu.VMEM((NY, 2 * NB, QB), F32),
        pltpu.VMEM((NI + NN, NQ), BF16),
        pltpu.VMEM((2, NZ, 2 * CH, H), F32),
        pltpu.VMEM((2, NZ - 1, 2 * CH + 16, H), I16),
        pltpu.VMEM((2, NZ - 1, 2 * CH + 16, H), I16),
        pltpu.VMEM((NZ, 2, CH + 16, H), I16),
        pltpu.VMEM((NC, 8, H), F32),
        pltpu.VMEM((NC, 8, H), F32),
        pltpu.VMEM((NZ, 2, 128 + 16, H), I16),
        pltpu.VMEM((ROWS, E), BF16),
        pltpu.VMEM((ROWS, E), BF16),
        pltpu.VMEM((NC // 2, 2, CH, E), F32),
        pltpu.VMEM((NC // 2, CH, E), F32),
        pltpu.VMEM((NC // 2, CH + 16, E), I16),
        pltpu.VMEM((NC // 2, CH + 16, E), I16),
        dma((NC,)), dma((NC,)),
        dma((NC,)), dma((NC,)),
        dma, dma,
        dma((NX,)), dma((NX,)),
        dma((NY,)), dma((NY,)),
        dma((2, NZ - 1)), dma((2, NZ - 1)),
        dma((2, 4, 2)), dma((2, 4, 2)),
        dma((NC,)), dma((NC,)),
        dma((2, 4, 2)), dma((2, 4, 2)),
        dma, dma,
        dma((NC // 2,)), dma((NC // 2,)),
    ]
    loss, query_grad, item_grad, cache_grad = pl.pallas_call(
        kernel,
        out_shape=(
            jax.ShapeDtypeStruct((NB, QB), F32),
            jax.ShapeDtypeStruct((CH, E), F32),
            jax.ShapeDtypeStruct((NI, E), F32),
            jax.ShapeDtypeStruct((ROWS, E), F32),
        ),
        in_specs=[vmem] * 5,
        out_specs=(vmem,) * 4,
        scratch_shapes=scratch,
        compiler_params=pltpu.CompilerParams(
            collective_id=0, has_side_effects=True, vmem_limit_bytes=62 * 1024 * 1024
        ),
    )(queries, positive.reshape(1, NQ), items, small, cache)
    return loss.reshape(NQ), query_grad, item_grad, cache_grad


def solution(mesh):
    placed = (
        P("pb", None),
        P("pb"),
        P("col", None),
        P("col"),
        P("col", None),
        P("col", None),
        P("col"),
        P("col"),
    )
    return jax.shard_map(
        body,
        mesh=mesh,
        in_specs=placed,
        out_specs=(P("pb"), P(("pb", "col"), None), P("col", None), P("col", None)),
        check_vma=False,
    )
```

```python
import functools

import jax
import jax.numpy as jnp
from jax import lax
from jax.experimental import pallas as pl
from jax.experimental.pallas import tpu as pltpu
from jax.sharding import PartitionSpec as P

MESH = pl.DeviceIdType.MESH
F32 = jnp.float32
BF16 = jnp.bfloat16
I32 = jnp.int32
I16 = jnp.int16

E = 512
H = E // 2
NQ = 2048
QB = 256
NB = NQ // QB
NI = 512
NN = 512
NC = 32
NX = 4
NY = 4
NZ = 8
CAP = 32
ROWS = 1024
CH = 64
INV_T = 20.0
NG = 2 * NX
W = E // 4
RB = 256


def iota(shape, dim):
    return lax.broadcasted_iota(I32, shape, dim)


def onehot(cond):
    return jnp.where(cond, 1.0, 0.0).astype(BF16)


def dot_nn(a, b):
    return lax.dot_general(a, b, (((1,), (0,)), ((), ())), preferred_element_type=F32)


def dot_nt(a, b):
    return lax.dot_general(a, b, (((1,), (1,)), ((), ())), preferred_element_type=F32)


def dot_tn(a, b):
    return lax.dot_general(a, b, (((0,), (0,)), ((), ())), preferred_element_type=F32)


def halves(x):
    hi = x.astype(BF16)
    return hi, (x - hi.astype(F32)).astype(BF16)


def encode(x, group):
    rows, width = x.shape
    cube = x.reshape(rows // group, group, width)
    top = jnp.max(jnp.abs(cube), axis=0)
    expo = jnp.ceil(jnp.log2(jnp.maximum(top, 1e-30)))
    code = jnp.round(cube * jnp.exp2(14.99 - expo)[None])
    return code.reshape(rows, width).astype(I32).astype(I16), expo


def decode(code, expo):
    rows, width = code.shape
    group = expo.shape[0]
    cube = code.astype(I32).astype(F32).reshape(rows // group, group, width)
    return (cube * jnp.exp2(expo - 14.99)[None]).reshape(rows, width)


def to_i16(x):
    return x.astype(I32).astype(I16)


def from_i16(x):
    return x.astype(I32).astype(F32)


def unit(x):
    scale = jnp.sqrt(jnp.sum(x * x, axis=1, keepdims=True) + 1e-06)
    return x * (1.0 / scale), scale


def unit_back(grad, rows):
    direction, scale = unit(rows)
    return (grad - direction * jnp.sum(grad * direction, axis=1, keepdims=True)) / scale


def kernel(
    queries_hbm, positive, items_hbm, counts_i_ref, counts_n_ref, owner_ref, row_ref, cache_hbm,
    loss_out, query_out, item_out, hi_out, lo_out, asked_out,
    queries, items, cache, msg, mrecv, rows_buf, fetched, perm, select, q_unit, cand_i, cand_n, cand, negs, shift,
    expo_i, expo_n, pos1, pos2, tot1, tot2, inverse_total, weight, part, rs_send, rs_recv,
    ag_item, sel_out, n_recv, ag_cache, q_part, q_core, q_msg, q_recv,
    in_s, m_s, m_r, f_s, f_r, p1_s, p1_r, p2_s, p2_r, t1_s, t1_r, t2_s, t2_r, rs_s, rs_r, ai_s, ai_r, n_s, n_r,
    ac_s, ac_r, qc_s, qc_r, qd_s, qd_r,
):
    me = lax.axis_index("col")
    z = lax.axis_index("pb")
    core = me % 2
    chip = me // 2
    my_g = me % NG
    my_y = me // NG
    up = (z + 1) % NZ
    down = (z + NZ - 1) % NZ
    sibling = chip * 2 + 1 - core

    barrier = pltpu.get_barrier_semaphore()

    @pl.loop(1, NC)
    def _(s):
        pl.semaphore_signal(barrier, inc=1, device_id={"col": (me + s) % NC}, device_id_type=MESH)

    for other in (up, down):
        pl.semaphore_signal(barrier, inc=1, device_id={"pb": other}, device_id_type=MESH)

    loads = [
        pltpu.make_async_copy(src, dst, in_s.at[i])
        for i, (src, dst) in enumerate(((cache_hbm, cache), (items_hbm, items), (queries_hbm, queries)))
    ]
    for load in loads:
        load.start()

    def remote(src, dst, send, recv, **where):
        return pltpu.make_async_remote_copy(
            src_ref=src, dst_ref=dst, send_sem=send, recv_sem=recv, device_id=where, device_id_type=MESH
        )

    counts_i = counts_i_ref[...]
    counts_n = counts_n_ref[...]
    owner = owner_ref[...]
    row = row_ref[...]
    table = jnp.where(iota((NC, NN), 0) == owner, 1.0, 0.0)
    before = onehot(iota((NN, NN), 0) < iota((NN, NN), 1))
    earlier = dot_nn(table.astype(BF16), before)
    rank = jnp.sum(earlier * table, axis=0, keepdims=True).astype(I32)
    per_owner = jnp.sum(table, axis=1, keepdims=True)
    first = jnp.sum(jnp.where(iota((NC, NN), 0) < owner, per_owner, 0.0), axis=0, keepdims=True).astype(I32)
    place = first + rank
    plane = place & (NZ - 1)
    index = place >> 3
    slot4 = rank >> 3
    slot = 4 * plane + slot4

    row_hi = (row >> 5).astype(F32)
    row_lo = (row & 31).astype(F32)
    to_plane = jnp.where(iota((NC * NZ, NN), 0) == NZ * owner + plane, 1.0, 0.0)
    lane1 = onehot(iota((128, NN), 0) == 4 * me + slot4)
    asked_msg = dot_nt((to_plane * row_hi).astype(BF16), lane1) * 32.0 + dot_nt(
        (to_plane * row_lo).astype(BF16), lane1
    )
    msg[:, 0:8, :] = asked_msg.reshape(NC, NZ, 128)
    lane2 = onehot(iota((128, NN), 0) == CAP * (me % 4) + slot)
    asked_rows = dot_nt((table * row_hi).astype(BF16), lane2) * 32.0 + dot_nt((table * row_lo).astype(BF16), lane2)
    mine = iota((NC, 8, 128), 1) == me // 4
    msg[:, 8:16, :] = jnp.where(mine, asked_rows.reshape(NC, 1, 128), 0.0)
    total_i = jnp.sum(counts_i.astype(F32), axis=1, keepdims=True)
    total_n = jnp.sum(counts_n.astype(F32), axis=1, keepdims=True)
    totals = jnp.where(iota((8, 128), 0) < 4, total_i, total_n)
    msg[:, 16:24, :] = jnp.broadcast_to(totals[None], (NC, 8, 128))

    pl.semaphore_wait(barrier, NC + 1)

    @pl.loop(1, NC)
    def _(s):
        other = (me + s) % NC
        remote(msg.at[other], mrecv.at[me], m_s.at[other], m_r.at[me], col=other).start()

    mrecv[me] = msg[me]

    ordered = jnp.where(iota((NN, NN), 0) == CH * plane + index, 1.0, 0.0)
    by_slot = onehot(iota((NC * CAP, NN), 0) == CAP * owner + slot)
    perm[...] = dot_nt(ordered.astype(BF16), by_slot).astype(BF16)
    loads[0].wait()

    @pl.loop(1, NC)
    def _(s):
        other = (me + s) % NC
        remote(msg.at[other], mrecv.at[other], m_s.at[other], m_r.at[other], col=other).wait()

    asked = jnp.sum(mrecv[...], axis=0)
    asked_out[...] = asked[0:8, :]

    by_sender = jnp.concatenate([asked[8:16, :], jnp.zeros((120, 128), F32)], axis=0).T

    @pl.loop(0, NC // 4)
    def _(s):
        group = (me // 4 + s) % (NC // 4)
        wanted = jnp.sum(jnp.where(iota((128, 128), 1) == group, by_sender, 0.0), axis=1, keepdims=True)
        pick = onehot(iota((128, ROWS), 1) == wanted.astype(I32))
        found = dot_nn(pick, cache[...]).astype(BF16).reshape(4, CAP, E)
        for i in range(4):
            other = group * 4 + i
            rows_buf[other] = found[i]

            @pl.when(other != me)
            def _():
                remote(rows_buf.at[other], fetched.at[me], f_s.at[other], f_r.at[me], col=other).start()

            @pl.when(other == me)
            def _():
                fetched[me] = found[i]

    log_i = jnp.log(
        jnp.sum(
            jnp.where(iota((NI, NI), 0) == iota((NI, NI), 1), counts_i.astype(F32), 0.0), axis=1, keepdims=True
        )
    )
    log_n = jnp.log(jnp.sum(ordered * counts_n.astype(F32), axis=1, keepdims=True))
    shift[0:NI, :] = log_i - jnp.log(asked[16:17, 0:1])
    shift[NI:, :] = log_n - jnp.log(asked[20:21, 0:1])
    loads[1].wait()
    item_unit = unit(items[...].astype(F32))[0].astype(BF16)
    cand_i[...] = item_unit
    cand[:, 0:CH, :] = item_unit.reshape(NZ, CH, E)
    loads[2].wait()
    first_item = me * NI

    @pl.loop(0, NB)
    def _(b):
        at = pl.ds(pl.multiple_of(b * QB, QB), QB)
        q_rows = unit(queries[at, :].astype(F32))[0].astype(BF16)
        q_unit[at, :] = q_rows
        logits = dot_nt(cand_i[...], q_rows) * INV_T - shift[0:NI, :]
        hit = positive[:, at] == first_item + iota((NI, QB), 0)
        expo = jnp.exp(logits)
        expo_i[:, at] = expo
        tot1[my_g, pl.ds(b, 1), :] = jnp.sum(expo, axis=0, keepdims=True)
        pos1[my_g, pl.ds(b, 1), :] = jnp.sum(jnp.where(hit, logits, 0.0), axis=0, keepdims=True)

    def group_copy(ref, send, recv, s, mine):
        other = (my_g + s) % NG
        slot = my_g if mine else other
        return remote(ref.at[my_g], ref.at[slot], send.at[other], recv.at[slot], col=my_y * NG + other)

    def y_copy(ref, send, recv, s, mine):
        other = (my_y + s) % NY
        slot = my_y if mine else other
        return remote(ref.at[my_y], ref.at[slot], send.at[other], recv.at[slot], col=other * NG + my_g)

    for s in range(1, NG):
        group_copy(pos1, p1_s, p1_r, s, True).start()

    q_row = iota((NC * 8, NN), 0)
    sel_slot = onehot(CAP * owner + slot == CAP * (q_row >> 3) + 4 * z + (q_row & 3))
    sel_index = onehot((iota((CH, NN), 0) == index) & (plane == z))
    select[...] = dot_nt(sel_slot, sel_index).astype(BF16)

    @pl.loop(1, NC)
    def _(s):
        other = (me + s) % NC
        remote(rows_buf.at[other], fetched.at[other], f_s.at[other], f_r.at[other], col=other).wait()

    neg_rows = dot_nn(perm[...], fetched[...].reshape(NC * CAP, E))
    negs[...] = neg_rows.astype(BF16)
    neg_unit = unit(neg_rows)[0].astype(BF16)
    cand_n[...] = neg_unit
    cand[:, CH:, :] = neg_unit.reshape(NZ, CH, E)

    @pl.loop(0, NB)
    def _(b):
        at = pl.ds(pl.multiple_of(b * QB, QB), QB)
        expo = jnp.exp(dot_nt(cand_n[...], q_unit[at, :]) * INV_T - shift[NI:, :])
        expo_n[:, at] = expo
        tot1[my_g, pl.ds(b, 1), :] = tot1[my_g, pl.ds(b, 1), :] + jnp.sum(expo, axis=0, keepdims=True)

    for s in range(1, NG):
        group_copy(tot1, t1_s, t1_r, s, True).start()
    for s in range(1, NG):
        group_copy(pos1, p1_s, p1_r, s, False).wait()
    pos2[my_y] = jnp.sum(pos1[...], axis=0)
    for s in range(1, NY):
        y_copy(pos2, p2_s, p2_r, s, True).start()
    for s in range(1, NG):
        group_copy(tot1, t1_s, t1_r, s, False).wait()
    tot2[my_y] = jnp.sum(tot1[...], axis=0)
    for s in range(1, NY):
        y_copy(tot2, t2_s, t2_r, s, True).start()
    for s in range(1, NY):
        y_copy(tot2, t2_s, t2_r, s, False).wait()
    total = jnp.sum(tot2[...], axis=0)
    inverse_total[...] = 1.0 / total

    @pl.loop(0, NB)
    def _(b):
        at = pl.ds(pl.multiple_of(b * QB, QB), QB)
        inverse = inverse_total[pl.ds(b, 1), :]
        hit = positive[:, at] == first_item + iota((NI, QB), 0)
        weight_i = (expo_i[:, at] * inverse - jnp.where(hit, 1.0, 0.0)).astype(BF16)
        weight[:, 0:CH, at] = weight_i.reshape(NZ, CH, QB)
        weight[:, CH:, at] = (expo_n[:, at] * inverse).astype(BF16).reshape(NZ, CH, QB)

    def cand_part(pair):
        at = pl.ds(pair * 2, 2)
        grad = dot_nn(weight[at].reshape(4 * CH, NQ), q_unit[...]) * INV_T
        for k in range(4):
            part[k, at] = grad[:, k * W : (k + 1) * W].reshape(2, 2 * CH, W)

    def ring_peer(d):
        return up if d == 0 else down

    def ring_chunk(d, t):
        return (z + 2 * NZ - 1 - t) % NZ if d == 0 else (z + 1 + t) % NZ

    def pack(ref, chunk):
        code, e = encode(chunk[0:CH], 8)
        ref[0:CH] = code
        code, e2 = encode(chunk[CH:], 8)
        ref[CH : 2 * CH] = code
        ref[2 * CH :] = to_i16(jnp.concatenate([e, e2], axis=0))

    def unpack(ref):
        e = from_i16(ref[2 * CH :])
        return jnp.concatenate([decode(ref[0:CH], e[0:8]), decode(ref[CH : 2 * CH], e[8:16])], axis=0)

    def rs_copy(k, t):
        return remote(
            rs_send.at[k, t], rs_recv.at[k, t], rs_s.at[k, t], rs_r.at[k, t], pb=ring_peer(k // 2)
        )

    def rs_first(d):
        for k in (2 * d, 2 * d + 1):
            pack(rs_send.at[k, 0], part[k, ring_chunk(d, 0)])
            rs_copy(k, 0).start()

    pair = ((z + NZ - 1) % NZ) // 2
    cand_part(pair)
    rs_first(0)
    cand_part((pair + 1) % (NZ // 2))
    rs_first(1)
    cand_part((pair + 2) % (NZ // 2))
    cand_part((pair + 3) % (NZ // 2))

    def q_block(b):
        at = pl.ds(pl.multiple_of(b * QB, QB), QB)
        grad = dot_tn(weight[:, :, at].reshape(NI + NN, QB), cand[...].reshape(NI + NN, E)) * INV_T
        q_part[pl.ds(b * 2, 2)] = grad.reshape(2, 2, CH, E)

    def q_code(c):
        code, e = encode(q_part[c, core] + q_core[c], 16)
        q_msg[c, 0:CH] = code
        q_msg[c, CH:] = to_i16(e)

    q_copy = remote(q_part.at[:, 1 - core], q_core, qc_s, qc_r, col=sibling)
    for t in range(1, NZ - 1):
        for s in range(2):
            for d in range(2):
                k = 2 * d + s
                rs_copy(k, t - 1).wait()
                pack(rs_send.at[k, t], part[k, ring_chunk(d, t)] + unpack(rs_recv.at[k, t - 1]))
                rs_copy(k, t).start()
        if t <= 4:
            q_block(2 * t - 2)
            q_block(2 * t - 1)
        if t == 4:
            q_copy.start()
        if t == 5:
            for s in range(1, NY):
                y_copy(pos2, p2_s, p2_r, s, False).wait()
            loss = jnp.log(total) - jnp.sum(pos2[...], axis=0)
            for b in range(NB):
                for half in range(2):
                    loss_out[2 * b + half : 2 * b + half + 1, :] = loss[b : b + 1, half * 128 : (half + 1) * 128]
        if t == 6:
            q_copy.wait()

            @pl.loop(0, NC // 4)
            def _(c):
                q_code(c)

    for k in range(4):
        rs_copy(k, NZ - 2).wait()
    own = jnp.concatenate([part[k, z] + unpack(rs_recv.at[k, NZ - 2]) for k in range(4)], axis=1)

    mine_at = pl.ds(pl.multiple_of(z * CH, CH), CH)
    neg_grad = unit_back(own[CH:], negs[mine_at, :].astype(F32))
    hi, lo = halves(neg_grad)
    wide = dot_nn(select[...], hi) + dot_nn(select[...], lo)
    left = (iota((NC * 8, H), 0) & 4) == 0
    sel_out[...] = jnp.where(left, wide[:, :H], wide[:, H:]).reshape(NC, 8, H)

    @pl.loop(1, NC)
    def _(s):
        other = (me + s) % NC
        remote(sel_out.at[other], n_recv.at[me], n_s.at[other], n_r.at[me], col=other).start()

    n_recv[me] = sel_out[me]

    item_grad = unit_back(own[0:CH], items[mine_at, :].astype(F32))
    for h in range(2):
        code, e = encode(item_grad[:, h * H : (h + 1) * H], 16)
        ag_item[z, h, 0:CH] = code
        ag_item[z, h, CH:] = to_i16(e)

    def gather_copy(ref, send, recv, d, s, h):
        source = (z + 2 * NZ - s) % NZ if d == 0 else (z + s) % NZ
        return remote(
            ref.at[source, h], ref.at[source, h], send.at[d, s, h], recv.at[d, s, h], pb=ring_peer(d)
        )

    def steps(d, h):
        return 4 if d == h else 3

    def gather_start(ref, send, recv, s):
        for i in range(2):
            for d in range(2):
                h = d if i == 0 else 1 - d
                if s < steps(d, h):
                    if s > 0:
                        gather_copy(ref, send, recv, d, s - 1, h).wait()
                    gather_copy(ref, send, recv, d, s, h).start()

    def gather_finish(ref, send, recv):
        for d in range(2):
            for h in range(2):
                gather_copy(ref, send, recv, d, steps(d, h) - 1, h).wait()

    gather_start(ag_item, ai_s, ai_r, 0)

    @pl.loop(NC // 4, NC // 2)
    def _(c):
        q_code(c)

    gather_start(ag_item, ai_s, ai_r, 1)

    @pl.loop(1, NC)
    def _(s):
        other = (me + s) % NC
        remote(sel_out.at[other], n_recv.at[other], n_s.at[other], n_r.at[other], col=other).wait()

    received = halves(n_recv[...].reshape(NC * 8, H))
    want = iota((128, NC * 8), 0)
    have = iota((128, NC * 8), 1)
    for h in range(2):
        order = onehot(have == 8 * (want >> 2) + 4 * h + (want & 3))
        code, e = encode(dot_nn(order, received[0]) + dot_nn(order, received[1]), 16)
        ag_cache[z, h, 0:128] = code
        ag_cache[z, h, 128:] = to_i16(e)

    gather_start(ag_cache, ac_s, ac_r, 0)

    @pl.loop(1, NC // 2)
    def _(s):
        other = (chip + s) % (NC // 2)
        remote(q_msg.at[other], q_recv.at[chip], qd_s.at[other], qd_r.at[chip], col=other * 2 + core).start()

    q_recv[chip] = q_msg[chip]

    def cache_rows(p):
        at = pl.ds(pl.multiple_of(p * 128, 128), 128)
        for h in range(2):
            hi, lo = halves(decode(ag_cache[p, h, 0:128], from_i16(ag_cache[p, h, 128:])))
            hi_out[at, h * H : (h + 1) * H] = hi
            lo_out[at, h * H : (h + 1) * H] = lo

    gather_start(ag_item, ai_s, ai_r, 2)
    cache_rows(z)
    gather_start(ag_item, ai_s, ai_r, 3)
    gather_start(ag_cache, ac_s, ac_r, 1)
    for d in range(2):
        cache_rows((z + 2 * NZ - 1) % NZ if d == 0 else (z + 1) % NZ)
    gather_finish(ag_item, ai_s, ai_r)

    @pl.loop(0, NZ)
    def _(p):
        at = pl.ds(pl.multiple_of(p * CH, CH), CH)
        for h in range(2):
            item_out[at, h * H : (h + 1) * H] = decode(ag_item[p, h, 0:CH], from_i16(ag_item[p, h, CH:]))

    gather_start(ag_cache, ac_s, ac_r, 2)
    for d in range(2):
        cache_rows((z + 2 * NZ - 2) % NZ if d == 0 else (z + 2) % NZ)

    gather_start(ag_cache, ac_s, ac_r, 3)

    @pl.loop(1, NC // 2)
    def _(s):
        other = (chip + s) % (NC // 2)
        remote(q_msg.at[other], q_recv.at[other], qd_s.at[other], qd_r.at[other], col=other * 2 + core).wait()

    q_grad = decode(q_recv[0, 0:CH], from_i16(q_recv[0, CH:]))
    for c in range(1, NC // 2):
        q_grad = q_grad + decode(q_recv[c, 0:CH], from_i16(q_recv[c, CH:]))
    query_out[...] = unit_back(q_grad, queries[pl.ds(pl.multiple_of(me * CH, CH), CH), :].astype(F32))

    gather_finish(ag_cache, ac_s, ac_r)
    for d in range(2):
        cache_rows((z + 2 * NZ - 3) % NZ if d == 0 else (z + 3) % NZ)
    cache_rows((z + 4) % NZ)


def last(asked, hi, lo, loss, query, item, loss_out, query_out, item_out, cache_out, scat):
    r = pl.program_id(0)
    for p in range(NZ):
        rows = iota((RB, 128), 0) + r * RB
        scat[:, p * 128 : (p + 1) * 128] = onehot(rows == asked[p : p + 1, :].astype(I32))
    cache_out[...] = dot_nn(scat[...], hi[...]) + dot_nn(scat[...], lo[...])
    item_out[...] = item[...]

    @pl.when(r == 0)
    def _():
        loss_out[...] = loss[...]
        query_out[...] = query[...]


def body(queries, positive, items, item_counts, cache, neg_owner, neg_row, neg_counts):
    vmem = pl.BlockSpec(memory_space=pltpu.VMEM)
    hbm = pl.BlockSpec(memory_space=pl.ANY)
    dma = pltpu.SemaphoreType.DMA
    scratch = [
        pltpu.VMEM((NQ, E), BF16),
        pltpu.VMEM((NI, E), BF16),
        pltpu.VMEM((ROWS, E), BF16),
        pltpu.VMEM((NC, 24, 128), F32),
        pltpu.VMEM((NC, 24, 128), F32),
        pltpu.VMEM((NC, CAP, E), BF16),
        pltpu.VMEM((NC, CAP, E), BF16),
        pltpu.VMEM((NN, NC * CAP), BF16),
        pltpu.VMEM((NC * 8, CH), BF16),
        pltpu.VMEM((NQ, E), BF16),
        pltpu.VMEM((NI, E), BF16),
        pltpu.VMEM((NN, E), BF16),
        pltpu.VMEM((NZ, 2 * CH, E), BF16),
        pltpu.VMEM((NN, E), BF16),
        pltpu.VMEM((NI + NN, 1), F32),
        pltpu.VMEM((NI, NQ), F32),
        pltpu.VMEM((NN, NQ), F32),
        pltpu.VMEM((NG, NB, QB), F32),
        pltpu.VMEM((NY, NB, QB), F32),
        pltpu.VMEM((NG, NB, QB), F32),
        pltpu.VMEM((NY, NB, QB), F32),
        pltpu.VMEM((NB, QB), F32),
        pltpu.VMEM((NZ, 2 * CH, NQ), BF16),
        pltpu.VMEM((4, NZ, 2 * CH, W), F32),
        pltpu.VMEM((4, NZ - 1, 2 * CH + 16, W), I16),
        pltpu.VMEM((4, NZ - 1, 2 * CH + 16, W), I16),
        pltpu.VMEM((NZ, 2, CH + 16, H), I16),
        pltpu.VMEM((NC, 8, H), F32),
        pltpu.VMEM((NC, 8, H), F32),
        pltpu.VMEM((NZ, 2, 128 + 16, H), I16),
        pltpu.VMEM((NC // 2, 2, CH, E), F32),
        pltpu.VMEM((NC // 2, CH, E), F32),
        pltpu.VMEM((NC // 2, CH + 16, E), I16),
        pltpu.VMEM((NC // 2, CH + 16, E), I16),
        dma((3,)),
        dma((NC,)), dma((NC,)),
        dma((NC,)), dma((NC,)),
        dma((NG,)), dma((NG,)),
        dma((NY,)), dma((NY,)),
        dma((NG,)), dma((NG,)),
        dma((NY,)), dma((NY,)),
        dma((4, NZ - 1)), dma((4, NZ - 1)),
        dma((2, 4, 2)), dma((2, 4, 2)),
        dma((NC,)), dma((NC,)),
        dma((2, 4, 2)), dma((2, 4, 2)),
        dma, dma,
        dma((NC // 2,)), dma((NC // 2,)),
    ]
    loss, query_grad, item_grad, hi, lo, asked = pl.pallas_call(
        kernel,
        out_shape=(
            jax.ShapeDtypeStruct((NQ // 128, 128), F32),
            jax.ShapeDtypeStruct((CH, E), F32),
            jax.ShapeDtypeStruct((NI, E), F32),
            jax.ShapeDtypeStruct((NZ * 128, E), BF16),
            jax.ShapeDtypeStruct((NZ * 128, E), BF16),
            jax.ShapeDtypeStruct((NZ, 128), F32),
        ),
        in_specs=[hbm, vmem, hbm, vmem, vmem, vmem, vmem, hbm],
        out_specs=(vmem,) * 6,
        scratch_shapes=scratch,
        compiler_params=pltpu.CompilerParams(
            collective_id=0, has_side_effects=True, vmem_limit_bytes=62 * 1024 * 1024
        ),
    )(
        queries,
        positive.reshape(1, NQ),
        items,
        item_counts.reshape(1, NI),
        neg_counts.reshape(1, NN),
        neg_owner.reshape(1, NN),
        neg_row.reshape(1, NN),
        cache,
    )

    def whole(*shape):
        return pl.BlockSpec(shape, lambda r: (0,) * len(shape))

    steps = ROWS // RB
    loss, query_grad, item_grad, cache_grad = pl.pallas_call(
        last,
        grid=(steps,),
        out_shape=(
            jax.ShapeDtypeStruct((NQ // 128, 128), F32),
            jax.ShapeDtypeStruct((CH, E), F32),
            jax.ShapeDtypeStruct((NI, E), F32),
            jax.ShapeDtypeStruct((ROWS, E), F32),
        ),
        in_specs=[
            whole(NZ, 128),
            whole(NZ * 128, E),
            whole(NZ * 128, E),
            whole(NQ // 128, 128),
            whole(CH, E),
            pl.BlockSpec((NI // steps, E), lambda r: (r, 0)),
        ],
        out_specs=(
            whole(NQ // 128, 128),
            whole(CH, E),
            pl.BlockSpec((NI // steps, E), lambda r: (r, 0)),
            pl.BlockSpec((RB, E), lambda r: (r, 0)),
        ),
        scratch_shapes=[pltpu.VMEM((RB, NZ * 128), BF16)],
        compiler_params=pltpu.CompilerParams(vmem_limit_bytes=32 * 1024 * 1024),
    )(asked, hi, lo, loss, query_grad, item_grad)
    return loss.reshape(NQ), query_grad, item_grad, cache_grad


def solution(mesh):
    placed = (
        P("pb", None),
        P("pb"),
        P("col", None),
        P("col"),
        P("col", None),
        P("col", None),
        P("col"),
        P("col"),
    )
    return jax.shard_map(
        body,
        mesh=mesh,
        in_specs=placed,
        out_specs=(P("pb"), P(("pb", "col"), None), P("col", None), P("col", None)),
        check_vma=False,
    )
```

```python
import jax
import jax.numpy as jnp
from jax import lax
from jax.experimental import pallas as pl
from jax.experimental.pallas import tpu as pltpu
from jax.sharding import PartitionSpec as P

MESH = pl.DeviceIdType.MESH
F32 = jnp.float32
BF16 = jnp.bfloat16
I32 = jnp.int32
I16 = jnp.int16

E = 512
H = E // 2
NQ = 2048
QB = 256
NB = NQ // QB
NI = 512
NN = 512
NS = 1024
NC = 32
NZ = 8
CAP = 32
ROWS = 1024
CH = 64
INV_T = 20.0
PB = 2
W = E // 4
CR = ROWS // NZ
LN2 = 0.6931471805599453
SCALE2 = INV_T / LN2


def iota(shape, dim):
    return lax.broadcasted_iota(I32, shape, dim)


def onehot(cond):
    return jnp.where(cond, 1.0, 0.0).astype(BF16)


def dot_nn(a, b):
    return lax.dot_general(a, b, (((1,), (0,)), ((), ())), preferred_element_type=F32)


def dot_nt(a, b):
    return lax.dot_general(a, b, (((1,), (1,)), ((), ())), preferred_element_type=F32)


def dot_tn(a, b):
    return lax.dot_general(a, b, (((0,), (0,)), ((), ())), preferred_element_type=F32)


def halves(x):
    hi = x.astype(BF16)
    return hi, (x - hi.astype(F32)).astype(BF16)


def encode(x, group):
    rows, width = x.shape
    cube = x.reshape(rows // group, group, width)
    top = jnp.max(jnp.abs(cube), axis=0)
    expo = jnp.ceil(jnp.log2(jnp.maximum(top, 1e-30)))
    code = jnp.round(cube * jnp.exp2(14.99 - expo)[None])
    return code.reshape(rows, width).astype(I32).astype(I16), expo


def decode(code, expo):
    rows, width = code.shape
    group = expo.shape[0]
    cube = code.astype(I32).astype(F32).reshape(rows // group, group, width)
    return (cube * jnp.exp2(expo - 14.99)[None]).reshape(rows, width)


def to_i16(x):
    return x.astype(I32).astype(I16)


def from_i16(x):
    return x.astype(I32).astype(F32)


def unit(x):
    scale = jnp.sqrt(jnp.sum(x * x, axis=1, keepdims=True) + 1e-06)
    return x * (1.0 / scale), scale


def unit_back(grad, rows):
    direction, scale = unit(rows)
    return (grad - direction * jnp.sum(grad * direction, axis=1, keepdims=True)) / scale


def kernel(
    queries_hbm, positive, items_hbm, counts_i_ref, counts_n_ref, owner_ref, row_ref, cache_hbm,
    loss_out, query_out, item_codes, cache_codes,
    queries, items, cache, msg, mrecv, cache_unit, scat, q_unit, cand_i, cand_n, shift_n,
    expo_i, expo_n, pos, tot, factor_i, factor_n, weight_i, weight_n, part_i, part_n, slot_hi, slot_lo,
    send_i, recv_i, send_n, recv_n, ag_item, ag_cache, q_part, q_core, q_msg, q_recv,
    in_s, m_s, m_r, p_s, p_r, t_s, t_r, ri_s, ri_r, rn_s, rn_r, ai_s, ai_r, ac_s, ac_r, oi_s, oc_s,
    qc_s, qc_r, qd_s, qd_r,
):
    me = lax.axis_index("col")
    z = lax.axis_index("pb")
    core = me % 2
    chip = me // 2
    my_g = me // 4
    up = (z + 1) % NZ
    down = (z + NZ - 1) % NZ
    sibling = chip * 2 + 1 - core

    barrier = pltpu.get_barrier_semaphore()

    @pl.loop(1, NC)
    def _(s):
        pl.semaphore_signal(barrier, inc=1, device_id={"col": (me + s) % NC}, device_id_type=MESH)

    for other in (up, down):
        pl.semaphore_signal(barrier, inc=1, device_id={"pb": other}, device_id_type=MESH)

    loads = [
        pltpu.make_async_copy(src, dst, in_s.at[i])
        for i, (src, dst) in enumerate(((items_hbm, items), (queries_hbm, queries), (cache_hbm, cache)))
    ]
    for load in loads:
        load.start()

    def remote(src, dst, send, recv, **where):
        return pltpu.make_async_remote_copy(
            src_ref=src, dst_ref=dst, send_sem=send, recv_sem=recv, device_id=where, device_id_type=MESH
        )

    counts_i = counts_i_ref[...].astype(F32)
    counts_n = counts_n_ref[...].astype(F32)
    owner = owner_ref[...]
    row = row_ref[...]
    table = jnp.where(iota((NC, NN), 0) == owner, 1.0, 0.0)
    before = onehot(iota((NN, NN), 0) < iota((NN, NN), 1))
    earlier = dot_nn(table.astype(BF16), before)
    rank = jnp.sum(earlier * table, axis=0, keepdims=True).astype(I32)
    lane = onehot(iota((128, NN), 0) == CAP * (me % 4) + rank)
    named = jnp.concatenate(
        [table * (row >> 5).astype(F32), table * (row & 31).astype(F32), table * counts_n], axis=0
    )
    named = dot_nt(named.astype(BF16), lane)
    named = named[0:NC] * 32.0 + named[NC : 2 * NC] + named[2 * NC :] * ROWS
    total_i = jnp.sum(counts_i, axis=1, keepdims=True).reshape(1, 1, 1)
    total_n = jnp.sum(counts_n, axis=1, keepdims=True).reshape(1, 1, 1)
    line = iota((NC, 8, 128), 1)
    totals = jnp.where(line == (my_g + 1) % 8, total_i, jnp.where(line == (my_g + 2) % 8, total_n, 0.0))
    msg[...] = jnp.where(line == my_g, named.reshape(NC, 1, 128), totals)

    pl.semaphore_wait(barrier, NC + 1)

    def to_all(ref, send, recv, s):
        other = (me + s) % NC
        return remote(ref.at[me], ref.at[me], send.at[other], recv.at[me], col=other)

    def from_all(ref, send, recv, s):
        other = (me + s) % NC
        return remote(ref.at[me], ref.at[other], send.at[other], recv.at[other], col=other)

    @pl.loop(1, NC)
    def _(s):
        other = (me + s) % NC
        remote(msg.at[other], mrecv.at[me], m_s.at[other], m_r.at[me], col=other).start()

    mrecv[me] = msg[me]

    loads[0].wait()
    cand_i[...] = unit(items[...].astype(F32))[0].astype(BF16)
    same = iota((NI, NI), 0) == iota((NI, NI), 1)
    shift_i = jnp.log2(jnp.sum(jnp.where(same, counts_i, 0.0), axis=1, keepdims=True))
    first_item = me * NI
    loads[1].wait()

    @pl.loop(0, NB)
    def _(b):
        at = pl.ds(pl.multiple_of(b * QB, QB), QB)
        q_rows = unit(queries[at, :].astype(F32))[0].astype(BF16)
        q_unit[at, :] = q_rows
        logits = dot_nt(cand_i[...], q_rows) * SCALE2 - shift_i
        hit = positive[:, at] == first_item + iota((NI, QB), 0)
        expo = jnp.exp2(logits)
        expo_i[:, at] = expo
        factor_i[pl.ds(b, 1), :] = jnp.sum(expo, axis=0, keepdims=True)
        pos[me, pl.ds(b, 1), :] = jnp.sum(jnp.where(hit, logits, 0.0), axis=0, keepdims=True)

    loads[2].wait()

    @pl.loop(0, ROWS // QB)
    def _(b):
        at = pl.ds(pl.multiple_of(b * QB, QB), QB)
        cache_unit[at, :] = unit(cache[at, :].astype(F32))[0].astype(BF16)

    @pl.loop(1, NC)
    def _(s):
        other = (me + s) % NC
        remote(msg.at[other], mrecv.at[other], m_s.at[other], m_r.at[other], col=other).wait()

    line = iota((8, 128), 0)
    asked = jnp.zeros((8, 128), F32)
    sum_i = jnp.zeros((8, 128), F32)
    sum_n = jnp.zeros((8, 128), F32)
    for g in range(8):
        four = (mrecv[4 * g] + mrecv[4 * g + 1]) + (mrecv[4 * g + 2] + mrecv[4 * g + 3])
        asked = jnp.where(line == g, four, asked)
        sum_i = sum_i + jnp.where(line == (g + 1) % 8, four, 0.0)
        sum_n = sum_n + jnp.where(line == (g + 2) % 8, four, 0.0)
    total_i = jnp.sum(sum_i, axis=0, keepdims=True)[:, 0:1]
    total_n = jnp.sum(sum_n, axis=0, keepdims=True)[:, 0:1]

    @pl.loop(1, NC)
    def _(s):
        to_all(pos, p_s, p_r, s).start()

    def parts(value):
        count = jnp.floor(value * (1.0 / ROWS))
        return count, (value - count * ROWS).astype(I32)

    by_slot = jnp.concatenate([asked, jnp.zeros((120, 128), F32)], axis=0).T
    for g in range(8):
        count, wanted = parts(by_slot[:, g : g + 1])
        at = pl.ds(g * 128, 128)
        cand_n[at, :] = dot_nn(onehot(iota((128, ROWS), 1) == wanted), cache_unit[...]).astype(BF16)
        shift_n[at, :] = jnp.where(count > 0.5, jnp.log2(jnp.maximum(count, 1.0)), 1e30)

    @pl.loop(0, NB)
    def _(b):
        at = pl.ds(pl.multiple_of(b * QB, QB), QB)
        expo = jnp.exp2(dot_nt(cand_n[...], q_unit[at, :]) * SCALE2 - shift_n[...])
        expo_n[:, at] = expo
        sum_i = total_i * factor_i[pl.ds(b, 1), :]
        tot[me, pl.ds(b, 1), :] = sum_i + total_n * jnp.sum(expo, axis=0, keepdims=True)

    @pl.loop(1, NC)
    def _(s):
        to_all(tot, t_s, t_r, s).start()

    slots = parts(asked)[1]
    for g in range(8):
        scat[:, g * 128 : (g + 1) * 128] = onehot(iota((ROWS, 128), 0) == slots[g : g + 1, :])

    @pl.loop(1, NC)
    def _(s):
        from_all(tot, t_s, t_r, s).wait()

    total = jnp.sum(tot[...], axis=0)
    factor_i[...] = total_i / total
    factor_n[...] = total_n / total

    @pl.loop(0, NB)
    def _(b):
        at = pl.ds(pl.multiple_of(b * QB, QB), QB)
        hit = positive[:, at] == first_item + iota((NI, QB), 0)
        weight_i[:, at] = (expo_i[:, at] * factor_i[pl.ds(b, 1), :] - jnp.where(hit, 1.0, 0.0)).astype(BF16)
        weight_n[:, at] = (expo_n[:, at] * factor_n[pl.ds(b, 1), :]).astype(BF16)

    def ring_peer(d):
        return up if d == 0 else down

    def ring_chunk(d, t):
        return (z + 4 - t) % NZ if d == 0 else (z + 4 + t) % NZ

    def far(d, k):
        return k // 2 == d

    def pack(ref, chunk, rows):
        code, e = encode(chunk, 16)
        ref[0:rows] = code
        ref[rows:] = to_i16(e)

    def unpack(ref, rows):
        return decode(ref[0:rows], from_i16(ref[rows:]))

    def ring_copy(kind, d, t, k):
        _, send, recv, s, r, _ = kind
        return remote(send.at[d, t, k], recv.at[d, t, k], s.at[d, t, k], r.at[d, t, k], pb=ring_peer(d))

    def ring_first(kind):
        part, send, _, _, _, rows = kind
        for t in range(2):
            for k in range(4):
                for d in range(2):
                    if far(d, k) == (t == 0):
                        pack(send.at[d, t, k], part[k, ring_chunk(d, t)], rows)
                        ring_copy(kind, d, t, k).start()

    def ring_step(kind, t):
        part, send, recv, _, _, rows = kind
        for k in (0, 2, 1, 3):
            for d in range(2):
                if t > 1 or far(d, k):
                    ring_copy(kind, d, t - 1, k).wait()
                    got = unpack(recv.at[d, t - 1, k], rows)
                    pack(send.at[d, t, k], part[k, ring_chunk(d, t)] + got, rows)
                    ring_copy(kind, d, t, k).start()

    def ring_last(kind):
        part, _, recv, _, _, rows = kind
        columns = []
        for k in range(4):
            own = part[k, z]
            for d in range(2):
                ring_copy(kind, d, 3, k).wait()
                own = own + unpack(recv.at[d, 3, k], rows)
            columns.append(own)
        return jnp.concatenate(columns, axis=1)

    kind_i = (part_i, send_i, recv_i, ri_s, ri_r, CH)
    kind_n = (part_n, send_n, recv_n, rn_s, rn_r, CR)

    for half in range(2):
        grad = dot_nn(weight_i[half * 256 : (half + 1) * 256, :], q_unit[...]) * INV_T
        for k in range(4):
            part_i[k, half * 4 : (half + 1) * 4] = grad[:, k * W : (k + 1) * W].reshape(4, CH, W)
    ring_first(kind_i)

    @pl.loop(0, NS // 256)
    def _(b):
        at = pl.ds(pl.multiple_of(b * 256, 256), 256)
        hi, lo = halves(dot_nn(weight_n[at, :], q_unit[...]) * INV_T)
        slot_hi[at, :] = hi
        slot_lo[at, :] = lo

    @pl.loop(0, ROWS // 256)
    def _(b):
        at = pl.ds(pl.multiple_of(b * 256, 256), 256)
        grad = dot_nn(scat[at, :], slot_hi[...]) + dot_nn(scat[at, :], slot_lo[...])
        for k in range(4):
            part_n[k, pl.ds(b * 2, 2)] = grad[:, k * W : (k + 1) * W].reshape(2, CR, W)

    ring_first(kind_n)

    def q_block(b):
        at = pl.ds(pl.multiple_of(b * QB, QB), QB)
        grad = dot_tn(weight_i[:, at], cand_i[...]) + dot_tn(weight_n[:, at], cand_n[...])
        q_part[pl.ds(b * 2, 2)] = (grad * INV_T).reshape(2, 2, CH, E)

    q_copy = remote(q_part.at[:, 1 - core], q_core, qc_s, qc_r, col=sibling)
    q_block(0)
    q_block(1)
    ring_step(kind_i, 1)
    q_block(2)
    ring_step(kind_n, 1)
    q_block(3)
    q_block(4)
    ring_step(kind_i, 2)
    q_block(5)
    ring_step(kind_n, 2)
    q_block(6)
    q_block(7)
    q_copy.start()
    ring_step(kind_i, 3)

    @pl.loop(1, NC)
    def _(s):
        from_all(pos, p_s, p_r, s).wait()

    loss = jnp.log(total) - (jnp.sum(pos[...], axis=0) * LN2 + jnp.log(total_i))
    for b in range(NB):
        for half in range(2):
            loss_out[2 * b + half : 2 * b + half + 1, :] = loss[b : b + 1, half * 128 : (half + 1) * 128]
    ring_step(kind_n, 3)

    def gather_copy(ref, send, recv, d, s, h):
        source = (z + 2 * NZ - s) % NZ if d == 0 else (z + s) % NZ
        return remote(
            ref.at[source, h], ref.at[source, h], send.at[d, s, h], recv.at[d, s, h], pb=ring_peer(d)
        )

    def steps(d, h):
        return 4 if d == h else 3

    def out_copy(ref, out, sem, p, h):
        return pltpu.make_async_copy(ref.at[p, h], out.at[p, h], sem.at[p, h])

    def gather_wait(kind, d, s, h):
        ref, send, recv, out, sem = kind
        gather_copy(ref, send, recv, d, s, h).wait()
        source = (z + 2 * NZ - s - 1) % NZ if d == 0 else (z + s + 1) % NZ
        out_copy(ref, out, sem, source, h).start()

    def gather_first(kind, grad, rows):
        ref, send, recv, out, sem = kind
        for h in range(2):
            pack(ref.at[z, h], grad[:, h * H : (h + 1) * H], rows)
            for d in (h, 1 - h):
                gather_copy(ref, send, recv, d, 0, h).start()
            out_copy(ref, out, sem, z, h).start()

    def gather_step(kind, s):
        ref, send, recv, _, _ = kind
        for i in range(2):
            for d in range(2):
                h = d if i == 0 else 1 - d
                if s < steps(d, h):
                    gather_wait(kind, d, s - 1, h)
                    gather_copy(ref, send, recv, d, s, h).start()

    def gather_last(kind):
        for i in range(2):
            for d in range(2):
                h = 1 - d if i == 0 else d
                gather_wait(kind, d, steps(d, h) - 1, h)

    out_i = (ag_item, ai_s, ai_r, item_codes, oi_s)
    out_n = (ag_cache, ac_s, ac_r, cache_codes, oc_s)

    own = ring_last(kind_i)
    gather_first(out_i, unit_back(own, items[pl.ds(pl.multiple_of(z * CH, CH), CH), :].astype(F32)), CH)
    q_copy.wait()

    @pl.loop(0, NC // 2)
    def _(c):
        code, e = encode(q_part[c, core] + q_core[c], 16)
        q_msg[c, 0:CH] = code
        q_msg[c, CH:] = to_i16(e)

    own = ring_last(kind_n)
    gather_first(out_n, unit_back(own, cache[pl.ds(pl.multiple_of(z * CR, CR), CR), :].astype(F32)), CR)

    @pl.loop(1, NC // 2)
    def _(s):
        other = (chip + s) % (NC // 2)
        remote(q_msg.at[other], q_recv.at[chip], qd_s.at[other], qd_r.at[chip], col=other * 2 + core).start()

    q_recv[chip] = q_msg[chip]
    gather_step(out_i, 1)
    gather_step(out_n, 1)
    gather_step(out_i, 2)
    gather_step(out_n, 2)
    gather_step(out_i, 3)
    gather_step(out_n, 3)

    @pl.loop(1, NC // 2)
    def _(s):
        other = (chip + s) % (NC // 2)
        remote(q_msg.at[other], q_recv.at[other], qd_s.at[other], qd_r.at[other], col=other * 2 + core).wait()

    q_grad = unpack(q_recv.at[0], CH)
    for c in range(1, NC // 2):
        q_grad = q_grad + unpack(q_recv.at[c], CH)
    query_out[...] = unit_back(q_grad, queries[pl.ds(pl.multiple_of(me * CH, CH), CH), :].astype(F32))

    gather_last(out_i)
    gather_last(out_n)

    @pl.loop(0, NZ)
    def _(p):
        for h in range(2):
            out_copy(ag_item, item_codes, oi_s, p, h).wait()
            out_copy(ag_cache, cache_codes, oc_s, p, h).wait()


def last(loss, query, item_codes, cache_codes, loss_out, query_out, item_out, cache_out):
    for p in range(PB):
        for h in range(2):
            columns = slice(h * H, (h + 1) * H)
            code = item_codes[p, h, 0:CH]
            item_out[p * CH : (p + 1) * CH, columns] = decode(code, from_i16(item_codes[p, h, CH:]))
            code = cache_codes[p, h, 0:CR]
            cache_out[p * CR : (p + 1) * CR, columns] = decode(code, from_i16(cache_codes[p, h, CR:]))

    @pl.when(pl.program_id(0) == 0)
    def _():
        loss_out[...] = loss[...]
        query_out[...] = query[...]


def body(queries, positive, items, item_counts, cache, neg_owner, neg_row, neg_counts):
    vmem = pl.BlockSpec(memory_space=pltpu.VMEM)
    hbm = pl.BlockSpec(memory_space=pl.ANY)
    dma = pltpu.SemaphoreType.DMA
    codes_i = (NZ, 2, CH + 16, H)
    codes_n = (NZ, 2, CR + 16, H)
    ring_i = (2, 4, 4, CH + 16, W)
    ring_n = (2, 4, 4, CR + 16, W)
    scratch = [
        pltpu.VMEM((NQ, E), BF16),
        pltpu.VMEM((NI, E), BF16),
        pltpu.VMEM((ROWS, E), BF16),
        pltpu.VMEM((NC, 8, 128), F32),
        pltpu.VMEM((NC, 8, 128), F32),
        pltpu.VMEM((ROWS, E), BF16),
        pltpu.VMEM((ROWS, NS), BF16),
        pltpu.VMEM((NQ, E), BF16),
        pltpu.VMEM((NI, E), BF16),
        pltpu.VMEM((NS, E), BF16),
        pltpu.VMEM((NS, 1), F32),
        pltpu.VMEM((NI, NQ), F32),
        pltpu.VMEM((NS, NQ), F32),
        pltpu.VMEM((NC, NB, QB), F32),
        pltpu.VMEM((NC, NB, QB), F32),
        pltpu.VMEM((NB, QB), F32),
        pltpu.VMEM((NB, QB), F32),
        pltpu.VMEM((NI, NQ), BF16),
        pltpu.VMEM((NS, NQ), BF16),
        pltpu.VMEM((4, NZ, CH, W), F32),
        pltpu.VMEM((4, NZ, CR, W), F32),
        pltpu.VMEM((NS, E), BF16),
        pltpu.VMEM((NS, E), BF16),
        pltpu.VMEM(ring_i, I16),
        pltpu.VMEM(ring_i, I16),
        pltpu.VMEM(ring_n, I16),
        pltpu.VMEM(ring_n, I16),
        pltpu.VMEM(codes_i, I16),
        pltpu.VMEM(codes_n, I16),
        pltpu.VMEM((NC // 2, 2, CH, E), F32),
        pltpu.VMEM((NC // 2, CH, E), F32),
        pltpu.VMEM((NC // 2, CH + 16, E), I16),
        pltpu.VMEM((NC // 2, CH + 16, E), I16),
        dma((3,)),
        dma((NC,)), dma((NC,)),
        dma((NC,)), dma((NC,)),
        dma((NC,)), dma((NC,)),
        dma((2, 4, 4)), dma((2, 4, 4)),
        dma((2, 4, 4)), dma((2, 4, 4)),
        dma((2, 4, 2)), dma((2, 4, 2)),
        dma((2, 4, 2)), dma((2, 4, 2)),
        dma((NZ, 2)), dma((NZ, 2)),
        dma, dma,
        dma((NC // 2,)), dma((NC // 2,)),
    ]
    loss, query_grad, item_codes, cache_codes = pl.pallas_call(
        kernel,
        out_shape=(
            jax.ShapeDtypeStruct((NQ // 128, 128), F32),
            jax.ShapeDtypeStruct((CH, E), F32),
            jax.ShapeDtypeStruct(codes_i, I16),
            jax.ShapeDtypeStruct(codes_n, I16),
        ),
        in_specs=[hbm, vmem, hbm, vmem, vmem, vmem, vmem, hbm],
        out_specs=(vmem, vmem, hbm, hbm),
        scratch_shapes=scratch,
        compiler_params=pltpu.CompilerParams(
            collective_id=0, has_side_effects=True, vmem_limit_bytes=62 * 1024 * 1024
        ),
    )(
        queries,
        positive.reshape(1, NQ),
        items,
        item_counts.reshape(1, NI),
        neg_counts.reshape(1, NN),
        neg_owner.reshape(1, NN),
        neg_row.reshape(1, NN),
        cache,
    )

    def whole(*shape):
        return pl.BlockSpec(shape, lambda r: (0,) * len(shape))

    def chunks(shape):
        return pl.BlockSpec((PB,) + shape[1:], lambda r: (r, 0, 0, 0))

    loss, query_grad, item_grad, cache_grad = pl.pallas_call(
        last,
        grid=(NZ // PB,),
        out_shape=(
            jax.ShapeDtypeStruct((NQ // 128, 128), F32),
            jax.ShapeDtypeStruct((CH, E), F32),
            jax.ShapeDtypeStruct((NI, E), F32),
            jax.ShapeDtypeStruct((ROWS, E), F32),
        ),
        in_specs=[whole(NQ // 128, 128), whole(CH, E), chunks(codes_i), chunks(codes_n)],
        out_specs=(
            whole(NQ // 128, 128),
            whole(CH, E),
            pl.BlockSpec((PB * CH, E), lambda r: (r, 0)),
            pl.BlockSpec((PB * CR, E), lambda r: (r, 0)),
        ),
        compiler_params=pltpu.CompilerParams(vmem_limit_bytes=62 * 1024 * 1024),
    )(loss, query_grad, item_codes, cache_codes)
    return loss.reshape(NQ), query_grad, item_grad, cache_grad


def solution(mesh):
    placed = (
        P("pb", None),
        P("pb"),
        P("col", None),
        P("col"),
        P("col", None),
        P("col", None),
        P("col"),
        P("col"),
    )
    return jax.shard_map(
        body,
        mesh=mesh,
        in_specs=placed,
        out_specs=(P("pb"), P(("pb", "col"), None), P("col", None), P("col", None)),
        check_vma=False,
    )
```

```python
import jax
import jax.numpy as jnp
from jax import lax
from jax.experimental import pallas as pl
from jax.experimental.pallas import tpu as pltpu
from jax.sharding import PartitionSpec as P

MESH = pl.DeviceIdType.MESH
F32 = jnp.float32
BF16 = jnp.bfloat16
I32 = jnp.int32
I16 = jnp.int16

E = 512
H = E // 2
NQ = 2048
QB = 256
NB = NQ // QB
NI = 512
NN = 512
NS = 1024
NC = 32
NZ = 8
CAP = 32
ROWS = 1024
CH = 64
INV_T = 20.0
PB = 4
W = E // 4
CR = ROWS // NZ
LN2 = 0.6931471805599453
SCALE2 = INV_T / LN2


def iota(shape, dim):
    return lax.broadcasted_iota(I32, shape, dim)


def onehot(cond):
    return jnp.where(cond, 1.0, 0.0).astype(BF16)


def dot_nn(a, b):
    return lax.dot_general(a, b, (((1,), (0,)), ((), ())), preferred_element_type=F32)


def dot_nt(a, b):
    return lax.dot_general(a, b, (((1,), (1,)), ((), ())), preferred_element_type=F32)


def dot_tn(a, b):
    return lax.dot_general(a, b, (((0,), (0,)), ((), ())), preferred_element_type=F32)


def halves(x):
    hi = x.astype(BF16)
    return hi, (x - hi.astype(F32)).astype(BF16)


def encode(x, group):
    rows, width = x.shape
    cube = x.reshape(rows // group, group, width)
    top = jnp.max(jnp.abs(cube), axis=0)
    expo = jnp.ceil(jnp.log2(jnp.maximum(top, 1e-30)))
    code = jnp.round(cube * jnp.exp2(14.99 - expo)[None])
    return code.reshape(rows, width).astype(I32).astype(I16), expo


def decode(code, expo):
    rows, width = code.shape
    group = expo.shape[0]
    cube = code.astype(I32).astype(F32).reshape(rows // group, group, width)
    return (cube * jnp.exp2(expo - 14.99)[None]).reshape(rows, width)


def to_i16(x):
    return x.astype(I32).astype(I16)


def from_i16(x):
    return x.astype(I32).astype(F32)


def unit(x):
    scale = jnp.sqrt(jnp.sum(x * x, axis=1, keepdims=True) + 1e-06)
    return x * (1.0 / scale), scale


def unit_back(grad, rows):
    direction, scale = unit(rows)
    return (grad - direction * jnp.sum(grad * direction, axis=1, keepdims=True)) / scale


def kernel(
    queries_hbm, positive_hbm, items_hbm, counts_i_hbm, counts_n_hbm, owner_hbm, row_hbm, cache_hbm,
    loss_out, query_out, item_codes, cache_codes,
    queries, positive, items, counts_i_ref, counts_n_ref, owner_ref, row_ref, cache, loss_buf, query_buf, msg, mrecv, cache_unit, scat, q_unit, cand_i, cand_n, shift_n,
    expo_i, expo_n, pos, tot, sums_i, factor_i, factor_n, weight_i, weight_n, part_i, part_n,
    slot_grad, slot_hi, slot_lo,
    send_i, recv_i, send_n, recv_n, ag_item, ag_cache, q_part, q_core, q_msg, q_recv,
    in_s, m_s, m_r, p_s, p_r, t_s, t_r, ri_s, ri_r, rn_s, rn_r, ai_s, ai_r, ac_s, ac_r, oi_s, oc_s,
    qc_s, qc_r, qd_s, qd_r, out_s,
):
    me = lax.axis_index("col")
    z = lax.axis_index("pb")
    core = me % 2
    chip = me // 2
    my_g = me // 4
    up = (z + 1) % NZ
    down = (z + NZ - 1) % NZ
    sibling = chip * 2 + 1 - core

    barrier = pltpu.get_barrier_semaphore()
    loads = [
        pltpu.make_async_copy(src, dst, in_s.at[i])
        for i, (src, dst) in enumerate(
            (
                (owner_hbm, owner_ref),
                (row_hbm, row_ref),
                (counts_n_hbm, counts_n_ref),
                (counts_i_hbm, counts_i_ref),
                (items_hbm, items),
                (positive_hbm, positive),
                (queries_hbm, queries),
                (cache_hbm, cache),
            )
        )
    ]
    for load in loads:
        load.start()

    @pl.loop(1, NC)
    def _(s):
        pl.semaphore_signal(barrier, inc=1, device_id={"col": (me + s) % NC}, device_id_type=MESH)

    for other in (up, down):
        pl.semaphore_signal(barrier, inc=1, device_id={"pb": other}, device_id_type=MESH)

    def remote(src, dst, send, recv, **where):
        return pltpu.make_async_remote_copy(
            src_ref=src, dst_ref=dst, send_sem=send, recv_sem=recv, device_id=where, device_id_type=MESH
        )

    def pair_row(ref, b):
        return jnp.concatenate([ref[pl.ds(2 * b, 1), :], ref[pl.ds(2 * b + 1, 1), :]], axis=1)

    def put_pair(ref, b, value):
        ref[pl.ds(2 * b, 1), :] = value[:, 0:128]
        ref[pl.ds(2 * b + 1, 1), :] = value[:, 128:]

    for load in loads[0:4]:
        load.wait()
    counts_i = counts_i_ref[...].astype(F32)
    counts_n = counts_n_ref[...].astype(F32)
    owner = owner_ref[...]
    row = row_ref[...]
    table = jnp.where(iota((NC, NN), 0) == owner, 1.0, 0.0)
    before = onehot(iota((NN, NN), 0) < iota((NN, NN), 1))
    earlier = dot_nn(table.astype(BF16), before)
    rank = jnp.sum(earlier * table, axis=0, keepdims=True).astype(I32)
    lane = onehot(iota((128, NN), 0) == CAP * (me % 4) + rank)
    named = jnp.concatenate(
        [table * (row >> 5).astype(F32), table * (row & 31).astype(F32), table * counts_n], axis=0
    )
    named = dot_nt(named.astype(BF16), lane)
    named = named[0:NC] * 32.0 + named[NC : 2 * NC] + named[2 * NC :] * ROWS
    total_i = jnp.sum(counts_i, axis=1, keepdims=True).reshape(1, 1, 1)
    total_n = jnp.sum(counts_n, axis=1, keepdims=True).reshape(1, 1, 1)
    line = iota((NC, 8, 128), 1)
    totals = jnp.where(line == (my_g + 1) % 8, total_i, jnp.where(line == (my_g + 2) % 8, total_n, 0.0))
    msg[...] = jnp.where(line == my_g, named.reshape(NC, 1, 128), totals)

    pl.semaphore_wait(barrier, NC + 1)

    def to_all(ref, send, recv, s):
        other = (me + s) % NC
        return remote(ref.at[me], ref.at[me], send.at[other], recv.at[me], col=other)

    def from_all(ref, send, recv, s):
        other = (me + s) % NC
        return remote(ref.at[me], ref.at[other], send.at[other], recv.at[other], col=other)

    @pl.loop(1, NC)
    def _(s):
        other = (me + s) % NC
        remote(msg.at[other], mrecv.at[me], m_s.at[other], m_r.at[me], col=other).start()

    mrecv[me] = msg[me]

    loads[4].wait()
    cand_i[...] = unit(items[...].astype(F32))[0].astype(BF16)
    same = iota((NI, NI), 0) == iota((NI, NI), 1)
    shift_i = jnp.log2(jnp.sum(jnp.where(same, counts_i, 0.0), axis=1, keepdims=True))
    first_item = me * NI
    loads[5].wait()
    loads[6].wait()

    @pl.loop(0, NB)
    def _(b):
        at = pl.ds(pl.multiple_of(b * QB, QB), QB)
        q_rows = unit(queries[at, :].astype(F32))[0].astype(BF16)
        q_unit[at, :] = q_rows
        logits = dot_nt(cand_i[...], q_rows) * SCALE2 - shift_i
        hit = positive[:, at] == first_item + iota((NI, QB), 0)
        expo = jnp.exp2(logits)
        expo_i[:, at] = expo
        put_pair(sums_i, b, jnp.sum(expo, axis=0, keepdims=True))
        put_pair(pos.at[me], b, jnp.sum(jnp.where(hit, logits, 0.0), axis=0, keepdims=True))

    loads[7].wait()

    @pl.loop(0, ROWS // QB)
    def _(b):
        at = pl.ds(pl.multiple_of(b * QB, QB), QB)
        cache_unit[at, :] = unit(cache[at, :].astype(F32))[0].astype(BF16)

    @pl.loop(1, NC)
    def _(s):
        other = (me + s) % NC
        remote(msg.at[other], mrecv.at[other], m_s.at[other], m_r.at[other], col=other).wait()

    line = iota((8, 128), 0)
    asked = jnp.zeros((8, 128), F32)
    sum_i = jnp.zeros((8, 128), F32)
    sum_n = jnp.zeros((8, 128), F32)
    for g in range(8):
        four = (mrecv[4 * g] + mrecv[4 * g + 1]) + (mrecv[4 * g + 2] + mrecv[4 * g + 3])
        asked = jnp.where(line == g, four, asked)
        sum_i = sum_i + jnp.where(line == (g + 1) % 8, four, 0.0)
        sum_n = sum_n + jnp.where(line == (g + 2) % 8, four, 0.0)
    total_i = jnp.sum(sum_i, axis=0, keepdims=True)[:, 0:1]
    total_n = jnp.sum(sum_n, axis=0, keepdims=True)[:, 0:1]

    @pl.loop(1, NC)
    def _(s):
        to_all(pos, p_s, p_r, s).start()

    def parts(value):
        count = jnp.floor(value * (1.0 / ROWS))
        return count, (value - count * ROWS).astype(I32)

    by_slot = jnp.concatenate([asked, jnp.zeros((120, 128), F32)], axis=0).T
    for g in range(8):
        count, wanted = parts(by_slot[:, g : g + 1])
        at = pl.ds(g * 128, 128)
        cand_n[at, :] = dot_nn(onehot(iota((128, ROWS), 1) == wanted), cache_unit[...]).astype(BF16)
        shift_n[at, :] = jnp.where(count > 0.5, jnp.log2(jnp.maximum(count, 1.0)), 1e30)

    def tot_copy(half, s, mine):
        other = (me + s) % NC
        slot = me if mine else other
        return remote(
            tot.at[half, me], tot.at[half, slot], t_s.at[half, other], t_r.at[half, slot], col=other
        )

    def scores_n(half):
        @pl.loop(half * NB // 2, (half + 1) * NB // 2)
        def _(b):
            at = pl.ds(pl.multiple_of(b * QB, QB), QB)
            expo = jnp.exp2(dot_nt(cand_n[...], q_unit[at, :]) * SCALE2 - shift_n[...])
            expo_n[:, at] = expo
            sum_n = total_n * jnp.sum(expo, axis=0, keepdims=True)
            put_pair(tot.at[half, me], b - half * (NB // 2), total_i * pair_row(sums_i, b) + sum_n)

        @pl.loop(1, NC)
        def _(s):
            tot_copy(half, s, True).start()

    scores_n(0)
    scores_n(1)
    slots = parts(asked)[1]
    for g in range(8):
        scat[:, g * 128 : (g + 1) * 128] = onehot(iota((ROWS, 128), 0) == slots[g : g + 1, :])

    def sums_in(half):
        @pl.loop(1, NC)
        def _(s):
            tot_copy(half, s, False).wait()

        total = jnp.sum(tot[half], axis=0)
        factor_i[half * 8 : (half + 1) * 8] = total_i / total
        factor_n[half * 8 : (half + 1) * 8] = total_n / total
        loss_buf[half * 8 : (half + 1) * 8] = jnp.log(total)

    def weights_i(half):
        @pl.loop(half * NB // 2, (half + 1) * NB // 2)
        def _(b):
            at = pl.ds(pl.multiple_of(b * QB, QB), QB)
            hit = positive[:, at] == first_item + iota((NI, QB), 0)
            weight_i[:, at] = (expo_i[:, at] * pair_row(factor_i, b) - jnp.where(hit, 1.0, 0.0)).astype(BF16)

    def weights_n(half):
        @pl.loop(half * NB // 2, (half + 1) * NB // 2)
        def _(b):
            at = pl.ds(pl.multiple_of(b * QB, QB), QB)
            weight_n[:, at] = (expo_n[:, at] * pair_row(factor_n, b)).astype(BF16)

    def grad_i(half):
        at = pl.ds(half * (NQ // 2), NQ // 2)
        grad = dot_nn(weight_i[:, at], q_unit[at, :]) * INV_T
        for k in range(4):
            piece = grad[:, k * W : (k + 1) * W].reshape(NZ, CH, W)
            part_i[k] = piece if half == 0 else part_i[k] + piece

    def grad_n(half):
        at = pl.ds(half * (NQ // 2), NQ // 2)

        @pl.loop(0, NS // 512)
        def _(b):
            rows = pl.ds(pl.multiple_of(b * 512, 512), 512)
            grad = dot_nn(weight_n[rows, at], q_unit[at, :]) * INV_T
            if half == 0:
                slot_grad[rows, :] = grad
            else:
                hi, lo = halves(slot_grad[rows, :] + grad)
                slot_hi[rows, :] = hi
                slot_lo[rows, :] = lo

    def ring_peer(d):
        return up if d == 0 else down

    def ring_chunk(d, t):
        return (z + 4 - t) % NZ if d == 0 else (z + 4 + t) % NZ

    def far(d, k):
        return k // 2 == d

    def pack(ref, chunk, rows):
        code, e = encode(chunk, 16)
        ref[0:rows] = code
        ref[rows:] = to_i16(e)

    def unpack(ref, rows):
        return decode(ref[0:rows], from_i16(ref[rows:]))

    def ring_copy(kind, d, t, k):
        _, send, recv, s, r, _ = kind
        return remote(send.at[d, t, k], recv.at[d, t, k], s.at[d, t, k], r.at[d, t, k], pb=ring_peer(d))

    def ring_first(kind, t):
        part, send, _, _, _, rows = kind
        for k in range(4):
            for d in range(2):
                if far(d, k) == (t == 0):
                    pack(send.at[d, t, k], part[k, ring_chunk(d, t)], rows)
                    ring_copy(kind, d, t, k).start()

    def ring_step(kind, t):
        part, send, recv, _, _, rows = kind
        for k in (0, 2, 1, 3):
            for d in range(2):
                if t > 1 or far(d, k):
                    ring_copy(kind, d, t - 1, k).wait()
                    got = unpack(recv.at[d, t - 1, k], rows)
                    pack(send.at[d, t, k], part[k, ring_chunk(d, t)] + got, rows)
                    ring_copy(kind, d, t, k).start()

    def ring_last(kind):
        part, _, recv, _, _, rows = kind
        columns = []
        for k in range(4):
            own = part[k, z]
            for d in range(2):
                ring_copy(kind, d, 3, k).wait()
                own = own + unpack(recv.at[d, 3, k], rows)
            columns.append(own)
        return jnp.concatenate(columns, axis=1)

    kind_i = (part_i, send_i, recv_i, ri_s, ri_r, CH)
    kind_n = (part_n, send_n, recv_n, rn_s, rn_r, CR)

    sums_in(0)
    weights_i(0)
    grad_i(0)
    weights_n(0)
    grad_n(0)
    sums_in(1)
    weights_i(1)
    grad_i(1)
    ring_first(kind_i, 0)
    ring_first(kind_i, 1)
    weights_n(1)
    grad_n(1)

    def by_row(pair):
        at = pl.ds(pl.multiple_of(pair * 256, 256), 256)
        grad = dot_nn(scat[at, :], slot_hi[...]) + dot_nn(scat[at, :], slot_lo[...])
        for k in range(4):
            part_n[k, pl.ds(pair * 2, 2)] = grad[:, k * W : (k + 1) * W].reshape(2, CR, W)

    pair = ((z + 4) % NZ) // 2
    by_row(pair)
    ring_first(kind_n, 0)
    by_row((pair + 3) % 4)
    by_row((pair + 1) % 4)
    ring_first(kind_n, 1)
    by_row((pair + 2) % 4)

    def q_block(b):
        at = pl.ds(pl.multiple_of(b * QB, QB), QB)
        grad = dot_tn(weight_i[:, at], cand_i[...]) + dot_tn(weight_n[:, at], cand_n[...])
        q_part[pl.ds(b * 2, 2)] = (grad * INV_T).reshape(2, 2, CH, E)

    q_copy = remote(q_part.at[:, 1 - core], q_core, qc_s, qc_r, col=sibling)
    q_block(0)
    q_block(1)
    ring_step(kind_i, 1)
    q_block(2)
    ring_step(kind_n, 1)
    q_block(3)
    q_block(4)
    ring_step(kind_i, 2)
    q_block(5)
    ring_step(kind_n, 2)
    q_block(6)
    q_block(7)
    q_copy.start()
    ring_step(kind_i, 3)

    @pl.loop(1, NC)
    def _(s):
        from_all(pos, p_s, p_r, s).wait()

    loss_buf[...] = loss_buf[...] - (jnp.sum(pos[...], axis=0) * LN2 + jnp.log(total_i))
    loss_copy = pltpu.make_async_copy(loss_buf, loss_out, out_s.at[0])
    loss_copy.start()
    ring_step(kind_n, 3)

    def gather_copy(ref, send, recv, d, s, h):
        source = (z + 2 * NZ - s) % NZ if d == 0 else (z + s) % NZ
        return remote(
            ref.at[source, h], ref.at[source, h], send.at[d, s, h], recv.at[d, s, h], pb=ring_peer(d)
        )

    def steps(d, h):
        return 4 if d == h else 3

    def out_copy(ref, out, sem, p, h):
        return pltpu.make_async_copy(ref.at[p, h], out.at[p, h], sem.at[p, h])

    def gather_wait(kind, d, s, h):
        ref, send, recv, out, sem = kind
        gather_copy(ref, send, recv, d, s, h).wait()
        source = (z + 2 * NZ - s - 1) % NZ if d == 0 else (z + s + 1) % NZ
        out_copy(ref, out, sem, source, h).start()

    def gather_first(kind, h):
        ref, send, recv, out, sem = kind
        for d in (h, 1 - h):
            gather_copy(ref, send, recv, d, 0, h).start()
        out_copy(ref, out, sem, z, h).start()

    def gather_step(kind, s):
        ref, send, recv, _, _ = kind
        for i in range(2):
            for d in range(2):
                h = d if i == 0 else 1 - d
                if s < steps(d, h):
                    gather_wait(kind, d, s - 1, h)
                    gather_copy(ref, send, recv, d, s, h).start()

    def gather_last(kind):
        for i in range(2):
            for d in range(2):
                h = 1 - d if i == 0 else d
                gather_wait(kind, d, steps(d, h) - 1, h)

    out_i = (ag_item, ai_s, ai_r, item_codes, oi_s)
    out_n = (ag_cache, ac_s, ac_r, cache_codes, oc_s)

    grad = unit_back(ring_last(kind_i), items[pl.ds(pl.multiple_of(z * CH, CH), CH), :].astype(F32))
    item_e = []
    for h in range(2):
        code, e = encode(grad[:, h * H : (h + 1) * H], 8)
        ag_item[z, h] = code
        gather_first(out_i, h)
        item_e.append(e)
    q_copy.wait()

    @pl.loop(0, NC // 2)
    def _(c):
        code, e = encode(q_part[c, core] + q_core[c], 16)
        q_msg[c, 0:CH] = code
        q_msg[c, CH:] = to_i16(e)

    grad = unit_back(ring_last(kind_n), cache[pl.ds(pl.multiple_of(z * CR, CR), CR), :].astype(F32))
    for h in range(2):
        code, e = encode(grad[:, h * H : (h + 1) * H], 8)
        ag_cache[z, h, 0:CR] = code
        ag_cache[z, h, CR:] = to_i16(jnp.concatenate([e, item_e[h]], axis=0))
        gather_first(out_n, h)

    @pl.loop(1, NC // 2)
    def _(s):
        other = (chip + s) % (NC // 2)
        remote(q_msg.at[other], q_recv.at[chip], qd_s.at[other], qd_r.at[chip], col=other * 2 + core).start()

    q_recv[chip] = q_msg[chip]
    gather_step(out_i, 1)
    gather_step(out_n, 1)
    gather_step(out_i, 2)
    gather_step(out_n, 2)
    gather_step(out_i, 3)
    gather_step(out_n, 3)

    @pl.loop(1, NC // 2)
    def _(s):
        other = (chip + s) % (NC // 2)
        remote(q_msg.at[other], q_recv.at[other], qd_s.at[other], qd_r.at[other], col=other * 2 + core).wait()

    q_grad = unpack(q_recv.at[0], CH)
    for c in range(1, NC // 2):
        q_grad = q_grad + unpack(q_recv.at[c], CH)
    query_buf[...] = unit_back(q_grad, queries[pl.ds(pl.multiple_of(me * CH, CH), CH), :].astype(F32))
    query_copy = pltpu.make_async_copy(query_buf, query_out, out_s.at[1])
    query_copy.start()

    gather_last(out_i)
    gather_last(out_n)

    @pl.loop(0, NZ)
    def _(p):
        for h in range(2):
            out_copy(ag_item, item_codes, oi_s, p, h).wait()
            out_copy(ag_cache, cache_codes, oc_s, p, h).wait()

    loss_copy.wait()
    query_copy.wait()


def last(loss, query, item_codes, cache_codes, loss_out, query_out, item_out, cache_out):
    for p in range(PB):
        for h in range(2):
            columns = slice(h * H, (h + 1) * H)
            e = from_i16(cache_codes[p, h, CR:])
            item_out[p * CH : (p + 1) * CH, columns] = decode(item_codes[p, h], e[8:16])
            cache_out[p * CR : (p + 1) * CR, columns] = decode(cache_codes[p, h, 0:CR], e[0:8])

    @pl.when(pl.program_id(0) == 0)
    def _():
        loss_out[...] = loss[...]
        query_out[...] = query[...]


def body(queries, positive, items, item_counts, cache, neg_owner, neg_row, neg_counts):
    hbm = pl.BlockSpec(memory_space=pl.ANY)
    dma = pltpu.SemaphoreType.DMA
    codes_i = (NZ, 2, CH, H)
    codes_n = (NZ, 2, CR + 16, H)
    ring_i = (2, 4, 4, CH + 16, W)
    ring_n = (2, 4, 4, CR + 16, W)
    scratch = [
        pltpu.VMEM((NQ, E), BF16),
        pltpu.VMEM((1, NQ), I32),
        pltpu.VMEM((NI, E), BF16),
        pltpu.VMEM((1, NI), I32),
        pltpu.VMEM((1, NN), I32),
        pltpu.VMEM((1, NN), I32),
        pltpu.VMEM((1, NN), I32),
        pltpu.VMEM((ROWS, E), BF16),
        pltpu.VMEM((NQ // 128, 128), F32),
        pltpu.VMEM((CH, E), F32),
        pltpu.VMEM((NC, 8, 128), F32),
        pltpu.VMEM((NC, 8, 128), F32),
        pltpu.VMEM((ROWS, E), BF16),
        pltpu.VMEM((ROWS, NS), BF16),
        pltpu.VMEM((NQ, E), BF16),
        pltpu.VMEM((NI, E), BF16),
        pltpu.VMEM((NS, E), BF16),
        pltpu.VMEM((NS, 1), F32),
        pltpu.VMEM((NI, NQ), F32),
        pltpu.VMEM((NS, NQ), F32),
        pltpu.VMEM((NC, NQ // 128, 128), F32),
        pltpu.VMEM((2, NC, NQ // 256, 128), F32),
        pltpu.VMEM((NQ // 128, 128), F32),
        pltpu.VMEM((NQ // 128, 128), F32),
        pltpu.VMEM((NQ // 128, 128), F32),
        pltpu.VMEM((NI, NQ), BF16),
        pltpu.VMEM((NS, NQ), BF16),
        pltpu.VMEM((4, NZ, CH, W), F32),
        pltpu.VMEM((4, NZ, CR, W), F32),
        pltpu.VMEM((NS, E), F32),
        pltpu.VMEM((NS, E), BF16),
        pltpu.VMEM((NS, E), BF16),
        pltpu.VMEM(ring_i, I16),
        pltpu.VMEM(ring_i, I16),
        pltpu.VMEM(ring_n, I16),
        pltpu.VMEM(ring_n, I16),
        pltpu.VMEM(codes_i, I16),
        pltpu.VMEM(codes_n, I16),
        pltpu.VMEM((NC // 2, 2, CH, E), F32),
        pltpu.VMEM((NC // 2, CH, E), F32),
        pltpu.VMEM((NC // 2, CH + 16, E), I16),
        pltpu.VMEM((NC // 2, CH + 16, E), I16),
        dma((8,)),
        dma((NC,)), dma((NC,)),
        dma((NC,)), dma((NC,)),
        dma((2, NC)), dma((2, NC)),
        dma((2, 4, 4)), dma((2, 4, 4)),
        dma((2, 4, 4)), dma((2, 4, 4)),
        dma((2, 4, 2)), dma((2, 4, 2)),
        dma((2, 4, 2)), dma((2, 4, 2)),
        dma((NZ, 2)), dma((NZ, 2)),
        dma, dma,
        dma((NC // 2,)), dma((NC // 2,)),
        dma((2,)),
    ]
    loss, query_grad, item_codes, cache_codes = pl.pallas_call(
        kernel,
        out_shape=(
            jax.ShapeDtypeStruct((NQ // 128, 128), F32),
            jax.ShapeDtypeStruct((CH, E), F32),
            jax.ShapeDtypeStruct(codes_i, I16),
            jax.ShapeDtypeStruct(codes_n, I16),
        ),
        in_specs=[hbm] * 8,
        out_specs=(hbm,) * 4,
        scratch_shapes=scratch,
        compiler_params=pltpu.CompilerParams(
            collective_id=0, has_side_effects=True, vmem_limit_bytes=62 * 1024 * 1024
        ),
    )(
        queries,
        positive.reshape(1, NQ),
        items,
        item_counts.reshape(1, NI),
        neg_counts.reshape(1, NN),
        neg_owner.reshape(1, NN),
        neg_row.reshape(1, NN),
        cache,
    )

    def whole(*shape):
        return pl.BlockSpec(shape, lambda r: (0,) * len(shape))

    def chunks(shape):
        return pl.BlockSpec((PB,) + shape[1:], lambda r: (r, 0, 0, 0))

    loss, query_grad, item_grad, cache_grad = pl.pallas_call(
        last,
        grid=(NZ // PB,),
        out_shape=(
            jax.ShapeDtypeStruct((NQ // 128, 128), F32),
            jax.ShapeDtypeStruct((CH, E), F32),
            jax.ShapeDtypeStruct((NI, E), F32),
            jax.ShapeDtypeStruct((ROWS, E), F32),
        ),
        in_specs=[whole(NQ // 128, 128), whole(CH, E), chunks(codes_i), chunks(codes_n)],
        out_specs=(
            whole(NQ // 128, 128),
            whole(CH, E),
            pl.BlockSpec((PB * CH, E), lambda r: (r, 0)),
            pl.BlockSpec((PB * CR, E), lambda r: (r, 0)),
        ),
        compiler_params=pltpu.CompilerParams(vmem_limit_bytes=62 * 1024 * 1024),
    )(loss, query_grad, item_codes, cache_codes)
    return loss.reshape(NQ), query_grad, item_grad, cache_grad


def solution(mesh):
    placed = (
        P("pb", None),
        P("pb"),
        P("col", None),
        P("col"),
        P("col", None),
        P("col", None),
        P("col"),
        P("col"),
    )
    return jax.shard_map(
        body,
        mesh=mesh,
        in_specs=placed,
        out_specs=(P("pb"), P(("pb", "col"), None), P("col", None), P("col", None)),
        check_vma=False,
    )
```

```python
import jax
import jax.numpy as jnp
from jax import lax
from jax.experimental import pallas as pl
from jax.experimental.pallas import tpu as pltpu
from jax.sharding import PartitionSpec as P

MESH = pl.DeviceIdType.MESH
F32 = jnp.float32
BF16 = jnp.bfloat16
I32 = jnp.int32
I16 = jnp.int16

E = 512
H = E // 2
NQ = 2048
QB = 256
NB = NQ // QB
NI = 512
NN = 512
NS = 1024
NC = 32
NZ = 8
CAP = 32
ROWS = 1024
CH = 64
INV_T = 20.0
PB = 4
W = E // 4
CR = ROWS // NZ
LN2 = 0.6931471805599453
SCALE2 = INV_T / LN2


def iota(shape, dim):
    return lax.broadcasted_iota(I32, shape, dim)


def onehot(cond):
    return jnp.where(cond, 1.0, 0.0).astype(BF16)


def dot_nn(a, b):
    return lax.dot_general(a, b, (((1,), (0,)), ((), ())), preferred_element_type=F32)


def dot_nt(a, b):
    return lax.dot_general(a, b, (((1,), (1,)), ((), ())), preferred_element_type=F32)


def dot_tn(a, b):
    return lax.dot_general(a, b, (((0,), (0,)), ((), ())), preferred_element_type=F32)


def halves(x):
    hi = x.astype(BF16)
    return hi, (x - hi.astype(F32)).astype(BF16)


def encode(x, group):
    rows, width = x.shape
    cube = x.reshape(rows // group, group, width)
    top = jnp.max(jnp.abs(cube), axis=0)
    expo = jnp.ceil(jnp.log2(jnp.maximum(top, 1e-30)))
    code = jnp.round(cube * jnp.exp2(14.99 - expo)[None])
    return code.reshape(rows, width).astype(I32).astype(I16), expo


def decode(code, expo):
    rows, width = code.shape
    group = expo.shape[0]
    cube = code.astype(I32).astype(F32).reshape(rows // group, group, width)
    return (cube * jnp.exp2(expo - 14.99)[None]).reshape(rows, width)


def to_i16(x):
    return x.astype(I32).astype(I16)


def from_i16(x):
    return x.astype(I32).astype(F32)


def unit(x):
    scale = jnp.sqrt(jnp.sum(x * x, axis=1, keepdims=True) + 1e-06)
    return x * (1.0 / scale), scale


def unit_back(grad, rows):
    direction, scale = unit(rows)
    return (grad - direction * jnp.sum(grad * direction, axis=1, keepdims=True)) / scale


def kernel(
    queries_hbm, positive_hbm, items_hbm, counts_i_hbm, counts_n_hbm, owner_hbm, row_hbm, cache_hbm,
    loss_out, query_out, item_codes, cache_codes,
    queries, positive, items, counts_i_ref, counts_n_ref, owner_ref, row_ref, cache, loss_buf, query_buf, msg, mrecv, cache_unit, scat, q_unit, cand_i, cand_n, shift_n,
    expo_i, expo_n, pos, tot, sums_i, factor_i, factor_n, weight_i, weight_n, part_i, part_n,
    slot_grad, slot_hi, slot_lo,
    send_i, recv_i, send_n, recv_n, ag_item, ag_cache, q_part, q_core, q_msg, q_recv,
    in_s, m_s, m_r, p_s, p_r, t_s, t_r, ri_s, ri_r, rn_s, rn_r, ai_s, ai_r, ac_s, ac_r, oi_s, oc_s,
    qc_s, qc_r, qd_s, qd_r, out_s,
):
    me = lax.axis_index("col")
    z = lax.axis_index("pb")
    core = me % 2
    chip = me // 2
    my_g = me // 4
    up = (z + 1) % NZ
    down = (z + NZ - 1) % NZ
    sibling = chip * 2 + 1 - core

    barrier = pltpu.get_barrier_semaphore()
    loads = [
        pltpu.make_async_copy(src, dst, in_s.at[i])
        for i, (src, dst) in enumerate(
            (
                (owner_hbm, owner_ref),
                (row_hbm, row_ref),
                (counts_n_hbm, counts_n_ref),
                (counts_i_hbm, counts_i_ref),
                (items_hbm, items),
                (positive_hbm, positive),
                (queries_hbm, queries),
                (cache_hbm, cache),
            )
        )
    ]
    for load in loads:
        load.start()

    @pl.loop(1, NC)
    def _(s):
        pl.semaphore_signal(barrier, inc=1, device_id={"col": (me + s) % NC}, device_id_type=MESH)

    for other in (up, down):
        pl.semaphore_signal(barrier, inc=1, device_id={"pb": other}, device_id_type=MESH)

    def remote(src, dst, send, recv, **where):
        return pltpu.make_async_remote_copy(
            src_ref=src, dst_ref=dst, send_sem=send, recv_sem=recv, device_id=where, device_id_type=MESH
        )

    def pair_row(ref, b):
        return jnp.concatenate([ref[pl.ds(2 * b, 1), :], ref[pl.ds(2 * b + 1, 1), :]], axis=1)

    def put_pair(ref, b, value):
        ref[pl.ds(2 * b, 1), :] = value[:, 0:128]
        ref[pl.ds(2 * b + 1, 1), :] = value[:, 128:]

    for load in loads[0:4]:
        load.wait()
    counts_i = counts_i_ref[...].astype(F32)
    counts_n = counts_n_ref[...].astype(F32)
    owner = owner_ref[...]
    row = row_ref[...]
    table = jnp.where(iota((NC, NN), 0) == owner, 1.0, 0.0)
    before = onehot(iota((NN, NN), 0) < iota((NN, NN), 1))
    earlier = dot_nn(table.astype(BF16), before)
    rank = jnp.sum(earlier * table, axis=0, keepdims=True).astype(I32)
    lane = onehot(iota((128, NN), 0) == CAP * (me % 4) + rank)
    named = jnp.concatenate(
        [table * (row >> 5).astype(F32), table * (row & 31).astype(F32), table * counts_n], axis=0
    )
    named = dot_nt(named.astype(BF16), lane)
    named = named[0:NC] * 32.0 + named[NC : 2 * NC] + named[2 * NC :] * ROWS
    total_i = jnp.sum(counts_i, axis=1, keepdims=True).reshape(1, 1, 1)
    total_n = jnp.sum(counts_n, axis=1, keepdims=True).reshape(1, 1, 1)
    line = iota((NC, 8, 128), 1)
    totals = jnp.where(line == (my_g + 1) % 8, total_i, jnp.where(line == (my_g + 2) % 8, total_n, 0.0))
    msg[...] = jnp.where(line == my_g, named.reshape(NC, 1, 128), totals)

    pl.semaphore_wait(barrier, NC + 1)

    def to_all(ref, send, recv, s):
        other = (me + s) % NC
        return remote(ref.at[me], ref.at[me], send.at[other], recv.at[me], col=other)

    def from_all(ref, send, recv, s):
        other = (me + s) % NC
        return remote(ref.at[me], ref.at[other], send.at[other], recv.at[other], col=other)

    @pl.loop(1, NC)
    def _(s):
        other = (me + s) % NC
        remote(msg.at[other], mrecv.at[me], m_s.at[other], m_r.at[me], col=other).start()

    mrecv[me] = msg[me]

    loads[4].wait()
    cand_i[...] = unit(items[...].astype(F32))[0].astype(BF16)
    same = iota((NI, NI), 0) == iota((NI, NI), 1)
    shift_i = jnp.log2(jnp.sum(jnp.where(same, counts_i, 0.0), axis=1, keepdims=True))
    first_item = me * NI
    loads[5].wait()
    loads[6].wait()

    @pl.loop(0, NB)
    def _(b):
        at = pl.ds(pl.multiple_of(b * QB, QB), QB)
        q_rows = unit(queries[at, :].astype(F32))[0].astype(BF16)
        q_unit[at, :] = q_rows
        logits = dot_nt(cand_i[...], q_rows) * SCALE2 - shift_i
        hit = positive[:, at] == first_item + iota((NI, QB), 0)
        expo = jnp.exp2(logits)
        expo_i[:, at] = expo
        put_pair(sums_i, b, jnp.sum(expo, axis=0, keepdims=True))
        put_pair(pos.at[me], b, jnp.sum(jnp.where(hit, logits, 0.0), axis=0, keepdims=True))

    loads[7].wait()

    @pl.loop(0, ROWS // QB)
    def _(b):
        at = pl.ds(pl.multiple_of(b * QB, QB), QB)
        cache_unit[at, :] = unit(cache[at, :].astype(F32))[0].astype(BF16)

    @pl.loop(1, NC)
    def _(s):
        other = (me + s) % NC
        remote(msg.at[other], mrecv.at[other], m_s.at[other], m_r.at[other], col=other).wait()

    line = iota((8, 128), 0)
    asked = jnp.zeros((8, 128), F32)
    sum_i = jnp.zeros((8, 128), F32)
    sum_n = jnp.zeros((8, 128), F32)
    for g in range(8):
        four = (mrecv[4 * g] + mrecv[4 * g + 1]) + (mrecv[4 * g + 2] + mrecv[4 * g + 3])
        asked = jnp.where(line == g, four, asked)
        sum_i = sum_i + jnp.where(line == (g + 1) % 8, four, 0.0)
        sum_n = sum_n + jnp.where(line == (g + 2) % 8, four, 0.0)
    total_i = jnp.sum(sum_i, axis=0, keepdims=True)[:, 0:1]
    total_n = jnp.sum(sum_n, axis=0, keepdims=True)[:, 0:1]

    @pl.loop(1, NC)
    def _(s):
        to_all(pos, p_s, p_r, s).start()

    def parts(value):
        count = jnp.floor(value * (1.0 / ROWS))
        return count, (value - count * ROWS).astype(I32)

    by_slot = jnp.concatenate([asked, jnp.zeros((120, 128), F32)], axis=0).T
    for half in range(2):
        picks = []
        for g in range(4 * half, 4 * half + 4):
            count, wanted = parts(by_slot[:, g : g + 1])
            shift_n[g * 128 : (g + 1) * 128, :] = jnp.where(
                count > 0.5, jnp.log2(jnp.maximum(count, 1.0)), 1e30
            )
            picks.append(onehot(iota((128, ROWS), 1) == wanted))
        picked = dot_nn(jnp.concatenate(picks, axis=0), cache_unit[...])
        cand_n[half * 512 : (half + 1) * 512, :] = picked.astype(BF16)

    def tot_copy(half, s, mine):
        other = (me + s) % NC
        slot = me if mine else other
        return remote(
            tot.at[half, me], tot.at[half, slot], t_s.at[half, other], t_r.at[half, slot], col=other
        )

    def scores_n(half):
        @pl.loop(half * NB // 2, (half + 1) * NB // 2)
        def _(b):
            at = pl.ds(pl.multiple_of(b * QB, QB), QB)
            expo = jnp.exp2(dot_nt(cand_n[...], q_unit[at, :]) * SCALE2 - shift_n[...])
            expo_n[:, at] = expo
            sum_n = total_n * jnp.sum(expo, axis=0, keepdims=True)
            put_pair(tot.at[half, me], b - half * (NB // 2), total_i * pair_row(sums_i, b) + sum_n)

        @pl.loop(1, NC)
        def _(s):
            tot_copy(half, s, True).start()

    scores_n(0)
    scores_n(1)
    slots = parts(asked)[1]
    for g in range(8):
        scat[:, g * 128 : (g + 1) * 128] = onehot(iota((ROWS, 128), 0) == slots[g : g + 1, :])

    def sums_in(half):
        @pl.loop(1, NC)
        def _(s):
            tot_copy(half, s, False).wait()

        total = jnp.sum(tot[half], axis=0)
        factor_i[half * 8 : (half + 1) * 8] = total_i / total
        factor_n[half * 8 : (half + 1) * 8] = total_n / total
        loss_buf[half * 8 : (half + 1) * 8] = jnp.log(total)

    def weights_i(half):
        @pl.loop(half * NB // 2, (half + 1) * NB // 2)
        def _(b):
            at = pl.ds(pl.multiple_of(b * QB, QB), QB)
            hit = positive[:, at] == first_item + iota((NI, QB), 0)
            weight_i[:, at] = (expo_i[:, at] * pair_row(factor_i, b) - jnp.where(hit, 1.0, 0.0)).astype(BF16)

    def weights_n(half):
        @pl.loop(half * NB // 2, (half + 1) * NB // 2)
        def _(b):
            at = pl.ds(pl.multiple_of(b * QB, QB), QB)
            weight_n[:, at] = (expo_n[:, at] * pair_row(factor_n, b)).astype(BF16)

    def grad_i(half):
        at = pl.ds(half * (NQ // 2), NQ // 2)
        grad = dot_nn(weight_i[:, at], q_unit[at, :]) * INV_T
        for k in range(4):
            piece = grad[:, k * W : (k + 1) * W].reshape(NZ, CH, W)
            part_i[k] = piece if half == 0 else part_i[k] + piece

    def grad_n(half):
        at = pl.ds(half * (NQ // 2), NQ // 2)

        @pl.loop(0, NS // 512)
        def _(b):
            rows = pl.ds(pl.multiple_of(b * 512, 512), 512)
            grad = dot_nn(weight_n[rows, at], q_unit[at, :]) * INV_T
            if half == 0:
                slot_grad[rows, :] = grad
            else:
                hi, lo = halves(slot_grad[rows, :] + grad)
                slot_hi[rows, :] = hi
                slot_lo[rows, :] = lo

    def ring_peer(d):
        return up if d == 0 else down

    def ring_chunk(d, t):
        return (z + 4 - t) % NZ if d == 0 else (z + 4 + t) % NZ

    def far(d, k):
        return k // 2 == d

    def pack(ref, chunk, rows):
        code, e = encode(chunk, 16)
        ref[0:rows] = code
        ref[rows:] = to_i16(e)

    def unpack(ref, rows):
        return decode(ref[0:rows], from_i16(ref[rows:]))

    def pack_two(ref, chunk):
        code, e = encode(chunk[0:CH], 8)
        code2, e2 = encode(chunk[CH:], 8)
        ref[0:CH] = code
        ref[CH : 2 * CH] = code2
        ref[2 * CH :] = to_i16(jnp.concatenate([e, e2], axis=0))

    def unpack_two(ref):
        e = from_i16(ref[2 * CH :])
        return jnp.concatenate([decode(ref[0:CH], e[0:8]), decode(ref[CH : 2 * CH], e[8:])], axis=0)

    def ring_copy(kind, d, t, k):
        _, send, recv, s, r, _ = kind
        return remote(send.at[d, t, k], recv.at[d, t, k], s.at[d, t, k], r.at[d, t, k], pb=ring_peer(d))

    def ring_first(kind, t):
        part, send, _, _, _, rows = kind
        for k in range(4):
            for d in range(2):
                if far(d, k) == (t == 0):
                    pack(send.at[d, t, k], part[k, ring_chunk(d, t)], rows)
                    ring_copy(kind, d, t, k).start()

    def ring_step(kind, t):
        part, send, recv, _, _, rows = kind
        for k in (0, 2, 1, 3):
            for d in range(2):
                if t > 1 or far(d, k):
                    ring_copy(kind, d, t - 1, k).wait()
                    got = unpack(recv.at[d, t - 1, k], rows)
                    pack(send.at[d, t, k], part[k, ring_chunk(d, t)] + got, rows)
                    ring_copy(kind, d, t, k).start()

    def ring_last(kind):
        part, _, recv, _, _, rows = kind
        columns = []
        for k in range(4):
            own = part[k, z]
            for d in range(2):
                ring_copy(kind, d, 3, k).wait()
                own = own + unpack(recv.at[d, 3, k], rows)
            columns.append(own)
        return jnp.concatenate(columns, axis=1)

    kind_i = (part_i, send_i, recv_i, ri_s, ri_r, CH)
    kind_n = (part_n, send_n, recv_n, rn_s, rn_r, CR)

    def by_row(pair):
        at = pl.ds(pl.multiple_of(pair * 256, 256), 256)
        grad = dot_nn(scat[at, :], slot_hi[...]) + dot_nn(scat[at, :], slot_lo[...])
        for k in range(4):
            part_n[k, pl.ds(pair * 2, 2)] = grad[:, k * W : (k + 1) * W].reshape(2, CR, W)

    def q_which(i):
        return (chip // 2 + i) % NB

    def q_copy(i):
        two = pl.ds(q_which(i) * 2, 2)
        return remote(q_part.at[two, 1 - core], q_core.at[two], qc_s.at[i], qc_r.at[i], col=sibling)

    def q_block(i):
        b = q_which(i)
        at = pl.ds(pl.multiple_of(b * QB, QB), QB)
        grad = dot_tn(weight_i[:, at], cand_i[...]) + dot_tn(weight_n[:, at], cand_n[...])
        q_part[pl.ds(b * 2, 2)] = (grad * INV_T).reshape(2, 2, CH, E)
        q_copy(i).start()

    def q_send(i):
        q_copy(i).wait()
        for j in range(2):
            c = q_which(i) * 2 + j
            grad = q_part[c, core] + q_core[c]
            pack_two(q_msg.at[c], jnp.concatenate([grad[:, :H], grad[:, H:]], axis=0))

            @pl.when(c != chip)
            def _():
                remote(q_msg.at[c], q_recv.at[chip], qd_s.at[c], qd_r.at[chip], col=c * 2 + core).start()

            @pl.when(c == chip)
            def _():
                q_recv[chip] = q_msg[c]

    def gather_copy(kind, d, s, k):
        ref, send, recv, _, _, _ = kind
        source = (z + 2 * NZ - s) % NZ if d == 0 else (z + s) % NZ
        return remote(
            ref.at[source, k], ref.at[source, k], send.at[d, s, k], recv.at[d, s, k], pb=ring_peer(d)
        )

    def streams(kind, d):
        n = kind[5]
        mine = [(k, 4) for k in range(n) if 2 * k // n == d]
        return mine + [(k, 3) for k in range(n) if 2 * k // n != d]

    def out_copy(kind, p, k):
        ref, _, _, out, sem, _ = kind
        return pltpu.make_async_copy(ref.at[p, k], out.at[p, k], sem.at[p, k])

    def gather_wait(kind, d, s, k):
        gather_copy(kind, d, s, k).wait()
        out_copy(kind, (z + 2 * NZ - s - 1) % NZ if d == 0 else (z + s + 1) % NZ, k).start()

    def gather_first(kind, k):
        for d in range(2):
            gather_copy(kind, d, 0, k).start()
        out_copy(kind, z, k).start()

    def gather_step(kind, s):
        for (k, n), (k2, n2) in zip(streams(kind, 0), streams(kind, 1)):
            for d, stream, steps in ((0, k, n), (1, k2, n2)):
                if s < steps:
                    gather_wait(kind, d, s - 1, stream)
                    gather_copy(kind, d, s, stream).start()

    def gather_last(kind):
        for three in (True, False):
            for d in range(2):
                for k, n in streams(kind, d):
                    if (n == 3) == three:
                        gather_wait(kind, d, n - 1, k)

    out_i = (ag_item, ai_s, ai_r, item_codes, oi_s, 2)
    out_n = (ag_cache, ac_s, ac_r, cache_codes, oc_s, 4)

    sums_in(0)
    weights_i(0)
    grad_i(0)
    weights_n(0)
    sums_in(1)
    weights_i(1)
    grad_i(1)
    ring_first(kind_i, 0)
    ring_first(kind_i, 1)
    grad_n(0)
    weights_n(1)
    grad_n(1)
    ring_step(kind_i, 1)
    pair = ((z + 4) % NZ) // 2
    by_row(pair)
    ring_first(kind_n, 0)
    by_row((pair + 3) % 4)
    by_row((pair + 1) % 4)
    ring_first(kind_n, 1)
    ring_step(kind_i, 2)
    by_row((pair + 2) % 4)
    q_block(0)
    q_block(1)
    ring_step(kind_n, 1)
    ring_step(kind_i, 3)
    q_block(2)
    q_block(3)
    q_block(4)
    ring_step(kind_n, 2)

    grad = unit_back(ring_last(kind_i), items[pl.ds(pl.multiple_of(z * CH, CH), CH), :].astype(F32))
    item_e = []
    for h in range(2):
        code, e = encode(grad[:, h * H : (h + 1) * H], 8)
        ag_item[z, h] = code
        gather_first(out_i, h)
        item_e.extend([e[:, 0:W], e[:, W:]])

    q_block(5)
    q_block(6)
    q_block(7)
    ring_step(kind_n, 3)
    gather_step(out_i, 1)
    q_send(0)
    q_send(1)
    q_send(2)

    grad = unit_back(ring_last(kind_n), cache[pl.ds(pl.multiple_of(z * CR, CR), CR), :].astype(F32))
    for k in range(4):
        code, e = encode(grad[:, k * W : (k + 1) * W], 8)
        ag_cache[z, k, 0:CR] = code
        ag_cache[z, k, CR:] = to_i16(jnp.concatenate([e, item_e[k]], axis=0))
        gather_first(out_n, k)

    gather_step(out_i, 2)
    q_send(3)
    q_send(4)
    q_send(5)
    gather_step(out_n, 1)
    gather_step(out_i, 3)
    q_send(6)
    q_send(7)
    gather_step(out_n, 2)
    gather_last(out_i)

    @pl.loop(1, NC)
    def _(s):
        from_all(pos, p_s, p_r, s).wait()

    loss_buf[...] = loss_buf[...] - (jnp.sum(pos[...], axis=0) * LN2 + jnp.log(total_i))
    loss_copy = pltpu.make_async_copy(loss_buf, loss_out, out_s.at[0])
    loss_copy.start()
    gather_step(out_n, 3)

    @pl.loop(1, NC // 2)
    def _(s):
        other = (chip + s) % (NC // 2)
        remote(q_msg.at[other], q_recv.at[other], qd_s.at[other], qd_r.at[other], col=other * 2 + core).wait()

    q_grad = unpack_two(q_recv.at[0])
    for c in range(1, NC // 2):
        q_grad = q_grad + unpack_two(q_recv.at[c])
    q_grad = jnp.concatenate([q_grad[0:CH], q_grad[CH:]], axis=1)
    query_buf[...] = unit_back(q_grad, queries[pl.ds(pl.multiple_of(me * CH, CH), CH), :].astype(F32))
    query_copy = pltpu.make_async_copy(query_buf, query_out, out_s.at[1])
    query_copy.start()

    gather_last(out_n)

    @pl.loop(0, NZ)
    def _(p):
        for kind in (out_i, out_n):
            for k in range(kind[5]):
                out_copy(kind, p, k).wait()

    loss_copy.wait()
    query_copy.wait()


def last(loss, query, item_codes, cache_codes, loss_out, query_out, item_out, cache_out):
    for p in range(PB):
        for k in range(4):
            columns = slice(k * W, (k + 1) * W)
            part = slice((k % 2) * W, (k % 2 + 1) * W)
            e = from_i16(cache_codes[p, k, CR:])
            item_out[p * CH : (p + 1) * CH, columns] = decode(item_codes[p, k // 2, :, part], e[8:16])
            cache_out[p * CR : (p + 1) * CR, columns] = decode(cache_codes[p, k, 0:CR], e[0:8])

    @pl.when(pl.program_id(0) == 0)
    def _():
        loss_out[...] = loss[...]
        query_out[...] = query[...]


def body(queries, positive, items, item_counts, cache, neg_owner, neg_row, neg_counts):
    hbm = pl.BlockSpec(memory_space=pl.ANY)
    dma = pltpu.SemaphoreType.DMA
    codes_i = (NZ, 2, CH, H)
    codes_n = (NZ, 4, CR + 16, W)
    ring_i = (2, 4, 4, CH + 16, W)
    ring_n = (2, 4, 4, CR + 16, W)
    scratch = [
        pltpu.VMEM((NQ, E), BF16),
        pltpu.VMEM((1, NQ), I32),
        pltpu.VMEM((NI, E), BF16),
        pltpu.VMEM((1, NI), I32),
        pltpu.VMEM((1, NN), I32),
        pltpu.VMEM((1, NN), I32),
        pltpu.VMEM((1, NN), I32),
        pltpu.VMEM((ROWS, E), BF16),
        pltpu.VMEM((NQ // 128, 128), F32),
        pltpu.VMEM((CH, E), F32),
        pltpu.VMEM((NC, 8, 128), F32),
        pltpu.VMEM((NC, 8, 128), F32),
        pltpu.VMEM((ROWS, E), BF16),
        pltpu.VMEM((ROWS, NS), BF16),
        pltpu.VMEM((NQ, E), BF16),
        pltpu.VMEM((NI, E), BF16),
        pltpu.VMEM((NS, E), BF16),
        pltpu.VMEM((NS, 1), F32),
        pltpu.VMEM((NI, NQ), F32),
        pltpu.VMEM((NS, NQ), F32),
        pltpu.VMEM((NC, NQ // 128, 128), F32),
        pltpu.VMEM((2, NC, NQ // 256, 128), F32),
        pltpu.VMEM((NQ // 128, 128), F32),
        pltpu.VMEM((NQ // 128, 128), F32),
        pltpu.VMEM((NQ // 128, 128), F32),
        pltpu.VMEM((NI, NQ), BF16),
        pltpu.VMEM((NS, NQ), BF16),
        pltpu.VMEM((4, NZ, CH, W), F32),
        pltpu.VMEM((4, NZ, CR, W), F32),
        pltpu.VMEM((NS, E), F32),
        pltpu.VMEM((NS, E), BF16),
        pltpu.VMEM((NS, E), BF16),
        pltpu.VMEM(ring_i, I16),
        pltpu.VMEM(ring_i, I16),
        pltpu.VMEM(ring_n, I16),
        pltpu.VMEM(ring_n, I16),
        pltpu.VMEM(codes_i, I16),
        pltpu.VMEM(codes_n, I16),
        pltpu.VMEM((NC // 2, 2, CH, E), F32),
        pltpu.VMEM((NC // 2, CH, E), F32),
        pltpu.VMEM((NC // 2, 2 * CH + 16, H), I16),
        pltpu.VMEM((NC // 2, 2 * CH + 16, H), I16),
        dma((8,)),
        dma((NC,)), dma((NC,)),
        dma((NC,)), dma((NC,)),
        dma((2, NC)), dma((2, NC)),
        dma((2, 4, 4)), dma((2, 4, 4)),
        dma((2, 4, 4)), dma((2, 4, 4)),
        dma((2, 4, 2)), dma((2, 4, 2)),
        dma((2, 4, 4)), dma((2, 4, 4)),
        dma((NZ, 2)), dma((NZ, 4)),
        dma((NB,)), dma((NB,)),
        dma((NC // 2,)), dma((NC // 2,)),
        dma((2,)),
    ]
    loss, query_grad, item_codes, cache_codes = pl.pallas_call(
        kernel,
        out_shape=(
            jax.ShapeDtypeStruct((NQ // 128, 128), F32),
            jax.ShapeDtypeStruct((CH, E), F32),
            jax.ShapeDtypeStruct(codes_i, I16),
            jax.ShapeDtypeStruct(codes_n, I16),
        ),
        in_specs=[hbm] * 8,
        out_specs=(hbm,) * 4,
        scratch_shapes=scratch,
        compiler_params=pltpu.CompilerParams(
            collective_id=0, has_side_effects=True, vmem_limit_bytes=62 * 1024 * 1024
        ),
    )(
        queries,
        positive.reshape(1, NQ),
        items,
        item_counts.reshape(1, NI),
        neg_counts.reshape(1, NN),
        neg_owner.reshape(1, NN),
        neg_row.reshape(1, NN),
        cache,
    )

    def whole(*shape):
        return pl.BlockSpec(shape, lambda r: (0,) * len(shape))

    def chunks(shape):
        return pl.BlockSpec((PB,) + shape[1:], lambda r: (r, 0, 0, 0))

    loss, query_grad, item_grad, cache_grad = pl.pallas_call(
        last,
        grid=(NZ // PB,),
        out_shape=(
            jax.ShapeDtypeStruct((NQ // 128, 128), F32),
            jax.ShapeDtypeStruct((CH, E), F32),
            jax.ShapeDtypeStruct((NI, E), F32),
            jax.ShapeDtypeStruct((ROWS, E), F32),
        ),
        in_specs=[whole(NQ // 128, 128), whole(CH, E), chunks(codes_i), chunks(codes_n)],
        out_specs=(
            whole(NQ // 128, 128),
            whole(CH, E),
            pl.BlockSpec((PB * CH, E), lambda r: (r, 0)),
            pl.BlockSpec((PB * CR, E), lambda r: (r, 0)),
        ),
        compiler_params=pltpu.CompilerParams(vmem_limit_bytes=62 * 1024 * 1024),
    )(loss, query_grad, item_codes, cache_codes)
    return loss.reshape(NQ), query_grad, item_grad, cache_grad


def solution(mesh):
    placed = (
        P("pb", None),
        P("pb"),
        P("col", None),
        P("col"),
        P("col", None),
        P("col", None),
        P("col"),
        P("col"),
    )
    return jax.shard_map(
        body,
        mesh=mesh,
        in_specs=placed,
        out_specs=(P("pb"), P(("pb", "col"), None), P("col", None), P("col", None)),
        check_vma=False,
    )
```

```python
import jax
import jax.numpy as jnp
from jax import lax
from jax.experimental import pallas as pl
from jax.experimental.pallas import tpu as pltpu
from jax.sharding import PartitionSpec as P

MESH = pl.DeviceIdType.MESH
F32 = jnp.float32
BF16 = jnp.bfloat16
I32 = jnp.int32
I16 = jnp.int16

E = 512
H = E // 2
NQ = 2048
QB = 256
NB = NQ // QB
NI = 512
NN = 512
NS = 1024
NC = 32
NZ = 8
CAP = 32
ROWS = 1024
CH = 64
INV_T = 20.0
PB = 4
W = E // 4
CR = ROWS // NZ
LN2 = 0.6931471805599453
SCALE2 = INV_T / LN2


def iota(shape, dim):
    return lax.broadcasted_iota(I32, shape, dim)


def onehot(cond):
    return jnp.where(cond, 1.0, 0.0).astype(BF16)


def dot_nn(a, b):
    return lax.dot_general(a, b, (((1,), (0,)), ((), ())), preferred_element_type=F32)


def dot_nt(a, b):
    return lax.dot_general(a, b, (((1,), (1,)), ((), ())), preferred_element_type=F32)


def dot_tn(a, b):
    return lax.dot_general(a, b, (((0,), (0,)), ((), ())), preferred_element_type=F32)


def halves(x):
    hi = x.astype(BF16)
    return hi, (x - hi.astype(F32)).astype(BF16)


def encode(x, group):
    rows, width = x.shape
    cube = x.reshape(rows // group, group, width)
    top = jnp.max(jnp.abs(cube), axis=0)
    expo = jnp.ceil(jnp.log2(jnp.maximum(top, 1e-30)))
    code = jnp.round(cube * jnp.exp2(14.99 - expo)[None])
    return code.reshape(rows, width).astype(I32).astype(I16), expo


def decode(code, expo):
    rows, width = code.shape
    group = expo.shape[0]
    cube = code.astype(I32).astype(F32).reshape(rows // group, group, width)
    return (cube * jnp.exp2(expo - 14.99)[None]).reshape(rows, width)


def to_i16(x):
    return x.astype(I32).astype(I16)


def from_i16(x):
    return x.astype(I32).astype(F32)


def unit(x):
    scale = jnp.sqrt(jnp.sum(x * x, axis=1, keepdims=True) + 1e-06)
    return x * (1.0 / scale), scale


def unit_back(grad, rows):
    direction, scale = unit(rows)
    return (grad - direction * jnp.sum(grad * direction, axis=1, keepdims=True)) / scale


def kernel(
    queries_hbm, positive_hbm, items_hbm, counts_i_hbm, counts_n_hbm, owner_hbm, row_hbm, cache_hbm,
    loss_out, query_out, item_codes, cache_codes,
    queries, positive, items, counts_i_ref, counts_n_ref, owner_ref, row_ref, cache, loss_buf, query_buf, msg, mrecv, cache_unit, scat, q_unit, cand_i, cand_n, shift_n,
    expo_i, expo_n, pos, tot, sums_i, factor_i, factor_n, weight_i, weight_n, part_i, part_n,
    slot_grad, slot_hi, slot_lo,
    send_i, recv_i, send_n, recv_n, ag_item, ag_cache, q_part, q_core, q_msg, q_recv,
    in_s, m_s, m_r, p_s, p_r, t_s, t_r, ri_s, ri_r, rn_s, rn_r, ai_s, ai_r, ac_s, ac_r, oi_s, oc_s,
    qc_s, qc_r, qd_s, qd_r, out_s,
):
    me = lax.axis_index("col")
    z = lax.axis_index("pb")
    core = me % 2
    chip = me // 2
    my_g = me // 4
    up = (z + 1) % NZ
    down = (z + NZ - 1) % NZ
    sibling = chip * 2 + 1 - core

    barrier = pltpu.get_barrier_semaphore()
    loads = [
        pltpu.make_async_copy(src, dst, in_s.at[i])
        for i, (src, dst) in enumerate(
            (
                (owner_hbm, owner_ref),
                (row_hbm, row_ref),
                (counts_n_hbm, counts_n_ref),
                (counts_i_hbm, counts_i_ref),
                (items_hbm, items),
                (positive_hbm, positive),
                (queries_hbm, queries),
                (cache_hbm, cache),
            )
        )
    ]
    for load in loads:
        load.start()

    @pl.loop(1, NC)
    def _(s):
        pl.semaphore_signal(barrier, inc=1, device_id={"col": (me + s) % NC}, device_id_type=MESH)

    for other in (up, down, (z + 2) % NZ, (z + NZ - 2) % NZ):
        pl.semaphore_signal(barrier, inc=1, device_id={"pb": other}, device_id_type=MESH)

    def remote(src, dst, send, recv, **where):
        return pltpu.make_async_remote_copy(
            src_ref=src, dst_ref=dst, send_sem=send, recv_sem=recv, device_id=where, device_id_type=MESH
        )

    def pair_row(ref, b):
        return jnp.concatenate([ref[pl.ds(2 * b, 1), :], ref[pl.ds(2 * b + 1, 1), :]], axis=1)

    def put_pair(ref, b, value):
        ref[pl.ds(2 * b, 1), :] = value[:, 0:128]
        ref[pl.ds(2 * b + 1, 1), :] = value[:, 128:]

    for load in loads[0:4]:
        load.wait()
    counts_i = counts_i_ref[...].astype(F32)
    counts_n = counts_n_ref[...].astype(F32)
    owner = owner_ref[...]
    row = row_ref[...]
    table = jnp.where(iota((NC, NN), 0) == owner, 1.0, 0.0)
    before = onehot(iota((NN, NN), 0) < iota((NN, NN), 1))
    earlier = dot_nn(table.astype(BF16), before)
    rank = jnp.sum(earlier * table, axis=0, keepdims=True).astype(I32)
    lane = onehot(iota((128, NN), 0) == CAP * (me % 4) + rank)
    named = jnp.concatenate(
        [table * (row >> 5).astype(F32), table * (row & 31).astype(F32), table * counts_n], axis=0
    )
    named = dot_nt(named.astype(BF16), lane)
    named = named[0:NC] * 32.0 + named[NC : 2 * NC] + named[2 * NC :] * ROWS
    total_i = jnp.sum(counts_i, axis=1, keepdims=True).reshape(1, 1, 1)
    total_n = jnp.sum(counts_n, axis=1, keepdims=True).reshape(1, 1, 1)
    line = iota((NC, 8, 128), 1)
    totals = jnp.where(line == (my_g + 1) % 8, total_i, jnp.where(line == (my_g + 2) % 8, total_n, 0.0))
    msg[...] = jnp.where(line == my_g, named.reshape(NC, 1, 128), totals)

    pl.semaphore_wait(barrier, NC + 3)

    def to_all(ref, send, recv, s):
        other = (me + s) % NC
        return remote(ref.at[me], ref.at[me], send.at[other], recv.at[me], col=other)

    def from_all(ref, send, recv, s):
        other = (me + s) % NC
        return remote(ref.at[me], ref.at[other], send.at[other], recv.at[other], col=other)

    @pl.loop(1, NC)
    def _(s):
        other = (me + s) % NC
        remote(msg.at[other], mrecv.at[me], m_s.at[other], m_r.at[me], col=other).start()

    mrecv[me] = msg[me]

    loads[4].wait()
    cand_i[...] = unit(items[...].astype(F32))[0].astype(BF16)
    same = iota((NI, NI), 0) == iota((NI, NI), 1)
    shift_i = jnp.log2(jnp.sum(jnp.where(same, counts_i, 0.0), axis=1, keepdims=True))
    first_item = me * NI
    loads[5].wait()
    loads[6].wait()

    @pl.loop(0, NB)
    def _(b):
        at = pl.ds(pl.multiple_of(b * QB, QB), QB)
        q_rows = unit(queries[at, :].astype(F32))[0].astype(BF16)
        q_unit[at, :] = q_rows
        logits = dot_nt(cand_i[...], q_rows) * SCALE2 - shift_i
        hit = positive[:, at] == first_item + iota((NI, QB), 0)
        expo = jnp.exp2(logits)
        expo_i[:, at] = expo
        put_pair(sums_i, b, jnp.sum(expo, axis=0, keepdims=True))
        put_pair(pos.at[me], b, jnp.sum(jnp.where(hit, logits, 0.0), axis=0, keepdims=True))

    loads[7].wait()

    @pl.loop(0, ROWS // QB)
    def _(b):
        at = pl.ds(pl.multiple_of(b * QB, QB), QB)
        cache_unit[at, :] = unit(cache[at, :].astype(F32))[0].astype(BF16)

    @pl.loop(1, NC)
    def _(s):
        other = (me + s) % NC
        remote(msg.at[other], mrecv.at[other], m_s.at[other], m_r.at[other], col=other).wait()

    line = iota((8, 128), 0)
    asked = jnp.zeros((8, 128), F32)
    sum_i = jnp.zeros((8, 128), F32)
    sum_n = jnp.zeros((8, 128), F32)
    for g in range(8):
        four = (mrecv[4 * g] + mrecv[4 * g + 1]) + (mrecv[4 * g + 2] + mrecv[4 * g + 3])
        asked = jnp.where(line == g, four, asked)
        sum_i = sum_i + jnp.where(line == (g + 1) % 8, four, 0.0)
        sum_n = sum_n + jnp.where(line == (g + 2) % 8, four, 0.0)
    total_i = jnp.sum(sum_i, axis=0, keepdims=True)[:, 0:1]
    total_n = jnp.sum(sum_n, axis=0, keepdims=True)[:, 0:1]

    @pl.loop(1, NC)
    def _(s):
        to_all(pos, p_s, p_r, s).start()

    def parts(value):
        count = jnp.floor(value * (1.0 / ROWS))
        return count, (value - count * ROWS).astype(I32)

    by_slot = jnp.concatenate([asked, jnp.zeros((120, 128), F32)], axis=0).T
    for half in range(2):
        picks = []
        for g in range(4 * half, 4 * half + 4):
            count, wanted = parts(by_slot[:, g : g + 1])
            shift_n[g * 128 : (g + 1) * 128, :] = jnp.where(
                count > 0.5, jnp.log2(jnp.maximum(count, 1.0)), 1e30
            )
            picks.append(onehot(iota((128, ROWS), 1) == wanted))
        picked = dot_nn(jnp.concatenate(picks, axis=0), cache_unit[...])
        cand_n[half * 512 : (half + 1) * 512, :] = picked.astype(BF16)

    def tot_copy(half, s, mine):
        other = (me + s) % NC
        slot = me if mine else other
        return remote(
            tot.at[half, me], tot.at[half, slot], t_s.at[half, other], t_r.at[half, slot], col=other
        )

    def scores_n(half):
        @pl.loop(half * NB // 2, (half + 1) * NB // 2)
        def _(b):
            at = pl.ds(pl.multiple_of(b * QB, QB), QB)
            expo = jnp.exp2(dot_nt(cand_n[...], q_unit[at, :]) * SCALE2 - shift_n[...])
            expo_n[:, at] = expo
            sum_n = total_n * jnp.sum(expo, axis=0, keepdims=True)
            put_pair(tot.at[half, me], b - half * (NB // 2), total_i * pair_row(sums_i, b) + sum_n)

        @pl.loop(1, NC)
        def _(s):
            tot_copy(half, s, True).start()

    scores_n(0)
    scores_n(1)
    slots = parts(asked)[1]
    for g in range(8):
        scat[:, g * 128 : (g + 1) * 128] = onehot(iota((ROWS, 128), 0) == slots[g : g + 1, :])

    def sums_in(half):
        @pl.loop(1, NC)
        def _(s):
            tot_copy(half, s, False).wait()

        total = jnp.sum(tot[half], axis=0)
        factor_i[half * 8 : (half + 1) * 8] = total_i / total
        factor_n[half * 8 : (half + 1) * 8] = total_n / total
        loss_buf[half * 8 : (half + 1) * 8] = jnp.log(total)

    def weights_i(half):
        @pl.loop(half * NB // 2, (half + 1) * NB // 2)
        def _(b):
            at = pl.ds(pl.multiple_of(b * QB, QB), QB)
            hit = positive[:, at] == first_item + iota((NI, QB), 0)
            weight_i[:, at] = (expo_i[:, at] * pair_row(factor_i, b) - jnp.where(hit, 1.0, 0.0)).astype(BF16)

    def weights_n(half):
        @pl.loop(half * NB // 2, (half + 1) * NB // 2)
        def _(b):
            at = pl.ds(pl.multiple_of(b * QB, QB), QB)
            weight_n[:, at] = (expo_n[:, at] * pair_row(factor_n, b)).astype(BF16)

    def grad_i(half):
        at = pl.ds(half * (NQ // 2), NQ // 2)
        grad = dot_nn(weight_i[:, at], q_unit[at, :]) * INV_T
        for k in range(4):
            at = (k // 2, slice(None), slice((k % 2) * CH, (k % 2 + 1) * CH))
            piece = grad[:, k * W : (k + 1) * W].reshape(NZ, CH, W)
            part_i[at] = piece if half == 0 else part_i[at] + piece

    def grad_n(half):
        at = pl.ds(half * (NQ // 2), NQ // 2)

        @pl.loop(0, NS // 512)
        def _(b):
            rows = pl.ds(pl.multiple_of(b * 512, 512), 512)
            grad = dot_nn(weight_n[rows, at], q_unit[at, :]) * INV_T
            if half == 0:
                slot_grad[rows, :] = grad
            else:
                hi, lo = halves(slot_grad[rows, :] + grad)
                slot_hi[rows, :] = hi
                slot_lo[rows, :] = lo

    def ring_peer(d):
        return up if d == 0 else down

    def ring_chunk(d, t):
        return (z + 4 - t) % NZ if d == 0 else (z + 4 + t) % NZ

    def streams(n, d):
        mine = [(k, 4) for k in range(n) if 2 * k // n == d]
        return mine + [(k, 3) for k in range(n) if 2 * k // n != d]

    def both_ways(n):
        for one, two in zip(streams(n, 0), streams(n, 1)):
            yield (0,) + one
            yield (1,) + two

    def pack(ref, chunk):
        code, e = encode(chunk, 16)
        ref[0:CR] = code
        ref[CR:] = to_i16(e)

    def unpack(ref):
        return decode(ref[0:CR], from_i16(ref[CR:]))

    def pack_two(ref, chunk):
        code, e = encode(chunk[0:CH], 8)
        code2, e2 = encode(chunk[CH:], 8)
        ref[0:CH] = code
        ref[CH : 2 * CH] = code2
        ref[2 * CH :] = to_i16(jnp.concatenate([e, e2], axis=0))

    def unpack_two(ref):
        e = from_i16(ref[2 * CH :])
        return jnp.concatenate([decode(ref[0:CH], e[0:8]), decode(ref[CH : 2 * CH], e[8:])], axis=0)

    def ring_copy(kind, d, t, k):
        _, send, recv, s, r = kind[:5]
        return remote(send.at[d, t, k], recv.at[d, t, k], s.at[d, t, k], r.at[d, t, k], pb=ring_peer(d))

    def ring_first(kind, t):
        part, send, _, _, _, n, put, _ = kind
        for d, k, steps in both_ways(n):
            if steps + t == 4:
                put(send.at[d, t, k], part[k, ring_chunk(d, t)])
                ring_copy(kind, d, t, k).start()

    def ring_step(kind, t):
        part, send, recv, _, _, n, put, get = kind
        for d, k, steps in both_ways(n):
            if steps + t > 4:
                ring_copy(kind, d, t - 1, k).wait()
                put(send.at[d, t, k], part[k, ring_chunk(d, t)] + get(recv.at[d, t - 1, k]))
                ring_copy(kind, d, t, k).start()

    def ring_last(kind):
        part, _, recv, _, _, n, _, get = kind
        own = [part[k, z] for k in range(n)]
        for d, k, _ in both_ways(n):
            ring_copy(kind, d, 3, k).wait()
            own[k] = own[k] + get(recv.at[d, 3, k])
        return own

    kind_i = (part_i, send_i, recv_i, ri_s, ri_r, 2, pack_two, unpack_two)
    kind_n = (part_n, send_n, recv_n, rn_s, rn_r, 4, pack, unpack)

    def by_row(pair):
        at = pl.ds(pl.multiple_of(pair * 256, 256), 256)
        grad = dot_nn(scat[at, :], slot_hi[...]) + dot_nn(scat[at, :], slot_lo[...])
        for k in range(4):
            part_n[k, pl.ds(pair * 2, 2)] = grad[:, k * W : (k + 1) * W].reshape(2, CR, W)

    def q_which(i):
        return (chip // 2 + i) % NB

    def q_copy(i):
        two = pl.ds(q_which(i) * 2, 2)
        return remote(q_part.at[two, 1 - core], q_core.at[two], qc_s.at[i], qc_r.at[i], col=sibling)

    def q_block(i):
        b = q_which(i)
        at = pl.ds(pl.multiple_of(b * QB, QB), QB)
        grad = dot_tn(weight_i[:, at], cand_i[...]) + dot_tn(weight_n[:, at], cand_n[...])
        q_part[pl.ds(b * 2, 2)] = (grad * INV_T).reshape(2, 2, CH, E)
        q_copy(i).start()

    def q_send(i):
        q_copy(i).wait()
        for j in range(2):
            c = q_which(i) * 2 + j
            grad = q_part[c, core] + q_core[c]
            pack_two(q_msg.at[c], jnp.concatenate([grad[:, :H], grad[:, H:]], axis=0))

            @pl.when(c != chip)
            def _():
                remote(q_msg.at[c], q_recv.at[chip], qd_s.at[c], qd_r.at[chip], col=c * 2 + core).start()

            @pl.when(c == chip)
            def _():
                q_recv[chip] = q_msg[c]

    def out_copy(kind, p, k):
        ref, _, _, out, sem, _ = kind
        return pltpu.make_async_copy(ref.at[p, k], out.at[p, k], sem.at[p, k])

    def behind(d, s):
        return (z + 2 * NZ - s) % NZ if d == 0 else (z + s) % NZ

    def gather_copy(d, s, k):
        ref = ag_cache.at[behind(d, s), k]
        return remote(ref, ref, ac_s.at[d, s, k], ac_r.at[d, s, k], pb=ring_peer(d))

    def gather_first(k):
        for d in range(2):
            gather_copy(d, 0, k).start()
        out_copy(out_n, z, k).start()

    def gather_wait(d, s, k):
        gather_copy(d, s, k).wait()
        out_copy(out_n, behind(d, s + 1), k).start()

    def gather_step(s):
        for d, k, steps in both_ways(4):
            if s < steps:
                gather_wait(d, s - 1, k)
                gather_copy(d, s, k).start()

    def gather_last():
        for three in (3, 4):
            for d, k, steps in both_ways(4):
                if steps == three:
                    gather_wait(d, steps - 1, k)

    def tree_copy(d, far, h):
        ref = ag_item.at[z if far <= 2 else behind(d, 2), h]
        hops = 2 - far % 2
        peer = behind(1 - d, hops)
        return remote(ref, ref, ai_s.at[d, far - 1, h], ai_r.at[d, far - 1, h], pb=peer)

    def tree_first(h):
        for far in (2, 1):
            for d in range(2):
                tree_copy(d, far, h).start()
        out_copy(out_i, z, h).start()

    def tree_wait(d, far, h):
        tree_copy(d, far, h).wait()
        out_copy(out_i, behind(d, far), h).start()

    def tree_second():
        for d, h, steps in both_ways(2):
            tree_wait(d, 2, h)
            for far in range(steps, 2, -1):
                tree_copy(d, far, h).start()

    def tree_last():
        for far in (1, 3, 4):
            for d, h, steps in both_ways(2):
                if far <= steps:
                    tree_wait(d, far, h)

    out_i = (ag_item, ai_s, ai_r, item_codes, oi_s, 2)
    out_n = (ag_cache, ac_s, ac_r, cache_codes, oc_s, 4)

    sums_in(0)
    weights_n(0)
    grad_n(0)
    sums_in(1)
    weights_n(1)
    grad_n(1)
    pair = ((z + 4) % NZ) // 2
    by_row(pair)
    ring_first(kind_n, 0)
    by_row((pair + 3) % 4)
    by_row((pair + 1) % 4)
    ring_first(kind_n, 1)
    weights_i(0)
    grad_i(0)
    ring_step(kind_n, 1)
    weights_i(1)
    grad_i(1)
    ring_first(kind_i, 0)
    ring_first(kind_i, 1)
    by_row((pair + 2) % 4)
    ring_step(kind_n, 2)
    q_block(0)
    q_block(1)
    ring_step(kind_i, 1)
    q_block(2)
    ring_step(kind_n, 3)
    q_block(3)
    ring_step(kind_i, 2)
    q_send(0)
    q_block(4)
    q_block(5)
    q_send(1)

    own = jnp.concatenate(ring_last(kind_n), axis=1)
    grad = unit_back(own, cache[pl.ds(pl.multiple_of(z * CR, CR), CR), :].astype(F32))
    for k in range(4):
        code, e = encode(grad[:, k * W : (k + 1) * W], 16)
        ag_cache[z, k, 0:CR] = code
        ag_cache[z, k, CR:] = to_i16(e)
        gather_first(k)

    ring_step(kind_i, 3)
    q_block(6)
    q_block(7)
    q_send(2)
    q_send(3)
    gather_step(1)

    own = ring_last(kind_i)
    own = jnp.concatenate([own[0][0:CH], own[0][CH:], own[1][0:CH], own[1][CH:]], axis=1)
    grad = unit_back(own, items[pl.ds(pl.multiple_of(z * CH, CH), CH), :].astype(F32))
    for h in range(2):
        wide = jnp.concatenate([grad[:, 2 * h * W : (2 * h + 1) * W], grad[:, (2 * h + 1) * W : (2 * h + 2) * W]], axis=0)
        pack_two(ag_item.at[z, h], wide)
        tree_first(h)

    q_send(4)
    q_send(5)
    q_send(6)
    q_send(7)
    gather_step(2)
    tree_second()

    @pl.loop(1, NC)
    def _(s):
        from_all(pos, p_s, p_r, s).wait()

    loss_buf[...] = loss_buf[...] - (jnp.sum(pos[...], axis=0) * LN2 + jnp.log(total_i))
    loss_copy = pltpu.make_async_copy(loss_buf, loss_out, out_s.at[0])
    loss_copy.start()
    gather_step(3)

    @pl.loop(1, NC // 2)
    def _(s):
        other = (chip + s) % (NC // 2)
        remote(q_msg.at[other], q_recv.at[other], qd_s.at[other], qd_r.at[other], col=other * 2 + core).wait()

    q_grad = unpack_two(q_recv.at[0])
    for c in range(1, NC // 2):
        q_grad = q_grad + unpack_two(q_recv.at[c])
    q_grad = jnp.concatenate([q_grad[0:CH], q_grad[CH:]], axis=1)
    query_buf[...] = unit_back(q_grad, queries[pl.ds(pl.multiple_of(me * CH, CH), CH), :].astype(F32))
    query_copy = pltpu.make_async_copy(query_buf, query_out, out_s.at[1])
    query_copy.start()

    tree_last()
    gather_last()

    @pl.loop(0, NZ)
    def _(p):
        for kind in (out_i, out_n):
            for k in range(kind[5]):
                out_copy(kind, p, k).wait()

    loss_copy.wait()
    query_copy.wait()


def last(loss, query, item_codes, cache_codes, loss_out, query_out, item_out, cache_out):
    for p in range(PB):
        for k in range(4):
            columns = slice(k * W, (k + 1) * W)
            part = k % 2
            e = from_i16(item_codes[p, k // 2, CR:])[8 * part : 8 * part + 8]
            item_out[p * CH : (p + 1) * CH, columns] = decode(item_codes[p, k // 2, part * CH : part * CH + CH], e)
            cache_out[p * CR : (p + 1) * CR, columns] = decode(
                cache_codes[p, k, 0:CR], from_i16(cache_codes[p, k, CR:])
            )

    @pl.when(pl.program_id(0) == 0)
    def _():
        loss_out[...] = loss[...]
        query_out[...] = query[...]


def body(queries, positive, items, item_counts, cache, neg_owner, neg_row, neg_counts):
    hbm = pl.BlockSpec(memory_space=pl.ANY)
    dma = pltpu.SemaphoreType.DMA
    codes_i = (NZ, 2, CR + 16, W)
    codes_n = (NZ, 4, CR + 16, W)
    ring_i = (2, 4, 2, CR + 16, W)
    ring_n = (2, 4, 4, CR + 16, W)
    scratch = [
        pltpu.VMEM((NQ, E), BF16),
        pltpu.VMEM((1, NQ), I32),
        pltpu.VMEM((NI, E), BF16),
        pltpu.VMEM((1, NI), I32),
        pltpu.VMEM((1, NN), I32),
        pltpu.VMEM((1, NN), I32),
        pltpu.VMEM((1, NN), I32),
        pltpu.VMEM((ROWS, E), BF16),
        pltpu.VMEM((NQ // 128, 128), F32),
        pltpu.VMEM((CH, E), F32),
        pltpu.VMEM((NC, 8, 128), F32),
        pltpu.VMEM((NC, 8, 128), F32),
        pltpu.VMEM((ROWS, E), BF16),
        pltpu.VMEM((ROWS, NS), BF16),
        pltpu.VMEM((NQ, E), BF16),
        pltpu.VMEM((NI, E), BF16),
        pltpu.VMEM((NS, E), BF16),
        pltpu.VMEM((NS, 1), F32),
        pltpu.VMEM((NI, NQ), F32),
        pltpu.VMEM((NS, NQ), F32),
        pltpu.VMEM((NC, NQ // 128, 128), F32),
        pltpu.VMEM((2, NC, NQ // 256, 128), F32),
        pltpu.VMEM((NQ // 128, 128), F32),
        pltpu.VMEM((NQ // 128, 128), F32),
        pltpu.VMEM((NQ // 128, 128), F32),
        pltpu.VMEM((NI, NQ), BF16),
        pltpu.VMEM((NS, NQ), BF16),
        pltpu.VMEM((2, NZ, 2 * CH, W), F32),
        pltpu.VMEM((4, NZ, CR, W), F32),
        pltpu.VMEM((NS, E), F32),
        pltpu.VMEM((NS, E), BF16),
        pltpu.VMEM((NS, E), BF16),
        pltpu.VMEM(ring_i, I16),
        pltpu.VMEM(ring_i, I16),
        pltpu.VMEM(ring_n, I16),
        pltpu.VMEM(ring_n, I16),
        pltpu.VMEM(codes_i, I16),
        pltpu.VMEM(codes_n, I16),
        pltpu.VMEM((NC // 2, 2, CH, E), F32),
        pltpu.VMEM((NC // 2, CH, E), F32),
        pltpu.VMEM((NC // 2, 2 * CH + 16, H), I16),
        pltpu.VMEM((NC // 2, 2 * CH + 16, H), I16),
        dma((8,)),
        dma((NC,)), dma((NC,)),
        dma((NC,)), dma((NC,)),
        dma((2, NC)), dma((2, NC)),
        dma((2, 4, 2)), dma((2, 4, 2)),
        dma((2, 4, 4)), dma((2, 4, 4)),
        dma((2, 4, 2)), dma((2, 4, 2)),
        dma((2, 4, 4)), dma((2, 4, 4)),
        dma((NZ, 2)), dma((NZ, 4)),
        dma((NB,)), dma((NB,)),
        dma((NC // 2,)), dma((NC // 2,)),
        dma((2,)),
    ]
    loss, query_grad, item_codes, cache_codes = pl.pallas_call(
        kernel,
        out_shape=(
            jax.ShapeDtypeStruct((NQ // 128, 128), F32),
            jax.ShapeDtypeStruct((CH, E), F32),
            jax.ShapeDtypeStruct(codes_i, I16),
            jax.ShapeDtypeStruct(codes_n, I16),
        ),
        in_specs=[hbm] * 8,
        out_specs=(hbm,) * 4,
        scratch_shapes=scratch,
        compiler_params=pltpu.CompilerParams(
            collective_id=0, has_side_effects=True, vmem_limit_bytes=62 * 1024 * 1024
        ),
    )(
        queries,
        positive.reshape(1, NQ),
        items,
        item_counts.reshape(1, NI),
        neg_counts.reshape(1, NN),
        neg_owner.reshape(1, NN),
        neg_row.reshape(1, NN),
        cache,
    )

    def whole(*shape):
        return pl.BlockSpec(shape, lambda r: (0,) * len(shape))

    def chunks(shape):
        return pl.BlockSpec((PB,) + shape[1:], lambda r: (r, 0, 0, 0))

    loss, query_grad, item_grad, cache_grad = pl.pallas_call(
        last,
        grid=(NZ // PB,),
        out_shape=(
            jax.ShapeDtypeStruct((NQ // 128, 128), F32),
            jax.ShapeDtypeStruct((CH, E), F32),
            jax.ShapeDtypeStruct((NI, E), F32),
            jax.ShapeDtypeStruct((ROWS, E), F32),
        ),
        in_specs=[whole(NQ // 128, 128), whole(CH, E), chunks(codes_i), chunks(codes_n)],
        out_specs=(
            whole(NQ // 128, 128),
            whole(CH, E),
            pl.BlockSpec((PB * CH, E), lambda r: (r, 0)),
            pl.BlockSpec((PB * CR, E), lambda r: (r, 0)),
        ),
        compiler_params=pltpu.CompilerParams(vmem_limit_bytes=62 * 1024 * 1024),
    )(loss, query_grad, item_codes, cache_codes)
    return loss.reshape(NQ), query_grad, item_grad, cache_grad


def solution(mesh):
    placed = (
        P("pb", None),
        P("pb"),
        P("col", None),
        P("col"),
        P("col", None),
        P("col", None),
        P("col"),
        P("col"),
    )
    return jax.shard_map(
        body,
        mesh=mesh,
        in_specs=placed,
        out_specs=(P("pb"), P(("pb", "col"), None), P("col", None), P("col", None)),
        check_vma=False,
    )
```

```python
import jax
import jax.numpy as jnp
from jax import lax
from jax.experimental import pallas as pl
from jax.experimental.pallas import tpu as pltpu
from jax.sharding import PartitionSpec as P

MESH = pl.DeviceIdType.MESH
F32 = jnp.float32
BF16 = jnp.bfloat16
I32 = jnp.int32
I16 = jnp.int16

E = 512
H = E // 2
NQ = 2048
QB = 256
NB = NQ // QB
NI = 512
NN = 512
NS = 1024
NC = 32
NZ = 8
CAP = 32
ROWS = 1024
CH = 64
INV_T = 20.0
PB = 4
W = E // 4
CR = ROWS // NZ
LN2 = 0.6931471805599453
SCALE2 = INV_T / LN2


def iota(shape, dim):
    return lax.broadcasted_iota(I32, shape, dim)


def onehot(cond):
    return jnp.where(cond, 1.0, 0.0).astype(BF16)


def dot_nn(a, b):
    return lax.dot_general(a, b, (((1,), (0,)), ((), ())), preferred_element_type=F32)


def dot_nt(a, b):
    return lax.dot_general(a, b, (((1,), (1,)), ((), ())), preferred_element_type=F32)


def dot_tn(a, b):
    return lax.dot_general(a, b, (((0,), (0,)), ((), ())), preferred_element_type=F32)


def halves(x):
    hi = x.astype(BF16)
    return hi, (x - hi.astype(F32)).astype(BF16)


def encode(x, group):
    rows, width = x.shape
    cube = x.reshape(rows // group, group, width)
    top = jnp.max(jnp.abs(cube), axis=0)
    expo = jnp.ceil(jnp.log2(jnp.maximum(top, 1e-30)))
    code = jnp.round(cube * jnp.exp2(14.99 - expo)[None])
    return code.reshape(rows, width).astype(I32).astype(I16), expo


def decode(code, expo):
    rows, width = code.shape
    group = expo.shape[0]
    cube = code.astype(I32).astype(F32).reshape(rows // group, group, width)
    return (cube * jnp.exp2(expo - 14.99)[None]).reshape(rows, width)


def to_i16(x):
    return x.astype(I32).astype(I16)


def from_i16(x):
    return x.astype(I32).astype(F32)


def unit(x):
    scale = jnp.sqrt(jnp.sum(x * x, axis=1, keepdims=True) + 1e-06)
    return x * (1.0 / scale), scale


def unit_back(grad, rows):
    direction, scale = unit(rows)
    return (grad - direction * jnp.sum(grad * direction, axis=1, keepdims=True)) / scale


def kernel(
    queries_hbm, positive_hbm, items_hbm, counts_i_hbm, counts_n_hbm, owner_hbm, row_hbm, cache_hbm,
    loss_out, query_out, item_codes, cache_codes,
    queries, positive, items, counts_i_ref, counts_n_ref, owner_ref, row_ref, cache, loss_buf, query_buf, msg, mrecv, cache_unit, scat, q_unit, cand_i, cand_n, shift_n,
    expo_i, expo_n, pos, tot, sums_i, factor_i, factor_n, weight_i, weight_n, part_i, part_n,
    slot_grad, slot_hi, slot_lo,
    send_i, recv_i, send_n, recv_n, ag_item, ag_cache, q_part, q_core, q_msg, q_recv,
    in_s, m_s, m_r, p_s, p_r, t_s, t_r, ri_s, ri_r, rn_s, rn_r, ai_s, ai_r, ac_s, ac_r, oi_s, oc_s,
    qc_s, qc_r, qd_s, qd_r, out_s,
):
    me = lax.axis_index("col")
    z = lax.axis_index("pb")
    core = me % 2
    chip = me // 2
    my_g = me // 4
    up = (z + 1) % NZ
    down = (z + NZ - 1) % NZ
    sibling = chip * 2 + 1 - core

    barrier = pltpu.get_barrier_semaphore()
    loads = [
        pltpu.make_async_copy(src, dst, in_s.at[i])
        for i, (src, dst) in enumerate(
            (
                (owner_hbm, owner_ref),
                (row_hbm, row_ref),
                (counts_n_hbm, counts_n_ref),
                (counts_i_hbm, counts_i_ref),
                (items_hbm, items),
                (positive_hbm, positive),
                (queries_hbm, queries),
                (cache_hbm, cache),
            )
        )
    ]
    for load in loads:
        load.start()

    @pl.loop(1, NC)
    def _(s):
        pl.semaphore_signal(barrier, inc=1, device_id={"col": (me + s) % NC}, device_id_type=MESH)

    for other in (up, down):
        pl.semaphore_signal(barrier, inc=1, device_id={"pb": other}, device_id_type=MESH)

    def remote(src, dst, send, recv, **where):
        return pltpu.make_async_remote_copy(
            src_ref=src, dst_ref=dst, send_sem=send, recv_sem=recv, device_id=where, device_id_type=MESH
        )

    def pair_row(ref, b):
        return jnp.concatenate([ref[pl.ds(2 * b, 1), :], ref[pl.ds(2 * b + 1, 1), :]], axis=1)

    def put_pair(ref, b, value):
        ref[pl.ds(2 * b, 1), :] = value[:, 0:128]
        ref[pl.ds(2 * b + 1, 1), :] = value[:, 128:]

    for load in loads[0:4]:
        load.wait()
    counts_i = counts_i_ref[...].astype(F32)
    counts_n = counts_n_ref[...].astype(F32)
    owner = owner_ref[...]
    row = row_ref[...]
    table = jnp.where(iota((NC, NN), 0) == owner, 1.0, 0.0)
    before = onehot(iota((NN, NN), 0) < iota((NN, NN), 1))
    earlier = dot_nn(table.astype(BF16), before)
    rank = jnp.sum(earlier * table, axis=0, keepdims=True).astype(I32)
    lane = onehot(iota((128, NN), 0) == CAP * (me % 4) + rank)
    named = jnp.concatenate(
        [table * (row >> 5).astype(F32), table * (row & 31).astype(F32), table * counts_n], axis=0
    )
    named = dot_nt(named.astype(BF16), lane)
    named = named[0:NC] * 32.0 + named[NC : 2 * NC] + named[2 * NC :] * ROWS
    total_i = jnp.sum(counts_i, axis=1, keepdims=True).reshape(1, 1, 1)
    total_n = jnp.sum(counts_n, axis=1, keepdims=True).reshape(1, 1, 1)
    line = iota((NC, 8, 128), 1)
    totals = jnp.where(line == (my_g + 1) % 8, total_i, jnp.where(line == (my_g + 2) % 8, total_n, 0.0))
    msg[...] = jnp.where(line == my_g, named.reshape(NC, 1, 128), totals)

    pl.semaphore_wait(barrier, NC + 1)

    def to_all(ref, send, recv, s):
        other = (me + s) % NC
        return remote(ref.at[me], ref.at[me], send.at[other], recv.at[me], col=other)

    def from_all(ref, send, recv, s):
        other = (me + s) % NC
        return remote(ref.at[me], ref.at[other], send.at[other], recv.at[other], col=other)

    @pl.loop(1, NC)
    def _(s):
        other = (me + s) % NC
        remote(msg.at[other], mrecv.at[me], m_s.at[other], m_r.at[me], col=other).start()

    mrecv[me] = msg[me]

    loads[4].wait()
    cand_i[...] = unit(items[...].astype(F32))[0].astype(BF16)
    same = iota((NI, NI), 0) == iota((NI, NI), 1)
    shift_i = jnp.log2(jnp.sum(jnp.where(same, counts_i, 0.0), axis=1, keepdims=True))
    first_item = me * NI
    loads[5].wait()
    loads[6].wait()

    @pl.loop(0, NB, unroll=4)
    def _(b):
        at = pl.ds(pl.multiple_of(b * QB, QB), QB)
        q_rows = unit(queries[at, :].astype(F32))[0].astype(BF16)
        q_unit[at, :] = q_rows
        logits = dot_nt(cand_i[...], q_rows) * SCALE2 - shift_i
        hit = positive[:, at] == first_item + iota((NI, QB), 0)
        expo = jnp.exp2(logits)
        expo_i[:, at] = expo
        put_pair(sums_i, b, jnp.sum(expo, axis=0, keepdims=True))
        put_pair(pos.at[me], b, jnp.sum(jnp.where(hit, logits, 0.0), axis=0, keepdims=True))

    loads[7].wait()

    @pl.loop(0, ROWS // QB)
    def _(b):
        at = pl.ds(pl.multiple_of(b * QB, QB), QB)
        cache_unit[at, :] = unit(cache[at, :].astype(F32))[0].astype(BF16)

    @pl.loop(1, NC)
    def _(s):
        other = (me + s) % NC
        remote(msg.at[other], mrecv.at[other], m_s.at[other], m_r.at[other], col=other).wait()

    line = iota((8, 128), 0)
    asked = jnp.zeros((8, 128), F32)
    sum_i = jnp.zeros((8, 128), F32)
    sum_n = jnp.zeros((8, 128), F32)
    for g in range(8):
        four = (mrecv[4 * g] + mrecv[4 * g + 1]) + (mrecv[4 * g + 2] + mrecv[4 * g + 3])
        asked = jnp.where(line == g, four, asked)
        sum_i = sum_i + jnp.where(line == (g + 1) % 8, four, 0.0)
        sum_n = sum_n + jnp.where(line == (g + 2) % 8, four, 0.0)
    total_i = jnp.sum(sum_i, axis=0, keepdims=True)[:, 0:1]
    total_n = jnp.sum(sum_n, axis=0, keepdims=True)[:, 0:1]

    @pl.loop(1, NC)
    def _(s):
        to_all(pos, p_s, p_r, s).start()

    def parts(value):
        count = jnp.floor(value * (1.0 / ROWS))
        return count, (value - count * ROWS).astype(I32)

    by_slot = jnp.concatenate([asked, jnp.zeros((120, 128), F32)], axis=0).T
    for half in range(2):
        picks = []
        for g in range(4 * half, 4 * half + 4):
            count, wanted = parts(by_slot[:, g : g + 1])
            shift_n[g * 128 : (g + 1) * 128, :] = jnp.where(
                count > 0.5, jnp.log2(jnp.maximum(count, 1.0)), 1e30
            )
            picks.append(onehot(iota((128, ROWS), 1) == wanted))
        picked = dot_nn(jnp.concatenate(picks, axis=0), cache_unit[...])
        cand_n[half * 512 : (half + 1) * 512, :] = picked.astype(BF16)

    def tot_copy(half, s, mine):
        other = (me + s) % NC
        slot = me if mine else other
        return remote(
            tot.at[half, me], tot.at[half, slot], t_s.at[half, other], t_r.at[half, slot], col=other
        )

    def scores_n(half):
        @pl.loop(half * NB // 2, (half + 1) * NB // 2, unroll=4)
        def _(b):
            at = pl.ds(pl.multiple_of(b * QB, QB), QB)
            expo = jnp.exp2(dot_nt(cand_n[...], q_unit[at, :]) * SCALE2 - shift_n[...])
            expo_n[:, at] = expo
            sum_n = total_n * jnp.sum(expo, axis=0, keepdims=True)
            put_pair(tot.at[half, me], b - half * (NB // 2), total_i * pair_row(sums_i, b) + sum_n)

        @pl.loop(1, NC)
        def _(s):
            tot_copy(half, s, True).start()

    scores_n(0)
    scores_n(1)
    slots = parts(asked)[1]
    for g in range(8):
        scat[:, g * 128 : (g + 1) * 128] = onehot(iota((ROWS, 128), 0) == slots[g : g + 1, :])

    def sums_in(half):
        @pl.loop(1, NC)
        def _(s):
            tot_copy(half, s, False).wait()

        total = jnp.sum(tot[half], axis=0)
        factor_i[half * 8 : (half + 1) * 8] = total_i / total
        factor_n[half * 8 : (half + 1) * 8] = total_n / total
        loss_buf[half * 8 : (half + 1) * 8] = jnp.log(total)

    def factors(ref, half):
        return jnp.concatenate([ref[half * 8 + k : half * 8 + k + 1, :] for k in range(8)], axis=1)

    def grad_i(half):
        at = pl.ds(half * (NQ // 2), NQ // 2)
        factor = factors(factor_i, half)
        for b in range(2):
            rows = slice(b * (NI // 2), (b + 1) * (NI // 2))
            hit = positive[:, at] == first_item + b * (NI // 2) + iota((NI // 2, NQ // 2), 0)
            weights = (expo_i[rows, at] * factor - jnp.where(hit, 1.0, 0.0)).astype(BF16)
            weight_i[rows, at] = weights
            grad = dot_nn(weights, q_unit[at, :]) * INV_T
            for k in range(4):
                to = (k // 2, slice(b * (NZ // 2), (b + 1) * (NZ // 2)), slice((k % 2) * CH, (k % 2 + 1) * CH))
                piece = grad[:, k * W : (k + 1) * W].reshape(NZ // 2, CH, W)
                part_i[to] = piece if half == 0 else part_i[to] + piece

    def grad_n(half):
        at = pl.ds(half * (NQ // 2), NQ // 2)
        factor = factors(factor_n, half)
        for b in range(2):
            rows = slice(b * (NS // 2), (b + 1) * (NS // 2))
            weights = (expo_n[rows, at] * factor).astype(BF16)
            weight_n[rows, at] = weights
            grad = dot_nn(weights, q_unit[at, :]) * INV_T
            if half == 0:
                slot_grad[rows, :] = grad
            else:
                hi, lo = halves(slot_grad[rows, :] + grad)
                slot_hi[rows, :] = hi
                slot_lo[rows, :] = lo

    def ring_peer(d):
        return up if d == 0 else down

    def ring_chunk(d, t):
        return (z + 4 - t) % NZ if d == 0 else (z + 4 + t) % NZ

    def streams(n, d):
        mine = [(k, 4) for k in range(n) if 2 * k // n == d]
        return mine + [(k, 3) for k in range(n) if 2 * k // n != d]

    def both_ways(n):
        for one, two in zip(streams(n, 0), streams(n, 1)):
            yield (0,) + one
            yield (1,) + two

    def pack(ref, chunk):
        code, e = encode(chunk, 16)
        ref[0:CR] = code
        ref[CR:] = to_i16(e)

    def unpack(ref):
        return decode(ref[0:CR], from_i16(ref[CR:]))

    def pack_two(ref, chunk):
        code, e = encode(chunk[0:CH], 8)
        code2, e2 = encode(chunk[CH:], 8)
        ref[0:CH] = code
        ref[CH : 2 * CH] = code2
        ref[2 * CH :] = to_i16(jnp.concatenate([e, e2], axis=0))

    def unpack_two(ref):
        e = from_i16(ref[2 * CH :])
        return jnp.concatenate([decode(ref[0:CH], e[0:8]), decode(ref[CH : 2 * CH], e[8:])], axis=0)

    def ring_copy(kind, d, t, k):
        _, send, recv, s, r = kind[:5]
        return remote(send.at[d, t, k], recv.at[d, t, k], s.at[d, t, k], r.at[d, t, k], pb=ring_peer(d))

    def ring_first(kind, t):
        part, send, _, _, _, n, put, _ = kind
        for d, k, steps in both_ways(n):
            if steps + t == 4:
                put(send.at[d, t, k], part[k, ring_chunk(d, t)])
                ring_copy(kind, d, t, k).start()

    def ring_step(kind, t):
        part, send, recv, _, _, n, put, get = kind
        for d, k, steps in both_ways(n):
            if steps + t > 4:
                ring_copy(kind, d, t - 1, k).wait()
                put(send.at[d, t, k], part[k, ring_chunk(d, t)] + get(recv.at[d, t - 1, k]))
                ring_copy(kind, d, t, k).start()

    def ring_last(kind):
        part, _, recv, _, _, n, _, get = kind
        own = [part[k, z] for k in range(n)]
        for d, k, _ in both_ways(n):
            ring_copy(kind, d, 3, k).wait()
            own[k] = own[k] + get(recv.at[d, 3, k])
        return own

    kind_i = (part_i, send_i, recv_i, ri_s, ri_r, 2, pack_two, unpack_two)
    kind_n = (part_n, send_n, recv_n, rn_s, rn_r, 4, pack, unpack)

    def by_row(pair):
        at = pl.ds(pl.multiple_of(pair * 256, 256), 256)
        grad = dot_nn(scat[at, :], slot_hi[...]) + dot_nn(scat[at, :], slot_lo[...])
        for k in range(4):
            part_n[k, pl.ds(pair * 2, 2)] = grad[:, k * W : (k + 1) * W].reshape(2, CR, W)

    def q_which(i):
        return (chip // 2 + i) % NB

    def q_copy(i):
        two = pl.ds(q_which(i) * 2, 2)
        return remote(q_part.at[two, 1 - core], q_core.at[two], qc_s.at[i], qc_r.at[i], col=sibling)

    def q_block(i):
        b = q_which(i)
        at = pl.ds(pl.multiple_of(b * QB, QB), QB)
        grad = dot_tn(weight_i[:, at], cand_i[...]) + dot_tn(weight_n[:, at], cand_n[...])
        q_part[pl.ds(b * 2, 2)] = (grad * INV_T).reshape(2, 2, CH, E)
        q_copy(i).start()

    def q_send(i):
        q_copy(i).wait()
        for j in range(2):
            c = q_which(i) * 2 + j
            grad = q_part[c, core] + q_core[c]
            pack_two(q_msg.at[c], jnp.concatenate([grad[:, :H], grad[:, H:]], axis=0))

            @pl.when(c != chip)
            def _():
                remote(q_msg.at[c], q_recv.at[chip], qd_s.at[c], qd_r.at[chip], col=c * 2 + core).start()

            @pl.when(c == chip)
            def _():
                q_recv[chip] = q_msg[c]

    def out_copy(kind, p, k):
        ref, _, _, out, sem, _ = kind
        return pltpu.make_async_copy(ref.at[p, k], out.at[p, k], sem.at[p, k])

    def behind(d, s):
        return (z + 2 * NZ - s) % NZ if d == 0 else (z + s) % NZ

    def gather_copy(kind, d, s, k):
        ref, send, recv = kind[:3]
        ref = ref.at[behind(d, s), k]
        return remote(ref, ref, send.at[d, s, k], recv.at[d, s, k], pb=ring_peer(d))

    def gather_first(kind, k):
        for d in range(2):
            gather_copy(kind, d, 0, k).start()
        out_copy(kind, z, k).start()

    def gather_wait(kind, d, s, k):
        gather_copy(kind, d, s, k).wait()
        out_copy(kind, behind(d, s + 1), k).start()

    def gather_step(kind, s):
        for d, k, steps in both_ways(kind[5]):
            if s < steps:
                gather_wait(kind, d, s - 1, k)
                gather_copy(kind, d, s, k).start()

    def gather_last(kind):
        for three in (3, 4):
            for d, k, steps in both_ways(kind[5]):
                if steps == three:
                    gather_wait(kind, d, steps - 1, k)

    out_i = (ag_item, ai_s, ai_r, item_codes, oi_s, 2)
    out_n = (ag_cache, ac_s, ac_r, cache_codes, oc_s, 4)

    sums_in(0)
    grad_n(0)
    sums_in(1)
    grad_n(1)
    pair = ((z + 4) % NZ) // 2
    by_row(pair)
    ring_first(kind_n, 0)
    grad_i(0)
    grad_i(1)
    ring_first(kind_i, 0)
    ring_first(kind_i, 1)
    by_row((pair + 3) % 4)
    by_row((pair + 1) % 4)
    ring_first(kind_n, 1)
    ring_step(kind_n, 1)
    by_row((pair + 2) % 4)
    ring_step(kind_i, 1)
    q_block(0)
    q_block(1)
    q_block(2)
    ring_step(kind_n, 2)
    ring_step(kind_i, 2)
    q_block(3)
    q_block(4)
    q_send(0)
    ring_step(kind_n, 3)
    ring_step(kind_i, 3)
    q_block(5)
    q_block(6)
    q_block(7)
    q_send(1)

    own = jnp.concatenate(ring_last(kind_n), axis=1)
    grad = unit_back(own, cache[pl.ds(pl.multiple_of(z * CR, CR), CR), :].astype(F32))
    for k in range(4):
        pack(ag_cache.at[z, k], grad[:, k * W : (k + 1) * W])
        gather_first(out_n, k)

    own = ring_last(kind_i)
    own = jnp.concatenate([own[0][0:CH], own[0][CH:], own[1][0:CH], own[1][CH:]], axis=1)
    grad = unit_back(own, items[pl.ds(pl.multiple_of(z * CH, CH), CH), :].astype(F32))
    for h in range(2):
        left, right = grad[:, 2 * h * W : (2 * h + 1) * W], grad[:, (2 * h + 1) * W : (2 * h + 2) * W]
        pack_two(ag_item.at[z, h], jnp.concatenate([left, right], axis=0))
        gather_first(out_i, h)

    q_send(2)
    q_send(3)
    q_send(4)
    gather_step(out_n, 1)
    gather_step(out_i, 1)
    q_send(5)
    q_send(6)
    q_send(7)
    gather_step(out_n, 2)
    gather_step(out_i, 2)

    @pl.loop(1, NC)
    def _(s):
        from_all(pos, p_s, p_r, s).wait()

    loss_buf[...] = loss_buf[...] - (jnp.sum(pos[...], axis=0) * LN2 + jnp.log(total_i))
    loss_copy = pltpu.make_async_copy(loss_buf, loss_out, out_s.at[0])
    loss_copy.start()
    gather_step(out_n, 3)
    gather_step(out_i, 3)

    @pl.loop(1, NC // 2)
    def _(s):
        other = (chip + s) % (NC // 2)
        remote(q_msg.at[other], q_recv.at[other], qd_s.at[other], qd_r.at[other], col=other * 2 + core).wait()

    q_grad = unpack_two(q_recv.at[0])
    for c in range(1, NC // 2):
        q_grad = q_grad + unpack_two(q_recv.at[c])
    q_grad = jnp.concatenate([q_grad[0:CH], q_grad[CH:]], axis=1)
    query_buf[...] = unit_back(q_grad, queries[pl.ds(pl.multiple_of(me * CH, CH), CH), :].astype(F32))
    query_copy = pltpu.make_async_copy(query_buf, query_out, out_s.at[1])
    query_copy.start()

    gather_last(out_n)
    gather_last(out_i)

    @pl.loop(0, NZ)
    def _(p):
        for kind in (out_i, out_n):
            for k in range(kind[5]):
                out_copy(kind, p, k).wait()

    loss_copy.wait()
    query_copy.wait()


def last(loss, query, item_codes, cache_codes, loss_out, query_out, item_out, cache_out):
    for p in range(PB):
        for k in range(4):
            columns = slice(k * W, (k + 1) * W)
            part = k % 2
            e = from_i16(item_codes[p, k // 2, CR:])[8 * part : 8 * part + 8]
            item_out[p * CH : (p + 1) * CH, columns] = decode(item_codes[p, k // 2, part * CH : part * CH + CH], e)
            cache_out[p * CR : (p + 1) * CR, columns] = decode(
                cache_codes[p, k, 0:CR], from_i16(cache_codes[p, k, CR:])
            )

    @pl.when(pl.program_id(0) == 0)
    def _():
        loss_out[...] = loss[...]
        query_out[...] = query[...]


def body(queries, positive, items, item_counts, cache, neg_owner, neg_row, neg_counts):
    hbm = pl.BlockSpec(memory_space=pl.ANY)
    dma = pltpu.SemaphoreType.DMA
    codes_i = (NZ, 2, CR + 16, W)
    codes_n = (NZ, 4, CR + 16, W)
    ring_i = (2, 4, 2, CR + 16, W)
    ring_n = (2, 4, 4, CR + 16, W)
    scratch = [
        pltpu.VMEM((NQ, E), BF16),
        pltpu.VMEM((1, NQ), I32),
        pltpu.VMEM((NI, E), BF16),
        pltpu.VMEM((1, NI), I32),
        pltpu.VMEM((1, NN), I32),
        pltpu.VMEM((1, NN), I32),
        pltpu.VMEM((1, NN), I32),
        pltpu.VMEM((ROWS, E), BF16),
        pltpu.VMEM((NQ // 128, 128), F32),
        pltpu.VMEM((CH, E), F32),
        pltpu.VMEM((NC, 8, 128), F32),
        pltpu.VMEM((NC, 8, 128), F32),
        pltpu.VMEM((ROWS, E), BF16),
        pltpu.VMEM((ROWS, NS), BF16),
        pltpu.VMEM((NQ, E), BF16),
        pltpu.VMEM((NI, E), BF16),
        pltpu.VMEM((NS, E), BF16),
        pltpu.VMEM((NS, 1), F32),
        pltpu.VMEM((NI, NQ), F32),
        pltpu.VMEM((NS, NQ), F32),
        pltpu.VMEM((NC, NQ // 128, 128), F32),
        pltpu.VMEM((2, NC, NQ // 256, 128), F32),
        pltpu.VMEM((NQ // 128, 128), F32),
        pltpu.VMEM((NQ // 128, 128), F32),
        pltpu.VMEM((NQ // 128, 128), F32),
        pltpu.VMEM((NI, NQ), BF16),
        pltpu.VMEM((NS, NQ), BF16),
        pltpu.VMEM((2, NZ, 2 * CH, W), F32),
        pltpu.VMEM((4, NZ, CR, W), F32),
        pltpu.VMEM((NS, E), F32),
        pltpu.VMEM((NS, E), BF16),
        pltpu.VMEM((NS, E), BF16),
        pltpu.VMEM(ring_i, I16),
        pltpu.VMEM(ring_i, I16),
        pltpu.VMEM(ring_n, I16),
        pltpu.VMEM(ring_n, I16),
        pltpu.VMEM(codes_i, I16),
        pltpu.VMEM(codes_n, I16),
        pltpu.VMEM((NC // 2, 2, CH, E), F32),
        pltpu.VMEM((NC // 2, CH, E), F32),
        pltpu.VMEM((NC // 2, 2 * CH + 16, H), I16),
        pltpu.VMEM((NC // 2, 2 * CH + 16, H), I16),
        dma((8,)),
        dma((NC,)), dma((NC,)),
        dma((NC,)), dma((NC,)),
        dma((2, NC)), dma((2, NC)),
        dma((2, 4, 2)), dma((2, 4, 2)),
        dma((2, 4, 4)), dma((2, 4, 4)),
        dma((2, 4, 2)), dma((2, 4, 2)),
        dma((2, 4, 4)), dma((2, 4, 4)),
        dma((NZ, 2)), dma((NZ, 4)),
        dma((NB,)), dma((NB,)),
        dma((NC // 2,)), dma((NC // 2,)),
        dma((2,)),
    ]
    loss, query_grad, item_codes, cache_codes = pl.pallas_call(
        kernel,
        out_shape=(
            jax.ShapeDtypeStruct((NQ // 128, 128), F32),
            jax.ShapeDtypeStruct((CH, E), F32),
            jax.ShapeDtypeStruct(codes_i, I16),
            jax.ShapeDtypeStruct(codes_n, I16),
        ),
        in_specs=[hbm] * 8,
        out_specs=(hbm,) * 4,
        scratch_shapes=scratch,
        compiler_params=pltpu.CompilerParams(
            collective_id=0, has_side_effects=True, vmem_limit_bytes=62 * 1024 * 1024
        ),
    )(
        queries,
        positive.reshape(1, NQ),
        items,
        item_counts.reshape(1, NI),
        neg_counts.reshape(1, NN),
        neg_owner.reshape(1, NN),
        neg_row.reshape(1, NN),
        cache,
    )

    def whole(*shape):
        return pl.BlockSpec(shape, lambda r: (0,) * len(shape))

    def chunks(shape):
        return pl.BlockSpec((PB,) + shape[1:], lambda r: (r, 0, 0, 0))

    loss, query_grad, item_grad, cache_grad = pl.pallas_call(
        last,
        grid=(NZ // PB,),
        out_shape=(
            jax.ShapeDtypeStruct((NQ // 128, 128), F32),
            jax.ShapeDtypeStruct((CH, E), F32),
            jax.ShapeDtypeStruct((NI, E), F32),
            jax.ShapeDtypeStruct((ROWS, E), F32),
        ),
        in_specs=[whole(NQ // 128, 128), whole(CH, E), chunks(codes_i), chunks(codes_n)],
        out_specs=(
            whole(NQ // 128, 128),
            whole(CH, E),
            pl.BlockSpec((PB * CH, E), lambda r: (r, 0)),
            pl.BlockSpec((PB * CR, E), lambda r: (r, 0)),
        ),
        compiler_params=pltpu.CompilerParams(vmem_limit_bytes=62 * 1024 * 1024),
    )(loss, query_grad, item_codes, cache_codes)
    return loss.reshape(NQ), query_grad, item_grad, cache_grad


def solution(mesh):
    placed = (
        P("pb", None),
        P("pb"),
        P("col", None),
        P("col"),
        P("col", None),
        P("col", None),
        P("col"),
        P("col"),
    )
    return jax.shard_map(
        body,
        mesh=mesh,
        in_specs=placed,
        out_specs=(P("pb"), P(("pb", "col"), None), P("col", None), P("col", None)),
        check_vma=False,
    )
```

```python
import jax
import jax.numpy as jnp
from jax import lax
from jax.experimental import pallas as pl
from jax.experimental.pallas import tpu as pltpu
from jax.sharding import PartitionSpec as P

MESH = pl.DeviceIdType.MESH
F32 = jnp.float32
BF16 = jnp.bfloat16
I32 = jnp.int32
I16 = jnp.int16

E = 512
H = E // 2
NQ = 2048
QB = 256
NB = NQ // QB
NI = 512
NN = 512
NS = 1024
NC = 32
NZ = 8
CAP = 32
ROWS = 1024
CH = 64
INV_T = 20.0
PB = 4
W = E // 4
CR = ROWS // NZ
LN2 = 0.6931471805599453
SCALE2 = INV_T / LN2


def iota(shape, dim):
    return lax.broadcasted_iota(I32, shape, dim)


def onehot(cond):
    return jnp.where(cond, 1.0, 0.0).astype(BF16)


def dot_nn(a, b):
    return lax.dot_general(a, b, (((1,), (0,)), ((), ())), preferred_element_type=F32)


def dot_nt(a, b):
    return lax.dot_general(a, b, (((1,), (1,)), ((), ())), preferred_element_type=F32)


def dot_tn(a, b):
    return lax.dot_general(a, b, (((0,), (0,)), ((), ())), preferred_element_type=F32)


def halves(x):
    hi = x.astype(BF16)
    return hi, (x - hi.astype(F32)).astype(BF16)


def encode(x, group):
    rows, width = x.shape
    cube = x.reshape(rows // group, group, width)
    top = jnp.max(jnp.abs(cube), axis=0)
    expo = jnp.ceil(jnp.log2(jnp.maximum(top, 1e-30)))
    code = jnp.round(cube * jnp.exp2(14.99 - expo)[None])
    return code.reshape(rows, width).astype(I32).astype(I16), expo


def decode(code, expo):
    rows, width = code.shape
    group = expo.shape[0]
    cube = code.astype(I32).astype(F32).reshape(rows // group, group, width)
    return (cube * jnp.exp2(expo - 14.99)[None]).reshape(rows, width)


def to_i16(x):
    return x.astype(I32).astype(I16)


def from_i16(x):
    return x.astype(I32).astype(F32)


def unit(x):
    scale = jnp.sqrt(jnp.sum(x * x, axis=1, keepdims=True) + 1e-06)
    return x * (1.0 / scale), scale


def unit_back(grad, rows):
    direction, scale = unit(rows)
    return (grad - direction * jnp.sum(grad * direction, axis=1, keepdims=True)) / scale


def kernel(
    queries_hbm, positive_hbm, items_hbm, counts_i_hbm, counts_n_hbm, owner_hbm, row_hbm, cache_hbm,
    loss_out, query_out, item_codes, cache_codes,
    queries, positive, items, counts_i_ref, counts_n_ref, owner_ref, row_ref, cache, loss_buf, query_buf, msg, mrecv, cache_unit, scat, q_unit, cand_i, cand_n, shift_n,
    expo_i, expo_n, pos, tot, sums_i, factor_i, factor_n, weight_i, weight_n, part_i, part_n,
    slot_grad, slot_hi, slot_lo,
    send_i, recv_i, send_n, recv_n, ag_item, ag_cache, q_part, q_core, q_msg, q_recv,
    in_s, m_s, m_r, p_s, p_r, t_s, t_r, ri_s, ri_r, rn_s, rn_r, ai_s, ai_r, ac_s, ac_r, oi_s, oc_s,
    qc_s, qc_r, qd_s, qd_r, out_s,
):
    me = lax.axis_index("col")
    z = lax.axis_index("pb")
    core = me % 2
    chip = me // 2
    my_g = me // 4
    up = (z + 1) % NZ
    down = (z + NZ - 1) % NZ
    sibling = chip * 2 + 1 - core

    barrier = pltpu.get_barrier_semaphore()
    loads = [
        pltpu.make_async_copy(src, dst, in_s.at[i])
        for i, (src, dst) in enumerate(
            (
                (owner_hbm, owner_ref),
                (row_hbm, row_ref),
                (counts_n_hbm, counts_n_ref),
                (counts_i_hbm, counts_i_ref),
                (items_hbm, items),
                (positive_hbm, positive),
                (queries_hbm, queries),
                (cache_hbm, cache),
            )
        )
    ]
    for load in loads:
        load.start()

    @pl.loop(1, NC)
    def _(s):
        pl.semaphore_signal(barrier, inc=1, device_id={"col": (me + s) % NC}, device_id_type=MESH)

    for other in (up, down, (z + 2) % NZ, (z + NZ - 2) % NZ):
        pl.semaphore_signal(barrier, inc=1, device_id={"pb": other}, device_id_type=MESH)

    def remote(src, dst, send, recv, **where):
        return pltpu.make_async_remote_copy(
            src_ref=src, dst_ref=dst, send_sem=send, recv_sem=recv, device_id=where, device_id_type=MESH
        )

    def pair_row(ref, b):
        return jnp.concatenate([ref[pl.ds(2 * b, 1), :], ref[pl.ds(2 * b + 1, 1), :]], axis=1)

    def put_pair(ref, b, value):
        ref[pl.ds(2 * b, 1), :] = value[:, 0:128]
        ref[pl.ds(2 * b + 1, 1), :] = value[:, 128:]

    for load in loads[0:4]:
        load.wait()
    counts_i = counts_i_ref[...].astype(F32)
    counts_n = counts_n_ref[...].astype(F32)
    owner = owner_ref[...]
    row = row_ref[...]
    table = jnp.where(iota((NC, NN), 0) == owner, 1.0, 0.0)
    before = onehot(iota((NN, NN), 0) < iota((NN, NN), 1))
    earlier = dot_nn(table.astype(BF16), before)
    rank = jnp.sum(earlier * table, axis=0, keepdims=True).astype(I32)
    lane = onehot(iota((128, NN), 0) == CAP * (me % 4) + rank)
    named = jnp.concatenate(
        [table * (row >> 5).astype(F32), table * (row & 31).astype(F32), table * counts_n], axis=0
    )
    named = dot_nt(named.astype(BF16), lane)
    named = named[0:NC] * 32.0 + named[NC : 2 * NC] + named[2 * NC :] * ROWS
    total_i = jnp.sum(counts_i, axis=1, keepdims=True).reshape(1, 1, 1)
    total_n = jnp.sum(counts_n, axis=1, keepdims=True).reshape(1, 1, 1)
    line = iota((NC, 8, 128), 1)
    totals = jnp.where(line == (my_g + 1) % 8, total_i, jnp.where(line == (my_g + 2) % 8, total_n, 0.0))
    msg[...] = jnp.where(line == my_g, named.reshape(NC, 1, 128), totals)

    pl.semaphore_wait(barrier, NC + 3)

    def to_all(ref, send, recv, s):
        other = (me + s) % NC
        return remote(ref.at[me], ref.at[me], send.at[other], recv.at[me], col=other)

    def from_all(ref, send, recv, s):
        other = (me + s) % NC
        return remote(ref.at[me], ref.at[other], send.at[other], recv.at[other], col=other)

    @pl.loop(1, NC)
    def _(s):
        other = (me + s) % NC
        remote(msg.at[other], mrecv.at[me], m_s.at[other], m_r.at[me], col=other).start()

    mrecv[me] = msg[me]

    loads[4].wait()
    cand_i[...] = unit(items[...].astype(F32))[0].astype(BF16)
    same = iota((NI, NI), 0) == iota((NI, NI), 1)
    shift_i = jnp.log2(jnp.sum(jnp.where(same, counts_i, 0.0), axis=1, keepdims=True))
    first_item = me * NI
    loads[5].wait()
    loads[6].wait()

    @pl.loop(0, NB, unroll=4)
    def _(b):
        at = pl.ds(pl.multiple_of(b * QB, QB), QB)
        q_rows = unit(queries[at, :].astype(F32))[0].astype(BF16)
        q_unit[at, :] = q_rows
        logits = dot_nt(cand_i[...], q_rows) * SCALE2 - shift_i
        hit = positive[:, at] == first_item + iota((NI, QB), 0)
        expo = jnp.exp2(logits)
        expo_i[:, at] = expo
        put_pair(sums_i, b, jnp.sum(expo, axis=0, keepdims=True))
        put_pair(pos.at[me], b, jnp.sum(jnp.where(hit, logits, 0.0), axis=0, keepdims=True))

    loads[7].wait()

    @pl.loop(0, ROWS // QB)
    def _(b):
        at = pl.ds(pl.multiple_of(b * QB, QB), QB)
        cache_unit[at, :] = unit(cache[at, :].astype(F32))[0].astype(BF16)

    @pl.loop(1, NC)
    def _(s):
        other = (me + s) % NC
        remote(msg.at[other], mrecv.at[other], m_s.at[other], m_r.at[other], col=other).wait()

    line = iota((8, 128), 0)
    asked = jnp.zeros((8, 128), F32)
    sum_i = jnp.zeros((8, 128), F32)
    sum_n = jnp.zeros((8, 128), F32)
    for g in range(8):
        four = (mrecv[4 * g] + mrecv[4 * g + 1]) + (mrecv[4 * g + 2] + mrecv[4 * g + 3])
        asked = jnp.where(line == g, four, asked)
        sum_i = sum_i + jnp.where(line == (g + 1) % 8, four, 0.0)
        sum_n = sum_n + jnp.where(line == (g + 2) % 8, four, 0.0)
    total_i = jnp.sum(sum_i, axis=0, keepdims=True)[:, 0:1]
    total_n = jnp.sum(sum_n, axis=0, keepdims=True)[:, 0:1]

    def parts(value):
        count = jnp.floor(value * (1.0 / ROWS))
        return count, (value - count * ROWS).astype(I32)

    by_slot = jnp.concatenate([asked, jnp.zeros((120, 128), F32)], axis=0).T
    for half in range(2):
        picks = []
        for g in range(4 * half, 4 * half + 4):
            count, wanted = parts(by_slot[:, g : g + 1])
            shift_n[g * 128 : (g + 1) * 128, :] = jnp.where(
                count > 0.5, jnp.log2(jnp.maximum(count, 1.0)), 1e30
            )
            picks.append(onehot(iota((128, ROWS), 1) == wanted))
        picked = dot_nn(jnp.concatenate(picks, axis=0), cache_unit[...])
        cand_n[half * 512 : (half + 1) * 512, :] = picked.astype(BF16)

    def tot_copy(half, s, mine):
        other = (me + s) % NC
        slot = me if mine else other
        return remote(
            tot.at[half, me], tot.at[half, slot], t_s.at[half, other], t_r.at[half, slot], col=other
        )

    def scores_n(half):
        @pl.loop(half * NB // 2, (half + 1) * NB // 2, unroll=4)
        def _(b):
            at = pl.ds(pl.multiple_of(b * QB, QB), QB)
            expo = jnp.exp2(dot_nt(cand_n[...], q_unit[at, :]) * SCALE2 - shift_n[...])
            expo_n[:, at] = expo
            sum_n = total_n * jnp.sum(expo, axis=0, keepdims=True)
            put_pair(tot.at[half, me], b - half * (NB // 2), total_i * pair_row(sums_i, b) + sum_n)

        @pl.loop(1, NC)
        def _(s):
            tot_copy(half, s, True).start()

    scores_n(0)
    scores_n(1)

    @pl.loop(1, NC)
    def _(s):
        to_all(pos, p_s, p_r, s).start()

    slots = parts(asked)[1]
    for g in range(8):
        scat[:, g * 128 : (g + 1) * 128] = onehot(iota((ROWS, 128), 0) == slots[g : g + 1, :])

    def sums_in(half):
        @pl.loop(1, NC)
        def _(s):
            tot_copy(half, s, False).wait()

        total = jnp.sum(tot[half], axis=0)
        factor_i[half * 8 : (half + 1) * 8] = total_i / total
        factor_n[half * 8 : (half + 1) * 8] = total_n / total
        loss_buf[half * 8 : (half + 1) * 8] = jnp.log(total)

    def factors(ref, half):
        return jnp.concatenate([ref[half * 8 + k : half * 8 + k + 1, :] for k in range(8)], axis=1)

    def grad_i(half):
        at = pl.ds(half * (NQ // 2), NQ // 2)
        factor = factors(factor_i, half)
        for b in range(2):
            rows = slice(b * (NI // 2), (b + 1) * (NI // 2))
            hit = positive[:, at] == first_item + b * (NI // 2) + iota((NI // 2, NQ // 2), 0)
            weights = (expo_i[rows, at] * factor - jnp.where(hit, 1.0, 0.0)).astype(BF16)
            weight_i[rows, at] = weights
            grad = dot_nn(weights, q_unit[at, :]) * INV_T
            for k in range(4):
                to = (k // 2, slice(b * (NZ // 2), (b + 1) * (NZ // 2)), slice((k % 2) * CH, (k % 2 + 1) * CH))
                piece = grad[:, k * W : (k + 1) * W].reshape(NZ // 2, CH, W)
                part_i[to] = piece if half == 0 else part_i[to] + piece

    def grad_n(half):
        at = pl.ds(half * (NQ // 2), NQ // 2)
        factor = factors(factor_n, half)
        for b in range(2):
            rows = slice(b * (NS // 2), (b + 1) * (NS // 2))
            weights = (expo_n[rows, at] * factor).astype(BF16)
            weight_n[rows, at] = weights
            grad = dot_nn(weights, q_unit[at, :]) * INV_T
            if half == 0:
                slot_grad[rows, :] = grad
            else:
                hi, lo = halves(slot_grad[rows, :] + grad)
                slot_hi[rows, :] = hi
                slot_lo[rows, :] = lo

    def ring_peer(d):
        return up if d == 0 else down

    def ring_chunk(d, t):
        return (z + 4 - t) % NZ if d == 0 else (z + 4 + t) % NZ

    def streams(n, d):
        mine = [(k, 4) for k in range(n) if 2 * k // n == d]
        return mine + [(k, 3) for k in range(n) if 2 * k // n != d]

    def both_ways(n):
        for one, two in zip(streams(n, 0), streams(n, 1)):
            yield (0,) + one
            yield (1,) + two

    def pack(ref, chunk):
        code, e = encode(chunk, 16)
        ref[0:CR] = code
        ref[CR:] = to_i16(e)

    def unpack(ref):
        return decode(ref[0:CR], from_i16(ref[CR:]))

    def pack_two(ref, chunk):
        code, e = encode(chunk[0:CH], 8)
        code2, e2 = encode(chunk[CH:], 8)
        ref[0:CH] = code
        ref[CH : 2 * CH] = code2
        ref[2 * CH :] = to_i16(jnp.concatenate([e, e2], axis=0))

    def unpack_two(ref):
        e = from_i16(ref[2 * CH :])
        return jnp.concatenate([decode(ref[0:CH], e[0:8]), decode(ref[CH : 2 * CH], e[8:])], axis=0)

    def ring_copy(kind, d, t, k):
        _, send, recv, s, r = kind[:5]
        return remote(send.at[d, t, k], recv.at[d, t, k], s.at[d, t, k], r.at[d, t, k], pb=ring_peer(d))

    def ring_first(kind, t):
        part, send, _, _, _, n, put, _ = kind
        for d, k, steps in both_ways(n):
            if steps + t == 4:
                put(send.at[d, t, k], part[k, ring_chunk(d, t)])
                ring_copy(kind, d, t, k).start()

    def ring_step(kind, t):
        part, send, recv, _, _, n, put, get = kind
        for d, k, steps in both_ways(n):
            if steps + t > 4:
                ring_copy(kind, d, t - 1, k).wait()
                put(send.at[d, t, k], part[k, ring_chunk(d, t)] + get(recv.at[d, t - 1, k]))
                ring_copy(kind, d, t, k).start()

    def ring_last(kind):
        part, _, recv, _, _, n, _, get = kind
        own = [part[k, z] for k in range(n)]
        for d, k, _ in both_ways(n):
            ring_copy(kind, d, 3, k).wait()
            own[k] = own[k] + get(recv.at[d, 3, k])
        return own

    kind_i = (part_i, send_i, recv_i, ri_s, ri_r, 2, pack_two, unpack_two)
    kind_n = (part_n, send_n, recv_n, rn_s, rn_r, 4, pack, unpack)

    def by_row(first, count):
        at = pl.ds(pl.multiple_of(first * CR, CR), count * CR)
        grad = dot_nn(scat[at, :], slot_hi[...]) + dot_nn(scat[at, :], slot_lo[...])
        for k in range(4):
            part_n[k, pl.ds(first, count)] = grad[:, k * W : (k + 1) * W].reshape(count, CR, W)

    def q_which(i):
        return (chip // 2 + i) % NB

    def q_copy(i):
        two = pl.ds(q_which(i) * 2, 2)
        return remote(q_part.at[two, 1 - core], q_core.at[two], qc_s.at[i], qc_r.at[i], col=sibling)

    def q_block(i):
        b = q_which(i)
        at = pl.ds(pl.multiple_of(b * QB, QB), QB)
        grad = dot_tn(weight_i[:, at], cand_i[...]) + dot_tn(weight_n[:, at], cand_n[...])
        q_part[pl.ds(b * 2, 2)] = (grad * INV_T).reshape(2, 2, CH, E)
        q_copy(i).start()

    def q_send(i):
        q_copy(i).wait()
        for j in range(2):
            c = q_which(i) * 2 + j
            grad = q_part[c, core] + q_core[c]
            pack_two(q_msg.at[c], jnp.concatenate([grad[:, :H], grad[:, H:]], axis=0))

            @pl.when(c != chip)
            def _():
                remote(q_msg.at[c], q_recv.at[chip], qd_s.at[c], qd_r.at[chip], col=c * 2 + core).start()

            @pl.when(c == chip)
            def _():
                q_recv[chip] = q_msg[c]

    def out_copy(kind, p, k):
        ref, _, _, out, sem, _ = kind
        return pltpu.make_async_copy(ref.at[p, k], out.at[p, k], sem.at[p, k])

    def behind(d, s):
        return (z + 2 * NZ - s) % NZ if d == 0 else (z + s) % NZ

    def gather_copy(kind, d, s, k):
        ref, send, recv = kind[:3]
        ref = ref.at[behind(d, min(s, 2)), k]
        return remote(ref, ref, send.at[d, s, k], recv.at[d, s, k], pb=behind(1 - d, 1 if s < 3 else 2))

    def gather_first(kind, k):
        for d in range(2):
            gather_copy(kind, d, 0, k).start()
        out_copy(kind, z, k).start()

    def gather_wait(kind, d, s, k):
        gather_copy(kind, d, s, k).wait()
        out_copy(kind, behind(d, s + 1), k).start()

    def gather_step(kind, s):
        for d, k, steps in both_ways(kind[5]):
            gather_wait(kind, d, s - 1, k)
            for last in range(s, steps if s == 2 else s + 1):
                gather_copy(kind, d, last, k).start()

    def gather_last(kind):
        for s in (2, 3):
            for d, k, steps in both_ways(kind[5]):
                if s < steps:
                    gather_wait(kind, d, s, k)

    out_i = (ag_item, ai_s, ai_r, item_codes, oi_s, 2)
    out_n = (ag_cache, ac_s, ac_r, cache_codes, oc_s, 4)

    sums_in(0)
    grad_n(0)
    sums_in(1)
    grad_n(1)
    pair = ((z + 4) % NZ) // 2
    by_row((z + 4) % NZ, 1)
    ring_first(kind_n, 0)
    grad_i(0)
    grad_i(1)
    ring_first(kind_i, 0)
    ring_first(kind_i, 1)
    by_row(2 * pair + 1 - z % 2, 1)
    by_row(2 * ((pair + 3) % 4), 2)
    by_row(2 * ((pair + 1) % 4), 2)
    ring_first(kind_n, 1)
    ring_step(kind_n, 1)
    by_row(2 * ((pair + 2) % 4), 2)
    ring_step(kind_i, 1)
    q_block(0)
    q_block(1)
    q_block(2)
    ring_step(kind_n, 2)
    ring_step(kind_i, 2)
    q_block(3)
    q_block(4)
    q_send(0)
    ring_step(kind_n, 3)
    ring_step(kind_i, 3)
    q_block(5)
    q_block(6)
    q_block(7)
    q_send(1)

    own = jnp.concatenate(ring_last(kind_n), axis=1)
    grad = unit_back(own, cache[pl.ds(pl.multiple_of(z * CR, CR), CR), :].astype(F32))
    for k in range(4):
        pack(ag_cache.at[z, k], grad[:, k * W : (k + 1) * W])
        gather_first(out_n, k)

    own = ring_last(kind_i)
    own = jnp.concatenate([own[0][0:CH], own[0][CH:], own[1][0:CH], own[1][CH:]], axis=1)
    grad = unit_back(own, items[pl.ds(pl.multiple_of(z * CH, CH), CH), :].astype(F32))
    for h in range(2):
        left, right = grad[:, 2 * h * W : (2 * h + 1) * W], grad[:, (2 * h + 1) * W : (2 * h + 2) * W]
        pack_two(ag_item.at[z, h], jnp.concatenate([left, right], axis=0))
        gather_first(out_i, h)

    q_send(2)
    q_send(3)
    q_send(4)
    gather_step(out_n, 1)
    gather_step(out_i, 1)
    q_send(5)
    q_send(6)
    q_send(7)
    gather_step(out_n, 2)
    gather_step(out_i, 2)

    @pl.loop(1, NC)
    def _(s):
        from_all(pos, p_s, p_r, s).wait()

    loss_buf[...] = loss_buf[...] - (jnp.sum(pos[...], axis=0) * LN2 + jnp.log(total_i))
    loss_copy = pltpu.make_async_copy(loss_buf, loss_out, out_s.at[0])
    loss_copy.start()

    @pl.loop(1, NC // 2)
    def _(s):
        other = (chip + s) % (NC // 2)
        remote(q_msg.at[other], q_recv.at[other], qd_s.at[other], qd_r.at[other], col=other * 2 + core).wait()

    q_grad = unpack_two(q_recv.at[0])
    for c in range(1, NC // 2):
        q_grad = q_grad + unpack_two(q_recv.at[c])
    q_grad = jnp.concatenate([q_grad[0:CH], q_grad[CH:]], axis=1)
    query_buf[...] = unit_back(q_grad, queries[pl.ds(pl.multiple_of(me * CH, CH), CH), :].astype(F32))
    query_copy = pltpu.make_async_copy(query_buf, query_out, out_s.at[1])
    query_copy.start()

    gather_last(out_n)
    gather_last(out_i)

    @pl.loop(0, NZ)
    def _(p):
        for kind in (out_i, out_n):
            for k in range(kind[5]):
                out_copy(kind, p, k).wait()

    loss_copy.wait()
    query_copy.wait()


def last(loss, query, item_codes, cache_codes, loss_out, query_out, item_out, cache_out):
    for p in range(PB):
        for k in range(4):
            columns = slice(k * W, (k + 1) * W)
            part = k % 2
            e = from_i16(item_codes[p, k // 2, CR:])[8 * part : 8 * part + 8]
            item_out[p * CH : (p + 1) * CH, columns] = decode(item_codes[p, k // 2, part * CH : part * CH + CH], e)
            cache_out[p * CR : (p + 1) * CR, columns] = decode(
                cache_codes[p, k, 0:CR], from_i16(cache_codes[p, k, CR:])
            )

    @pl.when(pl.program_id(0) == 0)
    def _():
        loss_out[...] = loss[...]
        query_out[...] = query[...]


def body(queries, positive, items, item_counts, cache, neg_owner, neg_row, neg_counts):
    hbm = pl.BlockSpec(memory_space=pl.ANY)
    dma = pltpu.SemaphoreType.DMA
    codes_i = (NZ, 2, CR + 16, W)
    codes_n = (NZ, 4, CR + 16, W)
    ring_i = (2, 4, 2, CR + 16, W)
    ring_n = (2, 4, 4, CR + 16, W)
    scratch = [
        pltpu.VMEM((NQ, E), BF16),
        pltpu.VMEM((1, NQ), I32),
        pltpu.VMEM((NI, E), BF16),
        pltpu.VMEM((1, NI), I32),
        pltpu.VMEM((1, NN), I32),
        pltpu.VMEM((1, NN), I32),
        pltpu.VMEM((1, NN), I32),
        pltpu.VMEM((ROWS, E), BF16),
        pltpu.VMEM((NQ // 128, 128), F32),
        pltpu.VMEM((CH, E), F32),
        pltpu.VMEM((NC, 8, 128), F32),
        pltpu.VMEM((NC, 8, 128), F32),
        pltpu.VMEM((ROWS, E), BF16),
        pltpu.VMEM((ROWS, NS), BF16),
        pltpu.VMEM((NQ, E), BF16),
        pltpu.VMEM((NI, E), BF16),
        pltpu.VMEM((NS, E), BF16),
        pltpu.VMEM((NS, 1), F32),
        pltpu.VMEM((NI, NQ), F32),
        pltpu.VMEM((NS, NQ), F32),
        pltpu.VMEM((NC, NQ // 128, 128), F32),
        pltpu.VMEM((2, NC, NQ // 256, 128), F32),
        pltpu.VMEM((NQ // 128, 128), F32),
        pltpu.VMEM((NQ // 128, 128), F32),
        pltpu.VMEM((NQ // 128, 128), F32),
        pltpu.VMEM((NI, NQ), BF16),
        pltpu.VMEM((NS, NQ), BF16),
        pltpu.VMEM((2, NZ, 2 * CH, W), F32),
        pltpu.VMEM((4, NZ, CR, W), F32),
        pltpu.VMEM((NS, E), F32),
        pltpu.VMEM((NS, E), BF16),
        pltpu.VMEM((NS, E), BF16),
        pltpu.VMEM(ring_i, I16),
        pltpu.VMEM(ring_i, I16),
        pltpu.VMEM(ring_n, I16),
        pltpu.VMEM(ring_n, I16),
        pltpu.VMEM(codes_i, I16),
        pltpu.VMEM(codes_n, I16),
        pltpu.VMEM((NC // 2, 2, CH, E), F32),
        pltpu.VMEM((NC // 2, CH, E), F32),
        pltpu.VMEM((NC // 2, 2 * CH + 16, H), I16),
        pltpu.VMEM((NC // 2, 2 * CH + 16, H), I16),
        dma((8,)),
        dma((NC,)), dma((NC,)),
        dma((NC,)), dma((NC,)),
        dma((2, NC)), dma((2, NC)),
        dma((2, 4, 2)), dma((2, 4, 2)),
        dma((2, 4, 4)), dma((2, 4, 4)),
        dma((2, 4, 2)), dma((2, 4, 2)),
        dma((2, 4, 4)), dma((2, 4, 4)),
        dma((NZ, 2)), dma((NZ, 4)),
        dma((NB,)), dma((NB,)),
        dma((NC // 2,)), dma((NC // 2,)),
        dma((2,)),
    ]
    loss, query_grad, item_codes, cache_codes = pl.pallas_call(
        kernel,
        out_shape=(
            jax.ShapeDtypeStruct((NQ // 128, 128), F32),
            jax.ShapeDtypeStruct((CH, E), F32),
            jax.ShapeDtypeStruct(codes_i, I16),
            jax.ShapeDtypeStruct(codes_n, I16),
        ),
        in_specs=[hbm] * 8,
        out_specs=(hbm,) * 4,
        scratch_shapes=scratch,
        compiler_params=pltpu.CompilerParams(
            collective_id=0, has_side_effects=True, vmem_limit_bytes=62 * 1024 * 1024
        ),
    )(
        queries,
        positive.reshape(1, NQ),
        items,
        item_counts.reshape(1, NI),
        neg_counts.reshape(1, NN),
        neg_owner.reshape(1, NN),
        neg_row.reshape(1, NN),
        cache,
    )

    def whole(*shape):
        return pl.BlockSpec(shape, lambda r: (0,) * len(shape))

    def chunks(shape):
        return pl.BlockSpec((PB,) + shape[1:], lambda r: (r, 0, 0, 0))

    loss, query_grad, item_grad, cache_grad = pl.pallas_call(
        last,
        grid=(NZ // PB,),
        out_shape=(
            jax.ShapeDtypeStruct((NQ // 128, 128), F32),
            jax.ShapeDtypeStruct((CH, E), F32),
            jax.ShapeDtypeStruct((NI, E), F32),
            jax.ShapeDtypeStruct((ROWS, E), F32),
        ),
        in_specs=[whole(NQ // 128, 128), whole(CH, E), chunks(codes_i), chunks(codes_n)],
        out_specs=(
            whole(NQ // 128, 128),
            whole(CH, E),
            pl.BlockSpec((PB * CH, E), lambda r: (r, 0)),
            pl.BlockSpec((PB * CR, E), lambda r: (r, 0)),
        ),
        compiler_params=pltpu.CompilerParams(vmem_limit_bytes=62 * 1024 * 1024),
    )(loss, query_grad, item_codes, cache_codes)
    return loss.reshape(NQ), query_grad, item_grad, cache_grad


def solution(mesh):
    placed = (
        P("pb", None),
        P("pb"),
        P("col", None),
        P("col"),
        P("col", None),
        P("col", None),
        P("col"),
        P("col"),
    )
    return jax.shard_map(
        body,
        mesh=mesh,
        in_specs=placed,
        out_specs=(P("pb"), P(("pb", "col"), None), P("col", None), P("col", None)),
        check_vma=False,
    )
```

```python
import jax
import jax.numpy as jnp
from jax import lax
from jax.experimental import pallas as pl
from jax.experimental.pallas import tpu as pltpu
from jax.sharding import PartitionSpec as P

MESH = pl.DeviceIdType.MESH
F32 = jnp.float32
BF16 = jnp.bfloat16
I32 = jnp.int32
I16 = jnp.int16

E = 512
H = E // 2
NQ = 2048
QB = 256
NB = NQ // QB
NI = 512
NN = 512
NS = 1024
NC = 32
NZ = 8
CAP = 32
ROWS = 1024
CH = 64
INV_T = 20.0
PB = 4
W = E // 4
CR = ROWS // NZ
LN2 = 0.6931471805599453
SCALE2 = INV_T / LN2


def iota(shape, dim):
    return lax.broadcasted_iota(I32, shape, dim)


def onehot(cond):
    return jnp.where(cond, 1.0, 0.0).astype(BF16)


def dot_nn(a, b):
    return lax.dot_general(a, b, (((1,), (0,)), ((), ())), preferred_element_type=F32)


def dot_nt(a, b):
    return lax.dot_general(a, b, (((1,), (1,)), ((), ())), preferred_element_type=F32)


def dot_tn(a, b):
    return lax.dot_general(a, b, (((0,), (0,)), ((), ())), preferred_element_type=F32)


def halves(x):
    hi = x.astype(BF16)
    return hi, (x - hi.astype(F32)).astype(BF16)


def encode(x, group):
    rows, width = x.shape
    cube = x.reshape(rows // group, group, width)
    top = jnp.max(jnp.abs(cube), axis=0)
    expo = jnp.ceil(jnp.log2(jnp.maximum(top, 1e-30)))
    code = jnp.round(cube * jnp.exp2(14.99 - expo)[None])
    return code.reshape(rows, width).astype(I32).astype(I16), expo


def encode4(x):
    rows, width = x.shape
    cube = x.reshape(rows // 8, 8, width)
    top = jnp.max(jnp.abs(cube), axis=0)
    top = jnp.maximum(top[0:4], top[4:8])
    expo = jnp.ceil(jnp.log2(jnp.maximum(top, 1e-30)))
    scale = jnp.exp2(14.99 - jnp.concatenate([expo, expo], axis=0))
    code = jnp.round(cube * scale[None])
    return code.reshape(rows, width).astype(I32).astype(I16), expo


def decode(code, expo):
    rows, width = code.shape
    group = expo.shape[0]
    cube = code.astype(I32).astype(F32).reshape(rows // group, group, width)
    return (cube * jnp.exp2(expo - 14.99)[None]).reshape(rows, width)


def to_i16(x):
    return x.astype(I32).astype(I16)


def from_i16(x):
    return x.astype(I32).astype(F32)


def unit(x):
    scale = jnp.sqrt(jnp.sum(x * x, axis=1, keepdims=True) + 1e-06)
    return x * (1.0 / scale), scale


def unit_back(grad, rows):
    direction, scale = unit(rows)
    return (grad - direction * jnp.sum(grad * direction, axis=1, keepdims=True)) / scale


def kernel(
    queries_hbm, positive_hbm, items_hbm, counts_i_hbm, counts_n_hbm, owner_hbm, row_hbm, cache_hbm,
    loss_out, query_out, item_codes, cache_codes,
    queries, positive, items, counts_i_ref, counts_n_ref, owner_ref, row_ref, cache, loss_buf, query_buf, msg, mrecv, cache_unit, scat, q_unit, cand_i, cand_n, shift_n,
    expo_i, expo_n, pos, tot, sums_i, factor_i, factor_n, weight_i, weight_n, part_i, part_n,
    slot_grad, slot_hi, slot_lo,
    send_i, recv_i, send_n, recv_n, ag_item, ag_cache, q_part, q_core, q_msg, q_recv,
    in_s, m_s, m_r, p_s, p_r, t_s, t_r, ri_s, ri_r, rn_s, rn_r, ai_s, ai_r, ac_s, ac_r, oi_s, oc_s,
    qc_s, qc_r, qd_s, qd_r, out_s,
):
    me = lax.axis_index("col")
    z = lax.axis_index("pb")
    core = me % 2
    chip = me // 2
    my_g = me // 4
    up = (z + 1) % NZ
    down = (z + NZ - 1) % NZ
    sibling = chip * 2 + 1 - core

    barrier = pltpu.get_barrier_semaphore()
    loads = [
        pltpu.make_async_copy(src, dst, in_s.at[i])
        for i, (src, dst) in enumerate(
            (
                (owner_hbm, owner_ref),
                (row_hbm, row_ref),
                (counts_n_hbm, counts_n_ref),
                (counts_i_hbm, counts_i_ref),
                (items_hbm, items),
                (positive_hbm, positive),
                (queries_hbm, queries),
                (cache_hbm, cache),
            )
        )
    ]
    for load in loads:
        load.start()

    @pl.loop(1, NC)
    def _(s):
        pl.semaphore_signal(barrier, inc=1, device_id={"col": (me + s) % NC}, device_id_type=MESH)

    for other in (up, down):
        pl.semaphore_signal(barrier, inc=1, device_id={"pb": other}, device_id_type=MESH)

    def remote(src, dst, send, recv, **where):
        return pltpu.make_async_remote_copy(
            src_ref=src, dst_ref=dst, send_sem=send, recv_sem=recv, device_id=where, device_id_type=MESH
        )

    def pair_row(ref, b):
        return jnp.concatenate([ref[pl.ds(2 * b, 1), :], ref[pl.ds(2 * b + 1, 1), :]], axis=1)

    def put_pair(ref, b, value):
        ref[pl.ds(2 * b, 1), :] = value[:, 0:128]
        ref[pl.ds(2 * b + 1, 1), :] = value[:, 128:]

    for load in loads[0:4]:
        load.wait()
    counts_i = counts_i_ref[...].astype(F32)
    counts_n = counts_n_ref[...].astype(F32)
    owner = owner_ref[...]
    row = row_ref[...]
    table = jnp.where(iota((NC, NN), 0) == owner, 1.0, 0.0)
    before = onehot(iota((NN, NN), 0) < iota((NN, NN), 1))
    earlier = dot_nn(table.astype(BF16), before)
    rank = jnp.sum(earlier * table, axis=0, keepdims=True).astype(I32)
    lane = onehot(iota((128, NN), 0) == CAP * (me % 4) + rank)
    named = jnp.concatenate(
        [table * (row >> 5).astype(F32), table * (row & 31).astype(F32), table * counts_n], axis=0
    )
    named = dot_nt(named.astype(BF16), lane)
    named = named[0:NC] * 32.0 + named[NC : 2 * NC] + named[2 * NC :] * ROWS
    total_i = jnp.sum(counts_i, axis=1, keepdims=True).reshape(1, 1, 1)
    total_n = jnp.sum(counts_n, axis=1, keepdims=True).reshape(1, 1, 1)
    line = iota((NC, 8, 128), 1)
    totals = jnp.where(line == (my_g + 1) % 8, total_i, jnp.where(line == (my_g + 2) % 8, total_n, 0.0))
    msg[...] = jnp.where(line == my_g, named.reshape(NC, 1, 128), totals)

    pl.semaphore_wait(barrier, NC + 1)

    def to_all(ref, send, recv, s):
        other = (me + s) % NC
        return remote(ref.at[me], ref.at[me], send.at[other], recv.at[me], col=other)

    def from_all(ref, send, recv, s):
        other = (me + s) % NC
        return remote(ref.at[me], ref.at[other], send.at[other], recv.at[other], col=other)

    @pl.loop(1, NC)
    def _(s):
        other = (me + s) % NC
        remote(msg.at[other], mrecv.at[me], m_s.at[other], m_r.at[me], col=other).start()

    mrecv[me] = msg[me]

    loads[4].wait()
    cand_i[...] = unit(items[...].astype(F32))[0].astype(BF16)
    same = iota((NI, NI), 0) == iota((NI, NI), 1)
    shift_i = jnp.log2(jnp.sum(jnp.where(same, counts_i, 0.0), axis=1, keepdims=True))
    first_item = me * NI
    loads[5].wait()
    loads[6].wait()

    @pl.loop(0, NB, unroll=4)
    def _(b):
        at = pl.ds(pl.multiple_of(b * QB, QB), QB)
        q_rows = unit(queries[at, :].astype(F32))[0].astype(BF16)
        q_unit[at, :] = q_rows
        logits = dot_nt(cand_i[...], q_rows) * SCALE2 - shift_i
        hit = positive[:, at] == first_item + iota((NI, QB), 0)
        expo = jnp.exp2(logits)
        expo_i[:, at] = expo
        put_pair(sums_i, b, jnp.sum(expo, axis=0, keepdims=True))
        put_pair(pos.at[me], b, jnp.sum(jnp.where(hit, logits, 0.0), axis=0, keepdims=True))

    loads[7].wait()

    @pl.loop(0, ROWS // QB)
    def _(b):
        at = pl.ds(pl.multiple_of(b * QB, QB), QB)
        cache_unit[at, :] = unit(cache[at, :].astype(F32))[0].astype(BF16)

    @pl.loop(1, NC)
    def _(s):
        other = (me + s) % NC
        remote(msg.at[other], mrecv.at[other], m_s.at[other], m_r.at[other], col=other).wait()

    line = iota((8, 128), 0)
    asked = jnp.zeros((8, 128), F32)
    sum_i = jnp.zeros((8, 128), F32)
    sum_n = jnp.zeros((8, 128), F32)
    for g in range(8):
        four = (mrecv[4 * g] + mrecv[4 * g + 1]) + (mrecv[4 * g + 2] + mrecv[4 * g + 3])
        asked = jnp.where(line == g, four, asked)
        sum_i = sum_i + jnp.where(line == (g + 1) % 8, four, 0.0)
        sum_n = sum_n + jnp.where(line == (g + 2) % 8, four, 0.0)
    total_i = jnp.sum(sum_i, axis=0, keepdims=True)[:, 0:1]
    total_n = jnp.sum(sum_n, axis=0, keepdims=True)[:, 0:1]

    def parts(value):
        count = jnp.floor(value * (1.0 / ROWS))
        return count, (value - count * ROWS).astype(I32)

    by_slot = jnp.concatenate([asked, jnp.zeros((120, 128), F32)], axis=0).T
    for half in range(2):
        picks = []
        for g in range(4 * half, 4 * half + 4):
            count, wanted = parts(by_slot[:, g : g + 1])
            shift_n[g * 128 : (g + 1) * 128, :] = jnp.where(
                count > 0.5, jnp.log2(jnp.maximum(count, 1.0)), 1e30
            )
            picks.append(onehot(iota((128, ROWS), 1) == wanted))
        picked = dot_nn(jnp.concatenate(picks, axis=0), cache_unit[...])
        cand_n[half * 512 : (half + 1) * 512, :] = picked.astype(BF16)

    def tot_copy(half, s, mine):
        other = (me + s) % NC
        slot = me if mine else other
        return remote(
            tot.at[half, me], tot.at[half, slot], t_s.at[half, other], t_r.at[half, slot], col=other
        )

    def scores_n(half):
        @pl.loop(half * NB // 2, (half + 1) * NB // 2, unroll=4)
        def _(b):
            at = pl.ds(pl.multiple_of(b * QB, QB), QB)
            expo = jnp.exp2(dot_nt(cand_n[...], q_unit[at, :]) * SCALE2 - shift_n[...])
            expo_n[:, at] = expo
            sum_n = total_n * jnp.sum(expo, axis=0, keepdims=True)
            put_pair(tot.at[half, me], b - half * (NB // 2), total_i * pair_row(sums_i, b) + sum_n)

        @pl.loop(1, NC)
        def _(s):
            tot_copy(half, s, True).start()

    scores_n(0)
    scores_n(1)

    @pl.loop(1, NC)
    def _(s):
        to_all(pos, p_s, p_r, s).start()

    slots = parts(asked)[1]
    for g in range(8):
        scat[:, g * 128 : (g + 1) * 128] = onehot(iota((ROWS, 128), 0) == slots[g : g + 1, :])

    def sums_in(half):
        @pl.loop(1, NC)
        def _(s):
            tot_copy(half, s, False).wait()

        total = jnp.sum(tot[half], axis=0)
        factor_i[half * 8 : (half + 1) * 8] = total_i / total
        factor_n[half * 8 : (half + 1) * 8] = total_n / total
        loss_buf[half * 8 : (half + 1) * 8] = jnp.log(total)

    def factors(ref, half):
        return jnp.concatenate([ref[half * 8 + k : half * 8 + k + 1, :] for k in range(8)], axis=1)

    def grad_i(half):
        at = pl.ds(half * (NQ // 2), NQ // 2)
        factor = factors(factor_i, half)
        for b in range(2):
            rows = slice(b * (NI // 2), (b + 1) * (NI // 2))
            hit = positive[:, at] == first_item + b * (NI // 2) + iota((NI // 2, NQ // 2), 0)
            weights = (expo_i[rows, at] * factor - jnp.where(hit, 1.0, 0.0)).astype(BF16)
            weight_i[rows, at] = weights
            grad = dot_nn(weights, q_unit[at, :]) * INV_T
            for k in range(4):
                to = (k // 2, slice(b * (NZ // 2), (b + 1) * (NZ // 2)), slice((k % 2) * CH, (k % 2 + 1) * CH))
                piece = grad[:, k * W : (k + 1) * W].reshape(NZ // 2, CH, W)
                part_i[to] = piece if half == 0 else part_i[to] + piece

    def grad_n(half):
        at = pl.ds(half * (NQ // 2), NQ // 2)
        factor = factors(factor_n, half)
        for b in range(2):
            rows = slice(b * (NS // 2), (b + 1) * (NS // 2))
            weights = (expo_n[rows, at] * factor).astype(BF16)
            weight_n[rows, at] = weights
            grad = dot_nn(weights, q_unit[at, :]) * INV_T
            if half == 0:
                slot_grad[rows, :] = grad
            else:
                hi, lo = halves(slot_grad[rows, :] + grad)
                slot_hi[rows, :] = hi
                slot_lo[rows, :] = lo

    def ring_peer(d):
        return up if d == 0 else down

    def ring_chunk(d, t):
        return (z + 4 - t) % NZ if d == 0 else (z + 4 + t) % NZ

    def streams(n, d):
        mine = [(k, 4) for k in range(n) if 2 * k // n == d]
        return mine + [(k, 3) for k in range(n) if 2 * k // n != d]

    def both_ways(n):
        for one, two in zip(streams(n, 0), streams(n, 1)):
            yield (0,) + one
            yield (1,) + two

    def pack(ref, chunk):
        code, e = encode(chunk, 16)
        ref[0:CR] = code
        ref[CR:] = to_i16(e)

    def unpack(ref):
        return decode(ref[0:CR], from_i16(ref[CR:]))

    def pack_two(ref, chunk):
        code, e = encode(chunk[0:CH], 8)
        code2, e2 = encode(chunk[CH:], 8)
        ref[0:CH] = code
        ref[CH : 2 * CH] = code2
        ref[2 * CH :] = to_i16(jnp.concatenate([e, e2], axis=0))

    def unpack_two(ref):
        e = from_i16(ref[2 * CH :])
        return jnp.concatenate([decode(ref[0:CH], e[0:8]), decode(ref[CH : 2 * CH], e[8:])], axis=0)

    def ring_copy(kind, d, t, k):
        _, send, recv, s, r = kind[:5]
        return remote(send.at[d, t, k], recv.at[d, t, k], s.at[d, t, k], r.at[d, t, k], pb=ring_peer(d))

    def ring_first(kind, t):
        part, send, _, _, _, n, put, _ = kind
        for d, k, steps in both_ways(n):
            if steps + t == 4:
                put(send.at[d, t, k], part[k, ring_chunk(d, t)])
                ring_copy(kind, d, t, k).start()

    def ring_step(kind, t):
        part, send, recv, _, _, n, put, get = kind
        for d, k, steps in both_ways(n):
            if steps + t > 4:
                ring_copy(kind, d, t - 1, k).wait()
                put(send.at[d, t, k], part[k, ring_chunk(d, t)] + get(recv.at[d, t - 1, k]))
                ring_copy(kind, d, t, k).start()

    def ring_last(kind):
        part, _, recv, _, _, n, _, get = kind
        own = [part[k, z] for k in range(n)]
        for d, k, _ in both_ways(n):
            ring_copy(kind, d, 3, k).wait()
            own[k] = own[k] + get(recv.at[d, 3, k])
        return own

    kind_i = (part_i, send_i, recv_i, ri_s, ri_r, 2, pack_two, unpack_two)
    kind_n = (part_n, send_n, recv_n, rn_s, rn_r, 4, pack, unpack)

    def by_row(first, count):
        at = pl.ds(pl.multiple_of(first * CR, CR), count * CR)
        grad = dot_nn(scat[at, :], slot_hi[...]) + dot_nn(scat[at, :], slot_lo[...])
        for k in range(4):
            part_n[k, pl.ds(first, count)] = grad[:, k * W : (k + 1) * W].reshape(count, CR, W)

    def q_which(i):
        return (chip // 2 + i) % NB

    def q_copy(i):
        two = pl.ds(q_which(i) * 2, 2)
        return remote(q_part.at[two, 1 - core], q_core.at[two], qc_s.at[i], qc_r.at[i], col=sibling)

    def q_block(i):
        b = q_which(i)
        at = pl.ds(pl.multiple_of(b * QB, QB), QB)
        grad = dot_tn(weight_i[:, at], cand_i[...]) + dot_tn(weight_n[:, at], cand_n[...])
        q_part[pl.ds(b * 2, 2)] = (grad * INV_T).reshape(2, 2, CH, E)
        q_copy(i).start()

    def q_send(i):
        q_copy(i).wait()
        for j in range(2):
            c = q_which(i) * 2 + j
            grad = q_part[c, core] + q_core[c]
            pack_two(q_msg.at[c], jnp.concatenate([grad[:, :H], grad[:, H:]], axis=0))

            @pl.when(c != chip)
            def _():
                remote(q_msg.at[c], q_recv.at[chip], qd_s.at[c], qd_r.at[chip], col=c * 2 + core).start()

            @pl.when(c == chip)
            def _():
                q_recv[chip] = q_msg[c]

    def out_copy(kind, p, k):
        ref, _, _, out, sem, _ = kind
        return pltpu.make_async_copy(ref.at[p, k], out.at[p, k], sem.at[p, k])

    def behind(d, s):
        return (z + 2 * NZ - s) % NZ if d == 0 else (z + s) % NZ

    def gather_copy(kind, d, s, k):
        ref, send, recv = kind[:3]
        ref = ref.at[behind(d, s), k]
        return remote(ref, ref, send.at[d, s, k], recv.at[d, s, k], pb=ring_peer(d))

    def gather_first(kind, k):
        for d in range(2):
            gather_copy(kind, d, 0, k).start()
        out_copy(kind, z, k).start()

    def gather_wait(kind, d, s, k):
        gather_copy(kind, d, s, k).wait()
        out_copy(kind, behind(d, s + 1), k).start()

    def gather_step(kind, s):
        for d, k, steps in both_ways(kind[5]):
            if s < steps:
                gather_wait(kind, d, s - 1, k)
                gather_copy(kind, d, s, k).start()

    def gather_last(kind):
        for three in (3, 4):
            for d, k, steps in both_ways(kind[5]):
                if steps == three:
                    gather_wait(kind, d, steps - 1, k)

    out_i = (ag_item, ai_s, ai_r, item_codes, oi_s, 2)
    out_n = (ag_cache, ac_s, ac_r, cache_codes, oc_s, 4)

    sums_in(0)
    grad_n(0)
    sums_in(1)
    grad_n(1)
    pair = ((z + 4) % NZ) // 2
    by_row((z + 4) % NZ, 1)
    ring_first(kind_n, 0)
    grad_i(0)
    grad_i(1)
    ring_first(kind_i, 0)
    ring_first(kind_i, 1)
    by_row(2 * pair + 1 - z % 2, 1)
    by_row(2 * ((pair + 3) % 4), 2)
    by_row(2 * ((pair + 1) % 4), 2)
    ring_first(kind_n, 1)
    ring_step(kind_n, 1)
    by_row(2 * ((pair + 2) % 4), 2)
    ring_step(kind_i, 1)
    q_block(0)
    q_block(1)
    q_block(2)
    ring_step(kind_n, 2)
    ring_step(kind_i, 2)
    q_block(3)
    q_block(4)
    q_send(0)
    ring_step(kind_n, 3)
    ring_step(kind_i, 3)
    q_block(5)
    q_block(6)
    q_block(7)
    q_send(1)

    cache_e = []
    own = jnp.concatenate(ring_last(kind_n), axis=1)
    grad = unit_back(own, cache[pl.ds(pl.multiple_of(z * CR, CR), CR), :].astype(F32))
    for k in range(4):
        code, e = encode4(grad[:, k * W : (k + 1) * W])
        ag_cache[z, k] = code
        gather_first(out_n, k)
        cache_e.append(e)

    own = ring_last(kind_i)
    own = jnp.concatenate([own[0][0:CH], own[0][CH:], own[1][0:CH], own[1][CH:]], axis=1)
    grad = unit_back(own, items[pl.ds(pl.multiple_of(z * CH, CH), CH), :].astype(F32))
    for h in range(2):
        e = []
        for k in range(2):
            code, e_item = encode4(grad[:, (2 * h + k) * W : (2 * h + k + 1) * W])
            ag_item[z, h, k * CH : (k + 1) * CH] = code
            e.append(e_item)
        ag_item[z, h, CR:] = to_i16(jnp.concatenate(e + cache_e[2 * h : 2 * h + 2], axis=0))
        gather_first(out_i, h)

    q_send(2)
    q_send(3)
    q_send(4)
    gather_step(out_n, 1)
    gather_step(out_i, 1)
    q_send(5)
    q_send(6)
    q_send(7)
    gather_step(out_n, 2)
    gather_step(out_i, 2)

    @pl.loop(1, NC)
    def _(s):
        from_all(pos, p_s, p_r, s).wait()

    loss_buf[...] = loss_buf[...] - (jnp.sum(pos[...], axis=0) * LN2 + jnp.log(total_i))
    loss_copy = pltpu.make_async_copy(loss_buf, loss_out, out_s.at[0])
    loss_copy.start()
    gather_step(out_n, 3)
    gather_step(out_i, 3)

    @pl.loop(1, NC // 2)
    def _(s):
        other = (chip + s) % (NC // 2)
        remote(q_msg.at[other], q_recv.at[other], qd_s.at[other], qd_r.at[other], col=other * 2 + core).wait()

    q_grad = unpack_two(q_recv.at[0])
    for c in range(1, NC // 2):
        q_grad = q_grad + unpack_two(q_recv.at[c])
    q_grad = jnp.concatenate([q_grad[0:CH], q_grad[CH:]], axis=1)
    query_buf[...] = unit_back(q_grad, queries[pl.ds(pl.multiple_of(me * CH, CH), CH), :].astype(F32))
    query_copy = pltpu.make_async_copy(query_buf, query_out, out_s.at[1])
    query_copy.start()

    gather_last(out_n)
    gather_last(out_i)

    @pl.loop(0, NZ)
    def _(p):
        for kind in (out_i, out_n):
            for k in range(kind[5]):
                out_copy(kind, p, k).wait()

    loss_copy.wait()
    query_copy.wait()


def last(loss, query, item_codes, cache_codes, loss_out, query_out, item_out, cache_out):
    for p in range(PB):
        for k in range(4):
            columns = slice(k * W, (k + 1) * W)
            part = k % 2
            e = from_i16(item_codes[p, k // 2, CR:])
            e_item = e[4 * part : 4 * part + 4]
            e_cache = e[8 + 4 * part : 12 + 4 * part]
            code = item_codes[p, k // 2, part * CH : part * CH + CH]
            item_out[p * CH : (p + 1) * CH, columns] = decode(code, jnp.concatenate([e_item, e_item], axis=0))
            code = cache_codes[p, k]
            cache_out[p * CR : (p + 1) * CR, columns] = decode(code, jnp.concatenate([e_cache, e_cache], axis=0))

    @pl.when(pl.program_id(0) == 0)
    def _():
        loss_out[...] = loss[...]
        query_out[...] = query[...]


def body(queries, positive, items, item_counts, cache, neg_owner, neg_row, neg_counts):
    hbm = pl.BlockSpec(memory_space=pl.ANY)
    dma = pltpu.SemaphoreType.DMA
    codes_i = (NZ, 2, CR + 16, W)
    codes_n = (NZ, 4, CR, W)
    ring_i = (2, 4, 2, CR + 16, W)
    ring_n = (2, 4, 4, CR + 16, W)
    scratch = [
        pltpu.VMEM((NQ, E), BF16),
        pltpu.VMEM((1, NQ), I32),
        pltpu.VMEM((NI, E), BF16),
        pltpu.VMEM((1, NI), I32),
        pltpu.VMEM((1, NN), I32),
        pltpu.VMEM((1, NN), I32),
        pltpu.VMEM((1, NN), I32),
        pltpu.VMEM((ROWS, E), BF16),
        pltpu.VMEM((NQ // 128, 128), F32),
        pltpu.VMEM((CH, E), F32),
        pltpu.VMEM((NC, 8, 128), F32),
        pltpu.VMEM((NC, 8, 128), F32),
        pltpu.VMEM((ROWS, E), BF16),
        pltpu.VMEM((ROWS, NS), BF16),
        pltpu.VMEM((NQ, E), BF16),
        pltpu.VMEM((NI, E), BF16),
        pltpu.VMEM((NS, E), BF16),
        pltpu.VMEM((NS, 1), F32),
        pltpu.VMEM((NI, NQ), F32),
        pltpu.VMEM((NS, NQ), F32),
        pltpu.VMEM((NC, NQ // 128, 128), F32),
        pltpu.VMEM((2, NC, NQ // 256, 128), F32),
        pltpu.VMEM((NQ // 128, 128), F32),
        pltpu.VMEM((NQ // 128, 128), F32),
        pltpu.VMEM((NQ // 128, 128), F32),
        pltpu.VMEM((NI, NQ), BF16),
        pltpu.VMEM((NS, NQ), BF16),
        pltpu.VMEM((2, NZ, 2 * CH, W), F32),
        pltpu.VMEM((4, NZ, CR, W), F32),
        pltpu.VMEM((NS, E), F32),
        pltpu.VMEM((NS, E), BF16),
        pltpu.VMEM((NS, E), BF16),
        pltpu.VMEM(ring_i, I16),
        pltpu.VMEM(ring_i, I16),
        pltpu.VMEM(ring_n, I16),
        pltpu.VMEM(ring_n, I16),
        pltpu.VMEM(codes_i, I16),
        pltpu.VMEM(codes_n, I16),
        pltpu.VMEM((NC // 2, 2, CH, E), F32),
        pltpu.VMEM((NC // 2, CH, E), F32),
        pltpu.VMEM((NC // 2, 2 * CH + 16, H), I16),
        pltpu.VMEM((NC // 2, 2 * CH + 16, H), I16),
        dma((8,)),
        dma((NC,)), dma((NC,)),
        dma((NC,)), dma((NC,)),
        dma((2, NC)), dma((2, NC)),
        dma((2, 4, 2)), dma((2, 4, 2)),
        dma((2, 4, 4)), dma((2, 4, 4)),
        dma((2, 4, 2)), dma((2, 4, 2)),
        dma((2, 4, 4)), dma((2, 4, 4)),
        dma((NZ, 2)), dma((NZ, 4)),
        dma((NB,)), dma((NB,)),
        dma((NC // 2,)), dma((NC // 2,)),
        dma((2,)),
    ]
    loss, query_grad, item_codes, cache_codes = pl.pallas_call(
        kernel,
        out_shape=(
            jax.ShapeDtypeStruct((NQ // 128, 128), F32),
            jax.ShapeDtypeStruct((CH, E), F32),
            jax.ShapeDtypeStruct(codes_i, I16),
            jax.ShapeDtypeStruct(codes_n, I16),
        ),
        in_specs=[hbm] * 8,
        out_specs=(hbm,) * 4,
        scratch_shapes=scratch,
        compiler_params=pltpu.CompilerParams(
            collective_id=0, has_side_effects=True, vmem_limit_bytes=62 * 1024 * 1024
        ),
    )(
        queries,
        positive.reshape(1, NQ),
        items,
        item_counts.reshape(1, NI),
        neg_counts.reshape(1, NN),
        neg_owner.reshape(1, NN),
        neg_row.reshape(1, NN),
        cache,
    )

    def whole(*shape):
        return pl.BlockSpec(shape, lambda r: (0,) * len(shape))

    def chunks(shape):
        return pl.BlockSpec((PB,) + shape[1:], lambda r: (r, 0, 0, 0))

    loss, query_grad, item_grad, cache_grad = pl.pallas_call(
        last,
        grid=(NZ // PB,),
        out_shape=(
            jax.ShapeDtypeStruct((NQ // 128, 128), F32),
            jax.ShapeDtypeStruct((CH, E), F32),
            jax.ShapeDtypeStruct((NI, E), F32),
            jax.ShapeDtypeStruct((ROWS, E), F32),
        ),
        in_specs=[whole(NQ // 128, 128), whole(CH, E), chunks(codes_i), chunks(codes_n)],
        out_specs=(
            whole(NQ // 128, 128),
            whole(CH, E),
            pl.BlockSpec((PB * CH, E), lambda r: (r, 0)),
            pl.BlockSpec((PB * CR, E), lambda r: (r, 0)),
        ),
        compiler_params=pltpu.CompilerParams(vmem_limit_bytes=62 * 1024 * 1024),
    )(loss, query_grad, item_codes, cache_codes)
    return loss.reshape(NQ), query_grad, item_grad, cache_grad


def solution(mesh):
    placed = (
        P("pb", None),
        P("pb"),
        P("col", None),
        P("col"),
        P("col", None),
        P("col", None),
        P("col"),
        P("col"),
    )
    return jax.shard_map(
        body,
        mesh=mesh,
        in_specs=placed,
        out_specs=(P("pb"), P(("pb", "col"), None), P("col", None), P("col", None)),
        check_vma=False,
    )
```

```python
import jax
import jax.numpy as jnp
from jax import lax
from jax.experimental import pallas as pl
from jax.experimental.pallas import tpu as pltpu
from jax.sharding import PartitionSpec as P

MESH = pl.DeviceIdType.MESH
F32 = jnp.float32
BF16 = jnp.bfloat16
I32 = jnp.int32
I16 = jnp.int16

E = 512
H = E // 2
NQ = 2048
QB = 256
NB = NQ // QB
NI = 512
NN = 512
NS = 1024
NC = 32
NZ = 8
CAP = 32
ROWS = 1024
CH = 64
INV_T = 20.0
PB = 4
W = E // 4
CR = ROWS // NZ
LN2 = 0.6931471805599453
SCALE2 = INV_T / LN2


def iota(shape, dim):
    return lax.broadcasted_iota(I32, shape, dim)


def onehot(cond):
    return jnp.where(cond, 1.0, 0.0).astype(BF16)


def dot_nn(a, b):
    return lax.dot_general(a, b, (((1,), (0,)), ((), ())), preferred_element_type=F32)


def dot_nt(a, b):
    return lax.dot_general(a, b, (((1,), (1,)), ((), ())), preferred_element_type=F32)


def dot_tn(a, b):
    return lax.dot_general(a, b, (((0,), (0,)), ((), ())), preferred_element_type=F32)


def halves(x):
    hi = x.astype(BF16)
    return hi, (x - hi.astype(F32)).astype(BF16)


def encode(x, group):
    rows, width = x.shape
    cube = x.reshape(rows // group, group, width)
    top = jnp.max(jnp.abs(cube), axis=0)
    expo = jnp.ceil(jnp.log2(jnp.maximum(top, 1e-30)))
    code = jnp.round(cube * jnp.exp2(14.99 - expo)[None])
    return code.reshape(rows, width).astype(I32).astype(I16), expo


def encode4(x):
    rows, width = x.shape
    cube = x.reshape(rows // 8, 8, width)
    top = jnp.max(jnp.abs(cube), axis=0)
    top = jnp.maximum(top[0:4], top[4:8])
    expo = jnp.ceil(jnp.log2(jnp.maximum(top, 1e-30)))
    scale = jnp.exp2(14.99 - jnp.concatenate([expo, expo], axis=0))
    code = jnp.round(cube * scale[None])
    return code.reshape(rows, width).astype(I32).astype(I16), expo


def decode(code, expo):
    rows, width = code.shape
    group = expo.shape[0]
    cube = code.astype(I32).astype(F32).reshape(rows // group, group, width)
    return (cube * jnp.exp2(expo - 14.99)[None]).reshape(rows, width)


def to_i16(x):
    return x.astype(I32).astype(I16)


def from_i16(x):
    return x.astype(I32).astype(F32)


def unit(x):
    scale = jnp.sqrt(jnp.sum(x * x, axis=1, keepdims=True) + 1e-06)
    return x * (1.0 / scale), scale


def unit_back(grad, rows):
    direction, scale = unit(rows)
    return (grad - direction * jnp.sum(grad * direction, axis=1, keepdims=True)) / scale


def kernel(
    queries_hbm, positive_hbm, items_hbm, counts_i_hbm, counts_n_hbm, owner_hbm, row_hbm, cache_hbm,
    loss_out, query_out, item_codes, cache_codes,
    queries, positive, items, counts_i_ref, counts_n_ref, owner_ref, row_ref, cache, loss_buf, query_buf, msg, mrecv, cache_unit, scat, q_unit, cand_i, cand_n, shift_n,
    expo_i, expo_n, pos, tot, sums_i, factor_i, factor_n, weight_i, weight_n, part_i, part_n,
    slot_grad, slot_hi, slot_lo,
    send_i, recv_i, send_n, recv_n, ag_item, ag_cache, q_part, q_core, q_msg, q_recv,
    in_s, m_s, m_r, p_s, p_r, t_s, t_r, ri_s, ri_r, rn_s, rn_r, ai_s, ai_r, ac_s, ac_r, oi_s, oc_s,
    qc_s, qc_r, qd_s, qd_r, out_s,
):
    me = lax.axis_index("col")
    z = lax.axis_index("pb")
    core = me % 2
    chip = me // 2
    my_g = me // 4
    up = (z + 1) % NZ
    down = (z + NZ - 1) % NZ
    sibling = chip * 2 + 1 - core

    barrier = pltpu.get_barrier_semaphore()
    loads = [
        pltpu.make_async_copy(src, dst, in_s.at[i])
        for i, (src, dst) in enumerate(
            (
                (owner_hbm, owner_ref),
                (row_hbm, row_ref),
                (counts_n_hbm, counts_n_ref),
                (counts_i_hbm, counts_i_ref),
                (items_hbm, items),
                (positive_hbm, positive),
                (queries_hbm, queries),
                (cache_hbm, cache),
            )
        )
    ]
    for load in loads:
        load.start()

    @pl.loop(1, NC)
    def _(s):
        pl.semaphore_signal(barrier, inc=1, device_id={"col": (me + s) % NC}, device_id_type=MESH)

    for other in (up, down):
        pl.semaphore_signal(barrier, inc=1, device_id={"pb": other}, device_id_type=MESH)

    def remote(src, dst, send, recv, **where):
        return pltpu.make_async_remote_copy(
            src_ref=src, dst_ref=dst, send_sem=send, recv_sem=recv, device_id=where, device_id_type=MESH
        )

    def pair_row(ref, b):
        return jnp.concatenate([ref[pl.ds(2 * b, 1), :], ref[pl.ds(2 * b + 1, 1), :]], axis=1)

    def put_pair(ref, b, value):
        ref[pl.ds(2 * b, 1), :] = value[:, 0:128]
        ref[pl.ds(2 * b + 1, 1), :] = value[:, 128:]

    for load in loads[0:4]:
        load.wait()
    counts_i = counts_i_ref[...].astype(F32)
    counts_n = counts_n_ref[...].astype(F32)
    owner = owner_ref[...]
    row = row_ref[...]
    table = jnp.where(iota((NC, NN), 0) == owner, 1.0, 0.0)
    before = onehot(iota((NN, NN), 0) < iota((NN, NN), 1))
    earlier = dot_nn(table.astype(BF16), before)
    rank = jnp.sum(earlier * table, axis=0, keepdims=True).astype(I32)
    lane = onehot(iota((128, NN), 0) == CAP * (me % 4) + rank)
    named = jnp.concatenate(
        [table * (row >> 5).astype(F32), table * (row & 31).astype(F32), table * counts_n], axis=0
    )
    named = dot_nt(named.astype(BF16), lane)
    named = named[0:NC] * 32.0 + named[NC : 2 * NC] + named[2 * NC :] * ROWS
    total_i = jnp.sum(counts_i, axis=1, keepdims=True).reshape(1, 1, 1)
    total_n = jnp.sum(counts_n, axis=1, keepdims=True).reshape(1, 1, 1)
    line = iota((NC, 8, 128), 1)
    totals = jnp.where(line == (my_g + 1) % 8, total_i, jnp.where(line == (my_g + 2) % 8, total_n, 0.0))
    msg[...] = jnp.where(line == my_g, named.reshape(NC, 1, 128), totals)

    pl.semaphore_wait(barrier, NC + 1)

    def to_all(ref, send, recv, s):
        other = (me + s) % NC
        return remote(ref.at[me], ref.at[me], send.at[other], recv.at[me], col=other)

    def from_all(ref, send, recv, s):
        other = (me + s) % NC
        return remote(ref.at[me], ref.at[other], send.at[other], recv.at[other], col=other)

    @pl.loop(1, NC)
    def _(s):
        other = (me + s) % NC
        remote(msg.at[other], mrecv.at[me], m_s.at[other], m_r.at[me], col=other).start()

    mrecv[me] = msg[me]

    loads[4].wait()
    cand_i[...] = unit(items[...].astype(F32))[0].astype(BF16)
    same = iota((NI, NI), 0) == iota((NI, NI), 1)
    shift_i = jnp.log2(jnp.sum(jnp.where(same, counts_i, 0.0), axis=1, keepdims=True))
    first_item = me * NI
    loads[5].wait()
    loads[6].wait()

    @pl.loop(0, NB, unroll=4)
    def _(b):
        at = pl.ds(pl.multiple_of(b * QB, QB), QB)
        q_rows = unit(queries[at, :].astype(F32))[0].astype(BF16)
        q_unit[at, :] = q_rows
        logits = dot_nt(cand_i[...], q_rows) * SCALE2 - shift_i
        hit = positive[:, at] == first_item + iota((NI, QB), 0)
        expo = jnp.exp2(logits)
        expo_i[:, at] = expo
        put_pair(sums_i, b, jnp.sum(expo, axis=0, keepdims=True))
        put_pair(pos.at[me], b, jnp.sum(jnp.where(hit, logits, 0.0), axis=0, keepdims=True))

    loads[7].wait()

    @pl.loop(0, ROWS // QB)
    def _(b):
        at = pl.ds(pl.multiple_of(b * QB, QB), QB)
        cache_unit[at, :] = unit(cache[at, :].astype(F32))[0].astype(BF16)

    @pl.loop(1, NC)
    def _(s):
        other = (me + s) % NC
        remote(msg.at[other], mrecv.at[other], m_s.at[other], m_r.at[other], col=other).wait()

    line = iota((8, 128), 0)
    asked = jnp.zeros((8, 128), F32)
    sum_i = jnp.zeros((8, 128), F32)
    sum_n = jnp.zeros((8, 128), F32)
    for g in range(8):
        four = (mrecv[4 * g] + mrecv[4 * g + 1]) + (mrecv[4 * g + 2] + mrecv[4 * g + 3])
        asked = jnp.where(line == g, four, asked)
        sum_i = sum_i + jnp.where(line == (g + 1) % 8, four, 0.0)
        sum_n = sum_n + jnp.where(line == (g + 2) % 8, four, 0.0)
    total_i = jnp.sum(sum_i, axis=0, keepdims=True)[:, 0:1]
    total_n = jnp.sum(sum_n, axis=0, keepdims=True)[:, 0:1]

    def parts(value):
        count = jnp.floor(value * (1.0 / ROWS))
        return count, (value - count * ROWS).astype(I32)

    by_slot = jnp.concatenate([asked, jnp.zeros((120, 128), F32)], axis=0).T
    for half in range(2):
        picks = []
        for g in range(4 * half, 4 * half + 4):
            count, wanted = parts(by_slot[:, g : g + 1])
            shift_n[g * 128 : (g + 1) * 128, :] = jnp.where(
                count > 0.5, jnp.log2(jnp.maximum(count, 1.0)), 1e30
            )
            picks.append(onehot(iota((128, ROWS), 1) == wanted))
        picked = dot_nn(jnp.concatenate(picks, axis=0), cache_unit[...])
        cand_n[half * 512 : (half + 1) * 512, :] = picked.astype(BF16)

    def tot_copy(half, s, mine):
        other = (me + s) % NC
        slot = me if mine else other
        return remote(
            tot.at[half, me], tot.at[half, slot], t_s.at[half, other], t_r.at[half, slot], col=other
        )

    def scores_n(half):
        @pl.loop(half * NB // 2, (half + 1) * NB // 2, unroll=4)
        def _(b):
            at = pl.ds(pl.multiple_of(b * QB, QB), QB)
            expo = jnp.exp2(dot_nt(cand_n[...], q_unit[at, :]) * SCALE2 - shift_n[...])
            expo_n[:, at] = expo
            sum_n = total_n * jnp.sum(expo, axis=0, keepdims=True)
            put_pair(tot.at[half, me], b - half * (NB // 2), total_i * pair_row(sums_i, b) + sum_n)

        @pl.loop(1, NC)
        def _(s):
            tot_copy(half, s, True).start()

    scores_n(0)
    scores_n(1)

    @pl.loop(1, NC)
    def _(s):
        to_all(pos, p_s, p_r, s).start()

    slots = parts(asked)[1]
    for g in range(8):
        scat[:, g * 128 : (g + 1) * 128] = onehot(iota((ROWS, 128), 0) == slots[g : g + 1, :])

    def sums_in(half):
        @pl.loop(1, NC)
        def _(s):
            tot_copy(half, s, False).wait()

        total = jnp.sum(tot[half], axis=0)
        factor_i[half * 8 : (half + 1) * 8] = total_i / total
        factor_n[half * 8 : (half + 1) * 8] = total_n / total
        loss_buf[half * 8 : (half + 1) * 8] = jnp.log(total)

    def factors(ref, half):
        return jnp.concatenate([ref[half * 8 + k : half * 8 + k + 1, :] for k in range(8)], axis=1)

    def grad_i(half):
        at = pl.ds(half * (NQ // 2), NQ // 2)
        factor = factors(factor_i, half)
        for b in range(2):
            rows = slice(b * (NI // 2), (b + 1) * (NI // 2))
            hit = positive[:, at] == first_item + b * (NI // 2) + iota((NI // 2, NQ // 2), 0)
            weights = (expo_i[rows, at] * factor - jnp.where(hit, 1.0, 0.0)).astype(BF16)
            weight_i[rows, at] = weights
            grad = dot_nn(weights, q_unit[at, :]) * INV_T
            for k in range(4):
                to = (k // 2, slice(b * (NZ // 2), (b + 1) * (NZ // 2)), slice((k % 2) * CH, (k % 2 + 1) * CH))
                piece = grad[:, k * W : (k + 1) * W].reshape(NZ // 2, CH, W)
                part_i[to] = piece if half == 0 else part_i[to] + piece

    def grad_n(half):
        at = pl.ds(half * (NQ // 2), NQ // 2)
        factor = factors(factor_n, half)
        for b in range(2):
            rows = slice(b * (NS // 2), (b + 1) * (NS // 2))
            weights = (expo_n[rows, at] * factor).astype(BF16)
            weight_n[rows, at] = weights
            grad = dot_nn(weights, q_unit[at, :]) * INV_T
            if half == 0:
                slot_grad[rows, :] = grad
            else:
                hi, lo = halves(slot_grad[rows, :] + grad)
                slot_hi[rows, :] = hi
                slot_lo[rows, :] = lo

    def ring_peer(d):
        return up if d == 0 else down

    def ring_chunk(d, t):
        return (z + 4 - t) % NZ if d == 0 else (z + 4 + t) % NZ

    def streams(n, d):
        mine = [(k, 4) for k in range(n) if 2 * k // n == d]
        return mine + [(k, 3) for k in range(n) if 2 * k // n != d]

    def both_ways(n):
        for one, two in zip(streams(n, 0), streams(n, 1)):
            yield (0,) + one
            yield (1,) + two

    def pack(ref, chunk):
        code, e = encode(chunk, 16)
        ref[0:CR] = code
        ref[CR:] = to_i16(e)

    def unpack(ref):
        return decode(ref[0:CR], from_i16(ref[CR:]))

    def pack_two(ref, chunk):
        code, e = encode(chunk[0:CH], 8)
        code2, e2 = encode(chunk[CH:], 8)
        ref[0:CH] = code
        ref[CH : 2 * CH] = code2
        ref[2 * CH :] = to_i16(jnp.concatenate([e, e2], axis=0))

    def unpack_two(ref):
        e = from_i16(ref[2 * CH :])
        return jnp.concatenate([decode(ref[0:CH], e[0:8]), decode(ref[CH : 2 * CH], e[8:])], axis=0)

    def ring_copy(kind, d, t, k):
        _, send, recv, s, r = kind[:5]
        return remote(send.at[d, t, k], recv.at[d, t, k], s.at[d, t, k], r.at[d, t, k], pb=ring_peer(d))

    def ring_first(kind, t):
        part, send, _, _, _, n, put, _ = kind
        for d, k, steps in both_ways(n):
            if steps + t == 4:
                put(send.at[d, t, k], part[k, ring_chunk(d, t)])
                ring_copy(kind, d, t, k).start()

    def ring_step(kind, t):
        part, send, recv, _, _, n, put, get = kind
        for d, k, steps in both_ways(n):
            if steps + t > 4:
                ring_copy(kind, d, t - 1, k).wait()
                put(send.at[d, t, k], part[k, ring_chunk(d, t)] + get(recv.at[d, t - 1, k]))
                ring_copy(kind, d, t, k).start()

    def ring_last(kind):
        part, _, recv, _, _, n, _, get = kind
        own = [part[k, z] for k in range(n)]
        for d, k, _ in both_ways(n):
            ring_copy(kind, d, 3, k).wait()
            own[k] = own[k] + get(recv.at[d, 3, k])
        return own

    kind_i = (part_i, send_i, recv_i, ri_s, ri_r, 2, pack_two, unpack_two)
    kind_n = (part_n, send_n, recv_n, rn_s, rn_r, 4, pack, unpack)

    def by_row(away):
        chunk = (z + away) % NZ
        at = pl.ds(pl.multiple_of(chunk * CR, CR), CR)
        grad = dot_nn(scat[at, :], slot_hi[...]) + dot_nn(scat[at, :], slot_lo[...])
        for k in range(4):
            part_n[k, chunk] = grad[:, k * W : (k + 1) * W]

    def q_which(i):
        return (chip // 2 + i) % NB

    def q_copy(i):
        two = pl.ds(q_which(i) * 2, 2)
        return remote(q_part.at[two, 1 - core], q_core.at[two], qc_s.at[i], qc_r.at[i], col=sibling)

    def q_block(i):
        b = q_which(i)
        at = pl.ds(pl.multiple_of(b * QB, QB), QB)
        grad = dot_tn(weight_i[:, at], cand_i[...]) + dot_tn(weight_n[:, at], cand_n[...])
        q_part[pl.ds(b * 2, 2)] = (grad * INV_T).reshape(2, 2, CH, E)
        q_copy(i).start()

    def q_send(i):
        q_copy(i).wait()
        for j in range(2):
            c = q_which(i) * 2 + j
            grad = q_part[c, core] + q_core[c]
            pack_two(q_msg.at[c], jnp.concatenate([grad[:, :H], grad[:, H:]], axis=0))

            @pl.when(c != chip)
            def _():
                remote(q_msg.at[c], q_recv.at[chip], qd_s.at[c], qd_r.at[chip], col=c * 2 + core).start()

            @pl.when(c == chip)
            def _():
                q_recv[chip] = q_msg[c]

    def out_copy(kind, p, k):
        ref, _, _, out, sem, _ = kind
        return pltpu.make_async_copy(ref.at[p, k], out.at[p, k], sem.at[p, k])

    def behind(d, s):
        return (z + 2 * NZ - s) % NZ if d == 0 else (z + s) % NZ

    def gather_copy(kind, d, s, k):
        ref, send, recv = kind[:3]
        ref = ref.at[behind(d, s), k]
        return remote(ref, ref, send.at[d, s, k], recv.at[d, s, k], pb=ring_peer(d))

    def gather_first(kind, k):
        for d in range(2):
            gather_copy(kind, d, 0, k).start()
        out_copy(kind, z, k).start()

    def gather_wait(kind, d, s, k):
        gather_copy(kind, d, s, k).wait()
        out_copy(kind, behind(d, s + 1), k).start()

    def gather_step(kind, s):
        for d, k, steps in both_ways(kind[5]):
            if s < steps:
                gather_wait(kind, d, s - 1, k)
                gather_copy(kind, d, s, k).start()

    def gather_last(kind):
        for three in (3, 4):
            for d, k, steps in both_ways(kind[5]):
                if steps == three:
                    gather_wait(kind, d, steps - 1, k)

    out_i = (ag_item, ai_s, ai_r, item_codes, oi_s, 2)
    out_n = (ag_cache, ac_s, ac_r, cache_codes, oc_s, 4)

    sums_in(0)
    grad_n(0)
    sums_in(1)
    grad_n(1)
    by_row(4)
    ring_first(kind_n, 0)
    by_row(3)
    by_row(5)
    ring_first(kind_n, 1)
    grad_i(0)
    grad_i(1)
    ring_first(kind_i, 0)
    ring_first(kind_i, 1)
    ring_step(kind_n, 1)
    by_row(2)
    by_row(6)
    ring_step(kind_i, 1)
    by_row(1)
    by_row(7)
    by_row(0)
    q_block(0)
    q_block(1)
    q_block(2)
    ring_step(kind_n, 2)
    ring_step(kind_i, 2)
    q_block(3)
    q_block(4)
    q_send(0)
    ring_step(kind_n, 3)
    ring_step(kind_i, 3)
    q_block(5)
    q_block(6)
    q_block(7)
    q_send(1)

    cache_e = []
    own = jnp.concatenate(ring_last(kind_n), axis=1)
    grad = unit_back(own, cache[pl.ds(pl.multiple_of(z * CR, CR), CR), :].astype(F32))
    for k in range(4):
        code, e = encode4(grad[:, k * W : (k + 1) * W])
        ag_cache[z, k] = code
        gather_first(out_n, k)
        cache_e.append(e)

    own = ring_last(kind_i)
    own = jnp.concatenate([own[0][0:CH], own[0][CH:], own[1][0:CH], own[1][CH:]], axis=1)
    grad = unit_back(own, items[pl.ds(pl.multiple_of(z * CH, CH), CH), :].astype(F32))
    for h in range(2):
        e = []
        for k in range(2):
            code, e_item = encode4(grad[:, (2 * h + k) * W : (2 * h + k + 1) * W])
            ag_item[z, h, k * CH : (k + 1) * CH] = code
            e.append(e_item)
        ag_item[z, h, CR:] = to_i16(jnp.concatenate(e + cache_e[2 * h : 2 * h + 2], axis=0))
        gather_first(out_i, h)

    q_send(2)
    q_send(3)
    q_send(4)
    gather_step(out_n, 1)
    gather_step(out_i, 1)
    q_send(5)
    q_send(6)
    q_send(7)
    gather_step(out_n, 2)
    gather_step(out_i, 2)

    @pl.loop(1, NC)
    def _(s):
        from_all(pos, p_s, p_r, s).wait()

    loss_buf[...] = loss_buf[...] - (jnp.sum(pos[...], axis=0) * LN2 + jnp.log(total_i))
    loss_copy = pltpu.make_async_copy(loss_buf, loss_out, out_s.at[0])
    loss_copy.start()
    gather_step(out_n, 3)
    gather_step(out_i, 3)

    @pl.loop(1, NC // 2)
    def _(s):
        other = (chip + s) % (NC // 2)
        remote(q_msg.at[other], q_recv.at[other], qd_s.at[other], qd_r.at[other], col=other * 2 + core).wait()

    q_grad = unpack_two(q_recv.at[0])
    for c in range(1, NC // 2):
        q_grad = q_grad + unpack_two(q_recv.at[c])
    q_grad = jnp.concatenate([q_grad[0:CH], q_grad[CH:]], axis=1)
    query_buf[...] = unit_back(q_grad, queries[pl.ds(pl.multiple_of(me * CH, CH), CH), :].astype(F32))
    query_copy = pltpu.make_async_copy(query_buf, query_out, out_s.at[1])
    query_copy.start()

    gather_last(out_n)
    gather_last(out_i)

    @pl.loop(0, NZ)
    def _(p):
        for kind in (out_i, out_n):
            for k in range(kind[5]):
                out_copy(kind, p, k).wait()

    loss_copy.wait()
    query_copy.wait()


def last(loss, query, item_codes, cache_codes, loss_out, query_out, item_out, cache_out):
    for p in range(PB):
        for k in range(4):
            columns = slice(k * W, (k + 1) * W)
            part = k % 2
            e = from_i16(item_codes[p, k // 2, CR:])
            e_item = e[4 * part : 4 * part + 4]
            e_cache = e[8 + 4 * part : 12 + 4 * part]
            code = item_codes[p, k // 2, part * CH : part * CH + CH]
            item_out[p * CH : (p + 1) * CH, columns] = decode(code, jnp.concatenate([e_item, e_item], axis=0))
            code = cache_codes[p, k]
            cache_out[p * CR : (p + 1) * CR, columns] = decode(code, jnp.concatenate([e_cache, e_cache], axis=0))

    @pl.when(pl.program_id(0) == 0)
    def _():
        loss_out[...] = loss[...]
        query_out[...] = query[...]


def body(queries, positive, items, item_counts, cache, neg_owner, neg_row, neg_counts):
    hbm = pl.BlockSpec(memory_space=pl.ANY)
    dma = pltpu.SemaphoreType.DMA
    codes_i = (NZ, 2, CR + 16, W)
    codes_n = (NZ, 4, CR, W)
    ring_i = (2, 4, 2, CR + 16, W)
    ring_n = (2, 4, 4, CR + 16, W)
    scratch = [
        pltpu.VMEM((NQ, E), BF16),
        pltpu.VMEM((1, NQ), I32),
        pltpu.VMEM((NI, E), BF16),
        pltpu.VMEM((1, NI), I32),
        pltpu.VMEM((1, NN), I32),
        pltpu.VMEM((1, NN), I32),
        pltpu.VMEM((1, NN), I32),
        pltpu.VMEM((ROWS, E), BF16),
        pltpu.VMEM((NQ // 128, 128), F32),
        pltpu.VMEM((CH, E), F32),
        pltpu.VMEM((NC, 8, 128), F32),
        pltpu.VMEM((NC, 8, 128), F32),
        pltpu.VMEM((ROWS, E), BF16),
        pltpu.VMEM((ROWS, NS), BF16),
        pltpu.VMEM((NQ, E), BF16),
        pltpu.VMEM((NI, E), BF16),
        pltpu.VMEM((NS, E), BF16),
        pltpu.VMEM((NS, 1), F32),
        pltpu.VMEM((NI, NQ), F32),
        pltpu.VMEM((NS, NQ), F32),
        pltpu.VMEM((NC, NQ // 128, 128), F32),
        pltpu.VMEM((2, NC, NQ // 256, 128), F32),
        pltpu.VMEM((NQ // 128, 128), F32),
        pltpu.VMEM((NQ // 128, 128), F32),
        pltpu.VMEM((NQ // 128, 128), F32),
        pltpu.VMEM((NI, NQ), BF16),
        pltpu.VMEM((NS, NQ), BF16),
        pltpu.VMEM((2, NZ, 2 * CH, W), F32),
        pltpu.VMEM((4, NZ, CR, W), F32),
        pltpu.VMEM((NS, E), F32),
        pltpu.VMEM((NS, E), BF16),
        pltpu.VMEM((NS, E), BF16),
        pltpu.VMEM(ring_i, I16),
        pltpu.VMEM(ring_i, I16),
        pltpu.VMEM(ring_n, I16),
        pltpu.VMEM(ring_n, I16),
        pltpu.VMEM(codes_i, I16),
        pltpu.VMEM(codes_n, I16),
        pltpu.VMEM((NC // 2, 2, CH, E), F32),
        pltpu.VMEM((NC // 2, CH, E), F32),
        pltpu.VMEM((NC // 2, 2 * CH + 16, H), I16),
        pltpu.VMEM((NC // 2, 2 * CH + 16, H), I16),
        dma((8,)),
        dma((NC,)), dma((NC,)),
        dma((NC,)), dma((NC,)),
        dma((2, NC)), dma((2, NC)),
        dma((2, 4, 2)), dma((2, 4, 2)),
        dma((2, 4, 4)), dma((2, 4, 4)),
        dma((2, 4, 2)), dma((2, 4, 2)),
        dma((2, 4, 4)), dma((2, 4, 4)),
        dma((NZ, 2)), dma((NZ, 4)),
        dma((NB,)), dma((NB,)),
        dma((NC // 2,)), dma((NC // 2,)),
        dma((2,)),
    ]
    loss, query_grad, item_codes, cache_codes = pl.pallas_call(
        kernel,
        out_shape=(
            jax.ShapeDtypeStruct((NQ // 128, 128), F32),
            jax.ShapeDtypeStruct((CH, E), F32),
            jax.ShapeDtypeStruct(codes_i, I16),
            jax.ShapeDtypeStruct(codes_n, I16),
        ),
        in_specs=[hbm] * 8,
        out_specs=(hbm,) * 4,
        scratch_shapes=scratch,
        compiler_params=pltpu.CompilerParams(
            collective_id=0, has_side_effects=True, vmem_limit_bytes=62 * 1024 * 1024
        ),
    )(
        queries,
        positive.reshape(1, NQ),
        items,
        item_counts.reshape(1, NI),
        neg_counts.reshape(1, NN),
        neg_owner.reshape(1, NN),
        neg_row.reshape(1, NN),
        cache,
    )

    def whole(*shape):
        return pl.BlockSpec(shape, lambda r: (0,) * len(shape))

    def chunks(shape):
        return pl.BlockSpec((PB,) + shape[1:], lambda r: (r, 0, 0, 0))

    loss, query_grad, item_grad, cache_grad = pl.pallas_call(
        last,
        grid=(NZ // PB,),
        out_shape=(
            jax.ShapeDtypeStruct((NQ // 128, 128), F32),
            jax.ShapeDtypeStruct((CH, E), F32),
            jax.ShapeDtypeStruct((NI, E), F32),
            jax.ShapeDtypeStruct((ROWS, E), F32),
        ),
        in_specs=[whole(NQ // 128, 128), whole(CH, E), chunks(codes_i), chunks(codes_n)],
        out_specs=(
            whole(NQ // 128, 128),
            whole(CH, E),
            pl.BlockSpec((PB * CH, E), lambda r: (r, 0)),
            pl.BlockSpec((PB * CR, E), lambda r: (r, 0)),
        ),
        compiler_params=pltpu.CompilerParams(vmem_limit_bytes=62 * 1024 * 1024),
    )(loss, query_grad, item_codes, cache_codes)
    return loss.reshape(NQ), query_grad, item_grad, cache_grad


def solution(mesh):
    placed = (
        P("pb", None),
        P("pb"),
        P("col", None),
        P("col"),
        P("col", None),
        P("col", None),
        P("col"),
        P("col"),
    )
    return jax.shard_map(
        body,
        mesh=mesh,
        in_specs=placed,
        out_specs=(P("pb"), P(("pb", "col"), None), P("col", None), P("col", None)),
        check_vma=False,
    )
```
